32 devices in a mesh: groups: 2 (over x), rep: 8 (over z, y), tp: 2 (over core).
Axes of the slice: x: 2, y: 2, z: 4, core: 2. Of those that a mesh axis runs over, the one named last changes fastest.
Arguments:
- normed_token_rows: bfloat16 [6144, 8192], P(('groups', 'rep'), 'tp'), parts along dimension 0, may hold values from -6 to 6
- base_value_rows: bfloat16 [6144, 1024], P(('groups', 'rep'), 'tp'), parts along dimension 0, may hold values from -6 to 6
- queries: bfloat16 [6144, 8192], P(('groups', 'rep'), 'tp'), parts along dimension 0, may hold values from -120 to 120
- stacked_key_rows: bfloat16 [6144, 1024], P(('groups', 'rep'), 'tp'), parts along dimension 0, may hold values from -5 to 5
- adapter_of_row: int32 [6144, 1], P(('groups', 'rep')), parts along dimension 0, may hold values from 0 to 7; in each aligned block of 384 rows (0 to 383, 384 to 767, ...) at most 96 rows name the same one
- sequence_lengths: int32 [16, 4], P(('groups', 'rep')), parts along dimension 0, may hold values from 1 to 192, 384 in all within a row
- adapter_down_weight: bfloat16 [16, 8192, 64], P(('groups', 'rep'), 'tp'), parts along dimension 0, may hold values from -0.0625 to 0.0625
- adapter_up_weight: bfloat16 [16, 64, 1024], P(('groups', 'rep'), None, 'tp'), parts along dimension 0, may hold values from -0.75 to 0.75
Outputs:
- attended: bfloat16 [6144, 8192], P(('groups', 'rep'), 'tp'), parts along dimension 0
The draws below stay inside these ranges and needn't reach their ends.
There are 2 independent parts, one for each index of `groups`. The reference program is written for one: setup_inputs(seed, part) draws one part's arguments, and reference() takes and returns one part's arrays. A program takes and returns all parts, laid end to end along the dimension named above; each array names one. Nothing has to cross between parts.
Inputs may be any that keep to these rules, and one draw needn't show every extreme that they name: `adapter_of_row`: in the rows of one replica each adapter is named by at most 96 rows, a bound that some block reaches. `sequence_lengths`: each replica's lengths sum to 384; the longest is exactly 192.
All inputs are finite; a program needn't handle non-finite values.
Results may differ from the reference program's by a relative error of at most 0.008.
Values may be sent and summed in bfloat16 or wider, within the bound.
No kernel may reach another device: no remote copies, remote signals or barrier semaphores. Data moves between devices by JAX's collectives and lax.ppermute only.
A program may use at most 192 MiB of HBM per device.

```python
import math
import jax
import jax.numpy as jnp
import numpy as np
from jax import lax

MODEL_WIDTH = 8192
HEADS = 64
KEY_VALUE_HEADS = 8
HEAD_SIZE = 128
ADAPTER_RANK = 64
TOK_DEV = 384
SEQS = 4
ADAPTER_COUNT = 8
MOST = 96
MAXLEN = 192
TOKENS = 3072
N_REP = 8


def key_field(key, closeness):
    base = jax.random.normal(jax.random.fold_in(key, 101), (TOKENS, KEY_VALUE_HEADS, HEAD_SIZE), jnp.float32)
    positions = jnp.arange(TOKENS)
    picked = ((positions % 16 == 5) | (positions % 16 == 11)).astype(jnp.float32)[:, None, None] * closeness
    field = jnp.clip(base * (1.0 - picked), -5.0, 5.0)
    return field


def draw_stacked_key_rows(key, part):
    field = key_field(key, 0.0)
    return field.reshape(TOKENS, KEY_VALUE_HEADS * HEAD_SIZE).astype(jnp.bfloat16)


def draw_queries(key, part):
    group = HEADS // KEY_VALUE_HEADS
    key = jax.random.fold_in(key, 9)
    result = jnp.clip(jax.random.normal(key, (TOKENS, KEY_VALUE_HEADS, group, HEAD_SIZE), jnp.float32), -6.0, 6.0)
    return result.reshape(TOKENS, HEADS * HEAD_SIZE).astype(jnp.bfloat16)


def levels(key, dims, cuts, least, high):
    gain, own = 1.0, jax.random.fold_in(key, 6)
    for axis_at, shards_of in cuts:
        steps = jnp.exp(jax.random.uniform(jax.random.fold_in(own, axis_at), (shards_of,), jnp.float32, least / len(cuts), high / len(cuts)))
        gain = gain * jnp.repeat(steps, dims[axis_at] // shards_of).reshape([-1 if axis == axis_at else 1 for axis in range(len(dims))])
    return gain


def length_profile(number_of, total, limit, skew):
    weights = [(1 << 20) // math.isqrt(grade ** skew) + 1 for grade in range(2, number_of + 1)]
    spare, counts = total - limit - (number_of - 1), [1] * (number_of - 1)
    while spare > 0:
        movable = [i for i in range(number_of - 1) if counts[i] < limit]
        mass, budget = sum([weights[i] for i in movable]), spare
        for i in movable:
            addition = min(limit - counts[i], max(1, budget * weights[i] // mass), spare)
            counts[i] = counts[i] + addition
            spare = spare - addition
    return np.array([limit] + counts)


def ragged_sizes(stream_key, count, total, bound, lean):
    if count == 2:
        one = jax.random.randint(stream_key, (), max(1, total - bound), min(bound, total - 1) + 1)
        return jnp.stack([one, total - one])
    tallies = jnp.asarray(length_profile(count, total, bound, lean), jnp.int32)
    twos = (count - 1) // 2
    source_of, sink = tallies[1:1 + 2 * twos:2], tallies[2:2 + 2 * twos:2]
    room = jnp.minimum(source_of - 1, bound - sink)
    shifted = jax.random.randint(jax.random.fold_in(stream_key, 1), (twos,), 0, 1 << 20) % (room + 1)
    tallies = tallies.at[1:1 + 2 * twos:2].set(source_of - shifted).at[2:2 + 2 * twos:2].set(sink + shifted)
    return tallies[jax.random.permutation(jax.random.fold_in(stream_key, 2), count)]


def shared_out(key, own, number, rows, number_of, top, limit, lean):
    sequence = jax.random.permutation(key, number_of)
    crowded, usual = load_shares(number_of, rows * top, limit, lean, True), load_shares(number_of, rows * top, limit, lean, False)
    places = jnp.arange(number_of)

    def named(sizes, offset_by):
        used = int((sizes > 0).sum())
        fixed = max(1, used // 4)
        passed = fixed + (places - fixed + offset_by * (used - fixed)) % max(1, number_of - fixed)
        return jnp.zeros((number_of,), jnp.int32).at[sequence[jnp.where(places < fixed, places, passed)]].set(jnp.asarray(sizes, jnp.int32))

    sizes = jnp.where(number % 4 == 0, named(crowded, number // 4), named(usual, number - number // 4 - 1))
    mixed = jax.random.permutation(jax.random.fold_in(own, 3), number_of)
    donor, sink = mixed[0:number_of // 2 * 2:2], mixed[1:number_of // 2 * 2:2]
    slack = jnp.minimum(sizes[donor] - 1, limit - sizes[sink]) // 2
    slack = jnp.where((donor == sequence[0]) | (sink == sequence[0]) | (sizes[sink] == 0), 0, jnp.maximum(slack, 0))
    passed = jax.random.randint(jax.random.fold_in(own, 4), (number_of // 2,), 0, 1 << 20) % (slack + 1)
    sizes = sizes.at[donor].add(-passed).at[sink].add(passed)
    items = jnp.searchsorted(jnp.cumsum(sizes), jnp.arange(rows * top), side="right").astype(jnp.int32)
    table = items.reshape(top, rows).T
    table = table[jax.random.permutation(jax.random.fold_in(own, 1), rows)]
    offset_by = jax.random.randint(jax.random.fold_in(own, 2), (rows, 1), 0, top)
    return jnp.take_along_axis(table, (jnp.arange(top)[None, :] + offset_by) % top, axis=1)


def load_shares(amount, total, reach, lean, full):
    loads = [(1 << 20) // math.isqrt(rank ** lean) + 1 for rank in range(1, amount + 1)]
    largest = reach if full else min(reach, max(-(-total // amount), total * loads[0] // sum(loads)))
    least = 1 if total - largest >= amount - 1 else 0
    holding, surplus = [largest] + [least] * (amount - 1), total - largest - least * (amount - 1)
    while surplus > 0:
        candidates = [i for i in range(1, amount) if holding[i] < largest] or [i for i in range(1, amount) if holding[i] < reach]
        pool, left = sum([loads[i] for i in candidates]), surplus
        for i in candidates:
            more = min(reach - holding[i], max(1, left * loads[i] // pool), surplus)
            holding[i] = holding[i] + more
            surplus = surplus - more
    return np.array(holding)


def normal_values(rng, dims, width, most, split=(), kind=jnp.bfloat16):
    array = jax.random.normal(rng, dims, jnp.float32) * width
    if len(split) > 0:
        array = levels(rng, dims, split, -0.22, 0.18) * array
    return jnp.clip(array, min=-most, max=most).astype(kind)


def setup_inputs(seed: int = 0, part: int = 0) -> dict:
    keys = jax.random.split(jax.random.key(seed), 9)
    part_splits = jax.random.split(jax.random.fold_in(keys[8], part), 9)
    normed_token_rows = normal_values(part_splits[0], (TOKENS, MODEL_WIDTH), 1.0, 6.0, ((0, 8), (1, 2)))
    base_value_rows = normal_values(part_splits[1], (TOKENS, KEY_VALUE_HEADS * HEAD_SIZE), 1.0, 6.0, ((0, 8), (1, 2)))
    queries = draw_queries(jax.random.fold_in(jax.random.fold_in(keys[8], part), 71), part)
    stacked_key_rows = draw_stacked_key_rows(jax.random.fold_in(jax.random.fold_in(keys[8], part), 71), part)
    adapter_of_row_keys = jax.random.split(jax.random.fold_in(part_splits[4], 1), TOKENS // TOK_DEV)
    adapter_of_row_turns = jax.random.permutation(jax.random.fold_in(part_splits[4], 3), TOKENS // TOK_DEV)
    adapter_of_row = jax.vmap(lambda own, number: shared_out(jax.random.fold_in(part_splits[4], 2), own, number, TOK_DEV, ADAPTER_COUNT, 1, MOST, 2))(adapter_of_row_keys, adapter_of_row_turns).reshape((TOKENS, 1))
    sequence_lengths = jax.vmap(lambda own: ragged_sizes(own, SEQS, TOK_DEV, MAXLEN, 2))(jax.random.split(part_splits[5], N_REP)).reshape((N_REP, SEQS)).astype(jnp.int32)
    adapter_down_weight = normal_values(part_splits[6], (ADAPTER_COUNT, MODEL_WIDTH, ADAPTER_RANK), MODEL_WIDTH ** -0.5, 0.0625, ((0, 8), (1, 2)))
    adapter_up_weight = normal_values(part_splits[7], (ADAPTER_COUNT, ADAPTER_RANK, KEY_VALUE_HEADS * HEAD_SIZE), ADAPTER_RANK ** -0.5, 0.75, ((0, 8), (2, 2)))
    return {"normed_token_rows": normed_token_rows, "base_value_rows": base_value_rows, "queries": queries, "stacked_key_rows": stacked_key_rows, "adapter_of_row": adapter_of_row, "sequence_lengths": sequence_lengths, "adapter_down_weight": adapter_down_weight, "adapter_up_weight": adapter_up_weight}


adapter_scale = 2.0


def attend_block(queries, stacked_key_rows, value_rows, lengths):
    count = queries.shape[0]
    kv_heads = stacked_key_rows.shape[1] // HEAD_SIZE
    group = HEADS // KEY_VALUE_HEADS
    positions = jnp.arange(count, dtype=jnp.int32)
    ends = jnp.cumsum(lengths)
    segment = jnp.sum((positions[:, None] >= ends[None, :]).astype(jnp.int32), axis=1)
    allowed = (segment[:, None] == segment[None, :]) & (positions[None, :] <= positions[:, None])
    query_heads = queries.reshape(count, kv_heads, group, HEAD_SIZE).astype(jnp.float32)
    key_heads = stacked_key_rows.reshape(count, kv_heads, HEAD_SIZE).astype(jnp.float32)
    value_heads = value_rows.reshape(count, kv_heads, HEAD_SIZE).astype(jnp.float32)
    scores = jnp.einsum("tjgd,sjd->jgts", query_heads, key_heads) * (HEAD_SIZE ** -0.5)
    scores = jnp.where(allowed[None, None], scores, -1e30)
    peak = jnp.max(scores, axis=-1, keepdims=True)
    weights = jnp.exp(scores - peak)
    probs = (weights / jnp.sum(weights, axis=-1, keepdims=True)).astype(jnp.bfloat16)
    mixed = jnp.einsum("jgts,sjd->tjgd", probs.astype(jnp.float32), value_heads)
    return mixed.astype(jnp.bfloat16).reshape(count, kv_heads * group * HEAD_SIZE)


def reference(normed_token_rows, base_value_rows, queries, stacked_key_rows, adapter_of_row, sequence_lengths, adapter_down_weight, adapter_up_weight):
    adapter_ids = adapter_of_row[:, 0]
    capacity = N_REP * MOST

    def visit_one(row_deltas, adapter_choice):
        picked = jnp.nonzero(adapter_ids == adapter_choice, size=capacity, fill_value=TOKENS)[0]
        collected_rows = normed_token_rows.at[picked].get(mode="fill", fill_value=0)
        narrow_projection = jnp.dot(collected_rows, adapter_down_weight[adapter_choice], preferred_element_type=jnp.float32).astype(jnp.bfloat16)
        value_update = jnp.dot(narrow_projection, adapter_up_weight[adapter_choice], preferred_element_type=jnp.float32).astype(jnp.bfloat16)
        return row_deltas.at[picked].set(value_update, mode="drop"), None

    start_rows = jnp.zeros((TOKENS, KEY_VALUE_HEADS * HEAD_SIZE), jnp.bfloat16)
    row_deltas, unused = lax.scan(visit_one, start_rows, jnp.arange(ADAPTER_COUNT, dtype=jnp.int32))
    value_rows = (base_value_rows.astype(jnp.float32) + adapter_scale * row_deltas.astype(jnp.float32)).astype(jnp.bfloat16)

    def attend_part(pieces):
        return attend_block(pieces[0], pieces[1], pieces[2], pieces[3])

    blocks = lax.map(attend_part, (queries.reshape(N_REP, TOK_DEV, HEADS * HEAD_SIZE), stacked_key_rows.reshape(N_REP, TOK_DEV, KEY_VALUE_HEADS * HEAD_SIZE), value_rows.reshape(N_REP, TOK_DEV, KEY_VALUE_HEADS * HEAD_SIZE), sequence_lengths))
    return blocks.reshape(TOKENS, HEADS * HEAD_SIZE)
```

```python
import functools

import jax
import jax.numpy as jnp
import numpy as np
from jax import lax
from jax.experimental import pallas as pl
from jax.experimental.pallas import tpu as pltpu
from jax.sharding import PartitionSpec as P

HEADS = 64
KEY_VALUE_HEADS = 8
HEAD_SIZE = 128
GROUP = HEADS // KEY_VALUE_HEADS
LONGEST = 192
TILE = 64
REACH = -(-(LONGEST - 1) // TILE)
adapter_scale = 2.0

VMEM = pl.BlockSpec(memory_space=pltpu.VMEM)
SMEM = pl.BlockSpec(memory_space=pltpu.SMEM)
NT = (((1,), (1,)), ((), ()))


def ring_order(n):
    if n == 8:
        return list(range(0, n, 2)) + list(range(n - 1, 0, -2))
    return list(range(n))


def windows(rows):
    found = []
    for tile in range(rows // TILE):
        first = max(0, tile - REACH) * TILE
        width = (tile + 1) * TILE - first
        width = -(-width // 128) * 128
        found.append((tile * TILE, first, width))
    return found


def probs_kernel(lengths_ref, q_ref, k_ref, *p_refs):
    rows = k_ref.shape[0]
    ends = []
    total = jnp.int32(0)
    for i in range(lengths_ref.shape[1]):
        total = total + lengths_ref[0, i]
        ends.append(total)
    factor = float(np.log2(np.e) * HEAD_SIZE**-0.5)
    for p_ref, (start, first, width) in zip(p_refs, windows(rows)):
        t = lax.broadcasted_iota(jnp.int32, (TILE, width), 0) + start
        s = lax.broadcasted_iota(jnp.int32, (TILE, width), 1) + first
        allowed = s <= t
        for end in ends:
            allowed = allowed & ((t >= end) == (s >= end))
        bias = jnp.where(allowed, 0.0, -1e30)
        keys = k_ref[first : first + width, :]
        for head in range(GROUP):
            q = q_ref[start : start + TILE, head * HEAD_SIZE : (head + 1) * HEAD_SIZE]
            scores = lax.dot_general(q, keys, NT, preferred_element_type=jnp.float32) + bias
            peak = jnp.max(scores, axis=1, keepdims=True)
            weights = jnp.exp2((scores - peak) * factor)
            inverse = 1.0 / jnp.sum(weights, axis=1, keepdims=True)
            p_ref[head * TILE : (head + 1) * TILE, :] = (weights * inverse).astype(jnp.bfloat16)


def probs_of(lengths, queries, keys, kv_head):
    rows = keys.shape[0]
    wide = GROUP * HEAD_SIZE
    shapes = [(GROUP * TILE, width) for _, _, width in windows(rows)]
    elements = sum(a * b for a, b in shapes)
    return pl.pallas_call(
        probs_kernel,
        grid=(1,),
        out_shape=[jax.ShapeDtypeStruct(s, jnp.bfloat16) for s in shapes],
        in_specs=[
            SMEM,
            pl.BlockSpec((rows, wide), lambda i: (0, kv_head)),
            pl.BlockSpec((rows, HEAD_SIZE), lambda i: (0, kv_head)),
        ],
        out_specs=[pl.BlockSpec(s, lambda i: (0, 0)) for s in shapes],
        cost_estimate=pl.CostEstimate(
            flops=2 * elements * HEAD_SIZE,
            bytes_accessed=2 * (rows * wide + elements),
            transcendentals=elements,
        ),
        name="probs",
    )(lengths, queries, keys)


def lowrank_kernel(ranks, ids_ref, adapter_ref, x_ref, before_ref, *refs):
    w_refs, out_ref = refs[:-1], refs[-1]
    adapter = adapter_ref[...]
    x = x_ref[...]
    total = jnp.zeros(out_ref.shape, jnp.float32) if before_ref is None else before_ref[...]
    pieces = [w_ref[...] for w_ref in w_refs]
    stacked = jnp.concatenate(pieces, axis=0)
    product = lax.dot_general(x, stacked, NT, preferred_element_type=jnp.float32)
    width = out_ref.shape[1]
    for i in range(ranks):
        total = total + jnp.where(adapter == ids_ref[i], product[:, i * width : (i + 1) * width], 0.0)
    out_ref[...] = total


def lowrank_of(ids, adapter_of_row, x, before, pieces):
    rows, features = x.shape
    rank = before.shape[1]
    depth = sum(p.shape[0] for p in pieces)
    return pl.pallas_call(
        functools.partial(lowrank_kernel, depth // rank),
        out_shape=jax.ShapeDtypeStruct((rows, rank), jnp.float32),
        in_specs=[SMEM, VMEM, VMEM, VMEM] + [VMEM] * len(pieces),
        out_specs=VMEM,
        cost_estimate=pl.CostEstimate(
            flops=2 * rows * features * depth,
            bytes_accessed=2 * features * (rows + depth),
            transcendentals=0,
        ),
        name="lowrank",
    )(ids, adapter_of_row, x, before, *pieces)


def attend_kernel(kv_heads, n, ids_ref, adapter_ref, mine_ref, theirs_ref, base_ref, *refs):
    up_refs = refs[:n]
    tiles = windows(base_ref.shape[0])
    p_refs = refs[n : n + kv_heads * len(tiles)]
    out_ref, block, sems = refs[n + kv_heads * len(tiles) :]
    rank = mine_ref.shape[1]
    adapter = adapter_ref[...]
    lowrank = (mine_ref[...] + theirs_ref[...]).astype(jnp.bfloat16)
    spread = jnp.concatenate(
        [jnp.where(adapter == ids_ref[i], lowrank, jnp.zeros_like(lowrank)) for i in range(n)], axis=1
    )
    copies = []
    wide = GROUP * HEAD_SIZE
    for kv in range(kv_heads):
        columns = slice(kv * HEAD_SIZE, (kv + 1) * HEAD_SIZE)
        up = jnp.concatenate([up_ref[:, columns] for up_ref in up_refs], axis=0)
        delta = jnp.dot(spread, up, preferred_element_type=jnp.float32).astype(jnp.bfloat16)
        values = (
            base_ref[:, columns].astype(jnp.float32) + adapter_scale * delta.astype(jnp.float32)
        ).astype(jnp.bfloat16)
        for i, (start, first, width) in enumerate(tiles):
            mixed = jnp.dot(
                p_refs[kv * len(tiles) + i][...],
                values[first : first + width, :],
                preferred_element_type=jnp.float32,
            ).astype(jnp.bfloat16)
            for head in range(GROUP):
                at = kv * wide + head * HEAD_SIZE
                block[start : start + TILE, at : at + HEAD_SIZE] = mixed[head * TILE : (head + 1) * TILE, :]
        copy = pltpu.make_async_copy(
            block.at[:, kv * wide : (kv + 1) * wide],
            out_ref.at[:, kv * wide : (kv + 1) * wide],
            sems.at[kv],
        )
        copy.start()
        copies.append(copy)
    for copy in copies:
        copy.wait()


def attend(ids, adapter_of_row, mine, theirs, base, ups, probs):
    rows, value_portion = base.shape
    kv_heads = value_portion // HEAD_SIZE
    wide = kv_heads * GROUP * HEAD_SIZE
    flat = [p for per_head in probs for p in per_head]
    return pl.pallas_call(
        functools.partial(attend_kernel, kv_heads, len(ups)),
        out_shape=jax.ShapeDtypeStruct((rows, wide), jnp.bfloat16),
        in_specs=[SMEM] + [VMEM] * (4 + len(ups) + len(flat)),
        out_specs=pl.BlockSpec(memory_space=pl.ANY),
        scratch_shapes=[pltpu.VMEM((rows, wide), jnp.bfloat16), pltpu.SemaphoreType.DMA((kv_heads,))],
        compiler_params=pltpu.CompilerParams(vmem_limit_bytes=40 * 2**20),
        name="attend",
    )(ids, adapter_of_row, mine, theirs, base, *ups, *flat)


def on_device(
    normed_token_rows,
    base_value_rows,
    queries,
    stacked_key_rows,
    adapter_of_row,
    sequence_lengths,
    adapter_down_weight,
    adapter_up_weight,
):
    n = lax.axis_size("rep")
    order = ring_order(n)
    ahead = [(order[i], order[(i + 1) % n]) for i in range(n)]
    back = [(b, a) for a, b in ahead]
    far = n // 2
    distances = [0] + [d for step in range(1, far) for d in (step, -step)] + [far]
    table = np.zeros((n, n), np.int32)
    for place, replica in enumerate(order):
        table[replica] = [order[(place - d) % n] for d in distances]
    ids = lax.dynamic_index_in_dim(jnp.asarray(table), lax.axis_index("rep"), 0, keepdims=False)

    down = jnp.swapaxes(adapter_down_weight[0], 0, 1)
    rank = down.shape[0]
    half = rank // 2
    up = adapter_up_weight[0]

    def pass_round(piece, steps_ahead, steps_back):
        held = {0: piece}
        moving_ahead = moving_back = piece
        for step in range(1, far + 1):
            if step <= steps_ahead:
                moving_ahead = lax.ppermute(moving_ahead, "rep", ahead)
                held[step] = moving_ahead
            if step <= steps_back:
                moving_back = lax.ppermute(moving_back, "rep", back)
                held[-step if step < far else far] = moving_back
        return held

    low = pass_round(down[:half], far, far - 1)
    high = pass_round(down[half:], far - 1, far)
    ups = pass_round(up, far, far - 1)

    kv_heads = stacked_key_rows.shape[1] // HEAD_SIZE
    probs = [probs_of(sequence_lengths, queries, stacked_key_rows, kv) for kv in range(kv_heads)]

    partial = jnp.zeros((normed_token_rows.shape[0], rank), jnp.float32)
    early = n - 3
    for lo, hi in [(a, min(a + 5, early)) for a in range(0, early, 5)] + [(early, n)]:
        pieces = [piece for d in distances[lo:hi] for piece in (low[d], high[d])]
        partial = lowrank_of(ids[lo:hi], adapter_of_row, normed_token_rows, partial, pieces)
    other = lax.ppermute(partial, "tp", [(0, 1), (1, 0)])
    return attend(ids, adapter_of_row, partial, other, base_value_rows, [ups[d] for d in distances], probs)


def solution(mesh):
    placed = (
        P(("groups", "rep"), "tp"),
        P(("groups", "rep"), "tp"),
        P(("groups", "rep"), "tp"),
        P(("groups", "rep"), "tp"),
        P(("groups", "rep"), None),
        P(("groups", "rep"), None),
        P(("groups", "rep"), "tp", None),
        P(("groups", "rep"), None, "tp"),
    )
    return jax.shard_map(
        on_device, mesh=mesh, in_specs=placed, out_specs=P(("groups", "rep"), "tp"), check_vma=False
    )
```

```python
import functools

import jax
import jax.numpy as jnp
import numpy as np
from jax import lax
from jax.experimental import pallas as pl
from jax.experimental.pallas import tpu as pltpu
from jax.sharding import PartitionSpec as P

HEADS = 64
KEY_VALUE_HEADS = 8
HEAD_SIZE = 128
GROUP = HEADS // KEY_VALUE_HEADS
LONGEST = 192
TILE = 64
REACH = -(-(LONGEST - 1) // TILE)
adapter_scale = 2.0

VMEM = pl.BlockSpec(memory_space=pltpu.VMEM)
SMEM = pl.BlockSpec(memory_space=pltpu.SMEM)
NT = (((1,), (1,)), ((), ()))


def ring_order(n):
    if n == 8:
        return list(range(0, n, 2)) + list(range(n - 1, 0, -2))
    return list(range(n))


def windows(rows):
    found = []
    for tile in range(rows // TILE):
        first = max(0, tile - REACH) * TILE
        width = (tile + 1) * TILE - first
        width = -(-width // 128) * 128
        found.append((tile * TILE, first, width))
    return found


def probs_kernel(lengths_ref, q_ref, k_ref, *p_refs):
    rows = k_ref.shape[0]
    ends = []
    total = jnp.int32(0)
    for i in range(lengths_ref.shape[1]):
        total = total + lengths_ref[0, i]
        ends.append(total)
    factor = float(np.log2(np.e) * HEAD_SIZE**-0.5)
    for p_ref, (start, first, width) in zip(p_refs, windows(rows)):
        t = lax.broadcasted_iota(jnp.int32, (TILE, width), 0) + start
        s = lax.broadcasted_iota(jnp.int32, (TILE, width), 1) + first
        allowed = s <= t
        for end in ends:
            allowed = allowed & ((t >= end) == (s >= end))
        bias = jnp.where(allowed, 0.0, -1e30)
        keys = k_ref[first : first + width, :]
        for head in range(GROUP):
            q = q_ref[start : start + TILE, head * HEAD_SIZE : (head + 1) * HEAD_SIZE]
            scores = lax.dot_general(q, keys, NT, preferred_element_type=jnp.float32) + bias
            peak = jnp.max(scores, axis=1, keepdims=True)
            weights = jnp.exp2((scores - peak) * factor)
            inverse = 1.0 / jnp.sum(weights, axis=1, keepdims=True)
            p_ref[head * TILE : (head + 1) * TILE, :] = (weights * inverse).astype(jnp.bfloat16)


def probs_of(lengths, queries, keys, kv_head):
    rows = keys.shape[0]
    wide = GROUP * HEAD_SIZE
    shapes = [(GROUP * TILE, width) for _, _, width in windows(rows)]
    elements = sum(a * b for a, b in shapes)
    return pl.pallas_call(
        probs_kernel,
        grid=(1,),
        out_shape=[jax.ShapeDtypeStruct(s, jnp.bfloat16) for s in shapes],
        in_specs=[
            SMEM,
            pl.BlockSpec((rows, wide), lambda i: (0, kv_head)),
            pl.BlockSpec((rows, HEAD_SIZE), lambda i: (0, kv_head)),
        ],
        out_specs=[pl.BlockSpec(s, lambda i: (0, 0)) for s in shapes],
        cost_estimate=pl.CostEstimate(
            flops=3_500_000_000, bytes_accessed=2 * (rows * wide + elements), transcendentals=elements
        ),
        compiler_params=pltpu.CompilerParams(vmem_limit_bytes=12 * 2**20),
        name="probs",
    )(lengths, queries, keys)


def lowrank_kernel(at, count, ids_ref, adapter_ref, x_ref, *refs):
    w_refs, out_ref = refs[:count], refs[-1]
    before_ref = refs[count] if at > 0 else None
    adapter = adapter_ref[...]
    rows, features = x_ref.shape
    half = w_refs[0].shape[0]
    stacked = jnp.concatenate([w_ref[:, :features] for w_ref in w_refs], axis=0)
    product = lax.dot_general(x_ref[...], stacked, NT, preferred_element_type=jnp.float32)
    sums = [jnp.zeros((rows, half), jnp.float32)] * 2
    for i in range(count):
        part = product[:, i * half : (i + 1) * half]
        sums[i % 2] = sums[i % 2] + jnp.where(adapter == ids_ref[at + i // 2], part, 0.0)
    total = jnp.concatenate(sums, axis=1)
    out_ref[...] = total if before_ref is None else total + before_ref[...]


def lowrank_of(ids, at, adapter_of_row, x, before, pieces, after):
    rows, features = x.shape
    rank = 2 * pieces[0].shape[0]
    operands = [ids, adapter_of_row, x] + pieces + ([] if before is None else [before])
    used = len(operands)
    operands = operands + after
    size = 2 * sum(p.size for p in pieces)
    return pl.pallas_call(
        functools.partial(lowrank_kernel, at, len(pieces)),
        out_shape=jax.ShapeDtypeStruct((rows, rank), jnp.float32),
        in_specs=[SMEM] + [VMEM] * (used - 1) + [pl.BlockSpec(memory_space=pl.ANY)] * len(after),
        out_specs=VMEM,
        cost_estimate=pl.CostEstimate(
            flops=2_500_000_000, bytes_accessed=2 * rows * features + size, transcendentals=0
        ),
        compiler_params=pltpu.CompilerParams(vmem_limit_bytes=8 * 2**20 + 2 * x.size + 2 * size),
        name="lowrank",
    )(*operands)


def attend_kernel(kv_heads, n, ids_ref, adapter_ref, mine_ref, theirs_ref, base_ref, *refs):
    rows, value_portion = base_ref.shape
    tiles = windows(rows)
    low_refs, high_refs = refs[:n], refs[n : 2 * n]
    p_refs = refs[2 * n : 2 * n + kv_heads * len(tiles)]
    out_ref, block, sems = refs[2 * n + kv_heads * len(tiles) :]
    rank = mine_ref.shape[1]
    features = low_refs[0].shape[1] - value_portion
    adapter = adapter_ref[...]
    lowrank = (mine_ref[...] + theirs_ref[...]).astype(jnp.bfloat16)
    twice = jnp.concatenate([lowrank, lowrank], axis=1)
    second = lax.broadcasted_iota(jnp.int32, twice.shape, 1) >= rank
    spread = jnp.concatenate(
        [
            jnp.where(adapter == jnp.where(second, ids_ref[i + 1], ids_ref[i]), twice, jnp.zeros_like(twice))
            for i in range(0, n, 2)
        ],
        axis=1,
    )
    copies = []
    wide = GROUP * HEAD_SIZE
    for kv in range(kv_heads):
        columns = slice(kv * HEAD_SIZE, (kv + 1) * HEAD_SIZE)
        held = slice(features + kv * HEAD_SIZE, features + (kv + 1) * HEAD_SIZE)
        up = jnp.concatenate([ref[:, held] for pair in zip(low_refs, high_refs) for ref in pair], axis=0)
        delta = jnp.dot(spread, up, preferred_element_type=jnp.float32).astype(jnp.bfloat16)
        values = (
            base_ref[:, columns].astype(jnp.float32) + adapter_scale * delta.astype(jnp.float32)
        ).astype(jnp.bfloat16)
        for i, (start, first, width) in enumerate(tiles):
            mixed = jnp.dot(
                p_refs[kv * len(tiles) + i][...],
                values[first : first + width, :],
                preferred_element_type=jnp.float32,
            ).astype(jnp.bfloat16)
            for head in range(GROUP):
                at = kv * wide + head * HEAD_SIZE
                block[start : start + TILE, at : at + HEAD_SIZE] = mixed[head * TILE : (head + 1) * TILE, :]
        copy = pltpu.make_async_copy(
            block.at[:, kv * wide : (kv + 1) * wide],
            out_ref.at[:, kv * wide : (kv + 1) * wide],
            sems.at[kv],
        )
        copy.start()
        copies.append(copy)
    for copy in copies:
        copy.wait()


def attend(ids, adapter_of_row, mine, theirs, base, lows, highs, probs):
    rows, value_portion = base.shape
    kv_heads = value_portion // HEAD_SIZE
    wide = kv_heads * GROUP * HEAD_SIZE
    flat = [p for per_head in probs for p in per_head]
    held = 2 * sum(a.size for a in lows + highs + flat)
    return pl.pallas_call(
        functools.partial(attend_kernel, kv_heads, len(lows)),
        out_shape=jax.ShapeDtypeStruct((rows, wide), jnp.bfloat16),
        in_specs=[SMEM] + [VMEM] * (4 + len(lows) + len(highs) + len(flat)),
        out_specs=pl.BlockSpec(memory_space=pl.ANY),
        scratch_shapes=[pltpu.VMEM((rows, wide), jnp.bfloat16), pltpu.SemaphoreType.DMA((kv_heads,))],
        compiler_params=pltpu.CompilerParams(vmem_limit_bytes=12 * 2**20),
        name="attend",
    )(ids, adapter_of_row, mine, theirs, base, *lows, *highs, *flat)


def on_device(
    normed_token_rows,
    base_value_rows,
    queries,
    stacked_key_rows,
    adapter_of_row,
    sequence_lengths,
    adapter_down_weight,
    adapter_up_weight,
):
    n = lax.axis_size("rep")
    order = ring_order(n)
    ahead = [(order[i], order[(i + 1) % n]) for i in range(n)]
    back = [(b, a) for a, b in ahead]
    far = n // 2
    distances = [0] + [d for step in range(1, far) for d in (step, -step)] + [far]
    table = np.zeros((n, n), np.int32)
    for place, replica in enumerate(order):
        table[replica] = [order[(place - d) % n] for d in distances]
    ids = lax.dynamic_index_in_dim(jnp.asarray(table), lax.axis_index("rep"), 0, keepdims=False)

    down = jnp.swapaxes(adapter_down_weight[0], 0, 1)
    both = jnp.concatenate([down, adapter_up_weight[0]], axis=1)
    half = both.shape[0] // 2

    def pass_round(piece, steps_ahead, steps_back):
        held = {0: piece}
        moving_ahead = moving_back = piece
        for step in range(1, far + 1):
            if step <= steps_ahead:
                moving_ahead = lax.ppermute(moving_ahead, "rep", ahead)
                held[step] = moving_ahead
            if step <= steps_back:
                moving_back = lax.ppermute(moving_back, "rep", back)
                held[-step if step < far else far] = moving_back
        return held

    low = pass_round(both[:half], far, far - 1)
    high = pass_round(both[half:], far - 1, far)

    kv_heads = stacked_key_rows.shape[1] // HEAD_SIZE
    probs = [probs_of(sequence_lengths, queries, stacked_key_rows, kv) for kv in range(kv_heads)]

    partial = None
    for lo, hi in [(0, 3)] + [(a, a + 2) for a in range(3, n - 3, 2)] + [(n - 3, n)]:
        pieces = [piece for d in distances[lo:hi] for piece in (low[d], high[d])]
        after = [p[0] for p in probs] if hi == n else []
        partial = lowrank_of(ids, lo, adapter_of_row, normed_token_rows, partial, pieces, after)
    other = lax.ppermute(partial, "tp", [(0, 1), (1, 0)])
    return attend(
        ids,
        adapter_of_row,
        partial,
        other,
        base_value_rows,
        [low[d] for d in distances],
        [high[d] for d in distances],
        probs,
    )


def solution(mesh):
    placed = (
        P(("groups", "rep"), "tp"),
        P(("groups", "rep"), "tp"),
        P(("groups", "rep"), "tp"),
        P(("groups", "rep"), "tp"),
        P(("groups", "rep"), None),
        P(("groups", "rep"), None),
        P(("groups", "rep"), "tp", None),
        P(("groups", "rep"), None, "tp"),
    )
    return jax.shard_map(
        on_device, mesh=mesh, in_specs=placed, out_specs=P(("groups", "rep"), "tp"), check_vma=False
    )
```

```python
import functools

import jax
import jax.numpy as jnp
import numpy as np
from jax import lax
from jax.experimental import pallas as pl
from jax.experimental.pallas import tpu as pltpu
from jax.sharding import PartitionSpec as P

HEADS = 64
KEY_VALUE_HEADS = 8
HEAD_SIZE = 128
GROUP = HEADS // KEY_VALUE_HEADS
LONGEST = 192
TILE = 64
REACH = -(-(LONGEST - 1) // TILE)
adapter_scale = 2.0

VMEM = pl.BlockSpec(memory_space=pltpu.VMEM)
SMEM = pl.BlockSpec(memory_space=pltpu.SMEM)
NT = (((1,), (1,)), ((), ()))


def ring_order(n):
    if n == 8:
        return list(range(0, n, 2)) + list(range(n - 1, 0, -2))
    return list(range(n))


def windows(rows):
    found = []
    for tile in range(rows // TILE):
        first = max(0, tile - REACH) * TILE
        width = (tile + 1) * TILE - first
        width = -(-width // 128) * 128
        found.append((tile * TILE, first, width))
    return found


def probs_kernel(waits, lengths_ref, q_ref, k_ref, *refs):
    p_refs = refs[waits:]
    rows = k_ref.shape[0]
    ends = []
    total = jnp.int32(0)
    for i in range(lengths_ref.shape[1]):
        total = total + lengths_ref[0, i]
        ends.append(total)
    factor = float(np.log2(np.e) * HEAD_SIZE**-0.5)
    for p_ref, (start, first, width) in zip(p_refs, windows(rows)):
        t = lax.broadcasted_iota(jnp.int32, (TILE, width), 0) + start
        s = lax.broadcasted_iota(jnp.int32, (TILE, width), 1) + first
        allowed = s <= t
        for end in ends:
            allowed = allowed & ((t >= end) == (s >= end))
        bias = jnp.where(allowed, 0.0, -1e30)
        keys = k_ref[first : first + width, :]
        for head in range(GROUP):
            q = q_ref[start : start + TILE, head * HEAD_SIZE : (head + 1) * HEAD_SIZE]
            scores = lax.dot_general(q, keys, NT, preferred_element_type=jnp.float32) + bias
            peak = jnp.max(scores, axis=1, keepdims=True)
            weights = jnp.exp2((scores - peak) * factor)
            inverse = 1.0 / jnp.sum(weights, axis=1, keepdims=True)
            p_ref[head * TILE : (head + 1) * TILE, :] = (weights * inverse).astype(jnp.bfloat16)


def probs_of(lengths, queries, keys, kv_head, after):
    rows = keys.shape[0]
    wide = GROUP * HEAD_SIZE
    shapes = [(GROUP * TILE, width) for _, _, width in windows(rows)]
    elements = sum(a * b for a, b in shapes)
    return pl.pallas_call(
        functools.partial(probs_kernel, len(after)),
        grid=(1,),
        out_shape=[jax.ShapeDtypeStruct(s, jnp.bfloat16) for s in shapes],
        in_specs=[
            SMEM,
            pl.BlockSpec((rows, wide), lambda i: (0, kv_head)),
            pl.BlockSpec((rows, HEAD_SIZE), lambda i: (0, kv_head)),
        ]
        + [pl.BlockSpec(memory_space=pl.ANY)] * len(after),
        out_specs=[pl.BlockSpec(s, lambda i: (0, 0)) for s in shapes],
        cost_estimate=pl.CostEstimate(
            flops=2_300_000_000, bytes_accessed=2 * (rows * wide + elements), transcendentals=elements
        ),
        compiler_params=pltpu.CompilerParams(vmem_limit_bytes=12 * 2**20),
        name="probs",
    )(lengths, queries, keys, *after)


def lowrank_kernel(at, count, ids_ref, adapter_ref, x_ref, *refs):
    w_refs, out_ref = refs[:count], refs[-1]
    before_ref = refs[count] if at > 0 else None
    adapter = adapter_ref[...]
    rows, features = x_ref.shape
    half = w_refs[0].shape[0]
    stacked = jnp.concatenate([w_ref[:, :features] for w_ref in w_refs], axis=0)
    product = lax.dot_general(x_ref[...], stacked, NT, preferred_element_type=jnp.float32)
    sums = [jnp.zeros((rows, half), jnp.float32)] * 2
    for i in range(count):
        part = product[:, i * half : (i + 1) * half]
        sums[i % 2] = sums[i % 2] + jnp.where(adapter == ids_ref[at + i // 2], part, 0.0)
    total = jnp.concatenate(sums, axis=1)
    out_ref[...] = total if before_ref is None else total + before_ref[...]


def lowrank_of(ids, at, adapter_of_row, x, before, pieces, after):
    rows, features = x.shape
    rank = 2 * pieces[0].shape[0]
    operands = [ids, adapter_of_row, x] + pieces + ([] if before is None else [before])
    used = len(operands)
    operands = operands + after
    size = 2 * sum(p.size for p in pieces)
    return pl.pallas_call(
        functools.partial(lowrank_kernel, at, len(pieces)),
        out_shape=jax.ShapeDtypeStruct((rows, rank), jnp.float32),
        in_specs=[SMEM] + [VMEM] * (used - 1) + [pl.BlockSpec(memory_space=pl.ANY)] * len(after),
        out_specs=VMEM,
        cost_estimate=pl.CostEstimate(
            flops=1_700_000_000, bytes_accessed=2 * rows * features + size, transcendentals=0
        ),
        compiler_params=pltpu.CompilerParams(vmem_limit_bytes=8 * 2**20 + 2 * x.size + 2 * size),
        name="lowrank",
    )(*operands)


def attend_kernel(kv_heads, n, ids_ref, adapter_ref, mine_ref, theirs_ref, base_ref, *refs):
    rows, value_portion = base_ref.shape
    tiles = windows(rows)
    low_refs, high_refs = refs[:n], refs[n : 2 * n]
    p_refs = refs[2 * n : 2 * n + kv_heads * len(tiles)]
    out_ref, block, sems = refs[2 * n + kv_heads * len(tiles) :]
    rank = mine_ref.shape[1]
    features = low_refs[0].shape[1] - value_portion
    adapter = adapter_ref[...]
    lowrank = (mine_ref[...] + theirs_ref[...]).astype(jnp.bfloat16)
    twice = jnp.concatenate([lowrank, lowrank], axis=1)
    second = lax.broadcasted_iota(jnp.int32, twice.shape, 1) >= rank
    spread = jnp.concatenate(
        [
            jnp.where(adapter == jnp.where(second, ids_ref[i + 1], ids_ref[i]), twice, jnp.zeros_like(twice))
            for i in range(0, n, 2)
        ],
        axis=1,
    )
    copies = []
    wide = GROUP * HEAD_SIZE
    for kv in range(kv_heads):
        columns = slice(kv * HEAD_SIZE, (kv + 1) * HEAD_SIZE)
        held = slice(features + kv * HEAD_SIZE, features + (kv + 1) * HEAD_SIZE)
        up = jnp.concatenate([ref[:, held] for pair in zip(low_refs, high_refs) for ref in pair], axis=0)
        delta = jnp.dot(spread, up, preferred_element_type=jnp.float32).astype(jnp.bfloat16)
        values = (
            base_ref[:, columns].astype(jnp.float32) + adapter_scale * delta.astype(jnp.float32)
        ).astype(jnp.bfloat16)
        for i, (start, first, width) in enumerate(tiles):
            mixed = jnp.dot(
                p_refs[kv * len(tiles) + i][...],
                values[first : first + width, :],
                preferred_element_type=jnp.float32,
            ).astype(jnp.bfloat16)
            for head in range(GROUP):
                at = kv * wide + head * HEAD_SIZE
                block[start : start + TILE, at : at + HEAD_SIZE] = mixed[head * TILE : (head + 1) * TILE, :]
        copy = pltpu.make_async_copy(
            block.at[:, kv * wide : (kv + 1) * wide],
            out_ref.at[:, kv * wide : (kv + 1) * wide],
            sems.at[kv],
        )
        copy.start()
        copies.append(copy)
    for copy in copies:
        copy.wait()


def attend(ids, adapter_of_row, mine, theirs, base, lows, highs, probs):
    rows, value_portion = base.shape
    kv_heads = value_portion // HEAD_SIZE
    wide = kv_heads * GROUP * HEAD_SIZE
    flat = [p for per_head in probs for p in per_head]
    held = 2 * sum(a.size for a in lows + highs + flat)
    return pl.pallas_call(
        functools.partial(attend_kernel, kv_heads, len(lows)),
        out_shape=jax.ShapeDtypeStruct((rows, wide), jnp.bfloat16),
        in_specs=[SMEM] + [VMEM] * (4 + len(lows) + len(highs) + len(flat)),
        out_specs=pl.BlockSpec(memory_space=pl.ANY),
        scratch_shapes=[pltpu.VMEM((rows, wide), jnp.bfloat16), pltpu.SemaphoreType.DMA((kv_heads,))],
        compiler_params=pltpu.CompilerParams(vmem_limit_bytes=12 * 2**20),
        name="attend",
    )(ids, adapter_of_row, mine, theirs, base, *lows, *highs, *flat)


def on_device(
    normed_token_rows,
    base_value_rows,
    queries,
    stacked_key_rows,
    adapter_of_row,
    sequence_lengths,
    adapter_down_weight,
    adapter_up_weight,
):
    n = lax.axis_size("rep")
    order = ring_order(n)
    ahead = [(order[i], order[(i + 1) % n]) for i in range(n)]
    back = [(b, a) for a, b in ahead]
    far = n // 2
    distances = [0] + [d for step in range(1, far) for d in (step, -step)] + [far]
    table = np.zeros((n, n), np.int32)
    for place, replica in enumerate(order):
        table[replica] = [order[(place - d) % n] for d in distances]
    ids = lax.dynamic_index_in_dim(jnp.asarray(table), lax.axis_index("rep"), 0, keepdims=False)

    down = jnp.swapaxes(adapter_down_weight[0], 0, 1)
    both = jnp.concatenate([down, adapter_up_weight[0]], axis=1)
    half = both.shape[0] // 2

    def pass_round(piece, steps_ahead, steps_back):
        held = {0: piece}
        moving_ahead = moving_back = piece
        for step in range(1, far + 1):
            if step <= steps_ahead:
                moving_ahead = lax.ppermute(moving_ahead, "rep", ahead)
                held[step] = moving_ahead
            if step <= steps_back:
                moving_back = lax.ppermute(moving_back, "rep", back)
                held[-step if step < far else far] = moving_back
        return held

    low = pass_round(both[:half], far, far - 1)
    high = pass_round(both[half:], far - 1, far)

    kv_heads = stacked_key_rows.shape[1] // HEAD_SIZE
    arrivals = [[piece[d] for d in (step, -step)] for step in range(1, far) for piece in (low, high)]
    probs = [
        probs_of(sequence_lengths, queries, stacked_key_rows, kv, arrivals[kv - 1] if kv > 0 else [])
        for kv in range(kv_heads)
    ]

    partial = None
    for lo, hi in [(0, 3)] + [(a, a + 2) for a in range(3, n - 1, 2)] + [(n - 1, n)]:
        pieces = [piece for d in distances[lo:hi] for piece in (low[d], high[d])]
        after = arrivals[kv_heads - 1] if lo == 0 else []
        if hi == n:
            after = [p[0] for p in probs]
        partial = lowrank_of(ids, lo, adapter_of_row, normed_token_rows, partial, pieces, after)
    other = lax.ppermute(partial, "tp", [(0, 1), (1, 0)])
    return attend(
        ids,
        adapter_of_row,
        partial,
        other,
        base_value_rows,
        [low[d] for d in distances],
        [high[d] for d in distances],
        probs,
    )


def solution(mesh):
    placed = (
        P(("groups", "rep"), "tp"),
        P(("groups", "rep"), "tp"),
        P(("groups", "rep"), "tp"),
        P(("groups", "rep"), "tp"),
        P(("groups", "rep"), None),
        P(("groups", "rep"), None),
        P(("groups", "rep"), "tp", None),
        P(("groups", "rep"), None, "tp"),
    )
    return jax.shard_map(
        on_device, mesh=mesh, in_specs=placed, out_specs=P(("groups", "rep"), "tp"), check_vma=False
    )
```

```python
import functools

import jax
import jax.numpy as jnp
import numpy as np
from jax import lax
from jax.experimental import pallas as pl
from jax.experimental.pallas import tpu as pltpu
from jax.sharding import PartitionSpec as P

HEADS = 64
KEY_VALUE_HEADS = 8
HEAD_SIZE = 128
GROUP = HEADS // KEY_VALUE_HEADS
LONGEST = 192
TILE = 64
REACH = -(-(LONGEST - 1) // TILE)
adapter_scale = 2.0

VMEM = pl.BlockSpec(memory_space=pltpu.VMEM)
SMEM = pl.BlockSpec(memory_space=pltpu.SMEM)
NT = (((1,), (1,)), ((), ()))


def ring_order(n):
    if n == 8:
        return list(range(0, n, 2)) + list(range(n - 1, 0, -2))
    return list(range(n))


def windows(rows):
    found = []
    for tile in range(rows // TILE):
        first = max(0, tile - REACH) * TILE
        width = (tile + 1) * TILE - first
        width = -(-width // 128) * 128
        found.append((tile * TILE, first, width))
    return found


def probs_kernel(waits, lengths_ref, q_ref, k_ref, *refs):
    p_refs = refs[waits:]
    rows = k_ref.shape[0]
    ends = []
    total = jnp.int32(0)
    for i in range(lengths_ref.shape[1]):
        total = total + lengths_ref[0, i]
        ends.append(total)
    factor = float(np.log2(np.e) * HEAD_SIZE**-0.5)
    for p_ref, (start, first, width) in zip(p_refs, windows(rows)):
        t = lax.broadcasted_iota(jnp.int32, (TILE, width), 0) + start
        s = lax.broadcasted_iota(jnp.int32, (TILE, width), 1) + first
        allowed = s <= t
        for end in ends:
            allowed = allowed & ((t >= end) == (s >= end))
        bias = jnp.where(allowed, 0.0, -1e30)
        keys = k_ref[first : first + width, :]
        for head in range(GROUP):
            q = q_ref[start : start + TILE, head * HEAD_SIZE : (head + 1) * HEAD_SIZE]
            scores = lax.dot_general(q, keys, NT, preferred_element_type=jnp.float32) + bias
            peak = jnp.max(scores, axis=1, keepdims=True)
            weights = jnp.exp2((scores - peak) * factor)
            inverse = 1.0 / jnp.sum(weights, axis=1, keepdims=True)
            p_ref[head * TILE : (head + 1) * TILE, :] = (weights * inverse).astype(jnp.bfloat16)


def probs_of(lengths, queries, keys, kv_head, after):
    rows = keys.shape[0]
    wide = GROUP * HEAD_SIZE
    shapes = [(GROUP * TILE, width) for _, _, width in windows(rows)]
    elements = sum(a * b for a, b in shapes)
    return pl.pallas_call(
        functools.partial(probs_kernel, len(after)),
        grid=(1,),
        out_shape=[jax.ShapeDtypeStruct(s, jnp.bfloat16) for s in shapes],
        in_specs=[
            SMEM,
            pl.BlockSpec((rows, wide), lambda i: (0, kv_head)),
            pl.BlockSpec((rows, HEAD_SIZE), lambda i: (0, kv_head)),
        ]
        + [pl.BlockSpec(memory_space=pl.ANY)] * len(after),
        out_specs=[pl.BlockSpec(s, lambda i: (0, 0)) for s in shapes],
        cost_estimate=pl.CostEstimate(
            flops=2_300_000_000, bytes_accessed=2 * (rows * wide + elements), transcendentals=elements
        ),
        compiler_params=pltpu.CompilerParams(vmem_limit_bytes=12 * 2**20),
        name="probs",
    )(lengths, queries, keys, *after)


def lowrank_kernel(at, count, place_ref, x_ref, *refs):
    w_refs, out_ref = refs[:count], refs[-1]
    before_ref = refs[count] if at > 0 else None
    place = place_ref[...]
    rows, features = x_ref.shape
    half = w_refs[0].shape[0]
    stacked = jnp.concatenate([w_ref[:, :features] for w_ref in w_refs], axis=0)
    product = lax.dot_general(x_ref[...], stacked, NT, preferred_element_type=jnp.float32)
    sums = [jnp.zeros((rows, half), jnp.float32)] * 2
    for i in range(count):
        part = product[:, i * half : (i + 1) * half]
        sums[i % 2] = sums[i % 2] + jnp.where(place == at + i // 2, part, 0.0)
    total = jnp.concatenate(sums, axis=1)
    out_ref[...] = total if before_ref is None else total + before_ref[...]


def lowrank_of(at, place, x, before, pieces, after):
    rows, features = x.shape
    rank = 2 * pieces[0].shape[0]
    operands = [place, x] + pieces + ([] if before is None else [before])
    used = len(operands)
    operands = operands + after
    size = 2 * sum(p.size for p in pieces)
    return pl.pallas_call(
        functools.partial(lowrank_kernel, at, len(pieces)),
        out_shape=jax.ShapeDtypeStruct((rows, rank), jnp.float32),
        in_specs=[VMEM] * used + [pl.BlockSpec(memory_space=pl.ANY)] * len(after),
        out_specs=VMEM,
        cost_estimate=pl.CostEstimate(
            flops=1_700_000_000, bytes_accessed=2 * rows * features + size, transcendentals=0
        ),
        compiler_params=pltpu.CompilerParams(vmem_limit_bytes=8 * 2**20 + 2 * x.size + 2 * size),
        name="lowrank",
    )(*operands)


def attend_kernel(kv_heads, n, place_ref, mine_ref, theirs_ref, base_ref, *refs):
    rows, value_portion = base_ref.shape
    tiles = windows(rows)
    low_refs, high_refs = refs[:n], refs[n : 2 * n]
    p_refs = refs[2 * n : 2 * n + kv_heads * len(tiles)]
    out_ref, block, sems = refs[2 * n + kv_heads * len(tiles) :]
    rank = mine_ref.shape[1]
    features = low_refs[0].shape[1] - value_portion
    place = place_ref[...]
    lowrank = (mine_ref[...] + theirs_ref[...]).astype(jnp.bfloat16)
    twice = jnp.concatenate([lowrank, lowrank], axis=1)
    second = (lax.broadcasted_iota(jnp.int32, twice.shape, 1) >= rank).astype(jnp.int32)
    offset = place - second
    spread = jnp.concatenate(
        [jnp.where(offset == i, twice, jnp.zeros_like(twice)) for i in range(0, n, 2)], axis=1
    )
    up = jnp.concatenate(
        [ref[:, features:] for pair in zip(low_refs, high_refs) for ref in pair], axis=0
    )
    delta = jnp.dot(spread, up, preferred_element_type=jnp.float32).astype(jnp.bfloat16)
    values = (
        base_ref[...].astype(jnp.float32) + adapter_scale * delta.astype(jnp.float32)
    ).astype(jnp.bfloat16)
    copies = []
    wide = GROUP * HEAD_SIZE
    done = 0
    for kv in range(kv_heads):
        columns = slice(kv * HEAD_SIZE, (kv + 1) * HEAD_SIZE)
        for i, (start, first, width) in enumerate(tiles):
            mixed = jnp.dot(
                p_refs[kv * len(tiles) + i][...],
                values[first : first + width, columns],
                preferred_element_type=jnp.float32,
            ).astype(jnp.bfloat16)
            for head in range(GROUP):
                at = kv * wide + head * HEAD_SIZE
                block[start : start + TILE, at : at + HEAD_SIZE] = mixed[head * TILE : (head + 1) * TILE, :]
            if 2 * (i + 1) in (len(tiles), 2 * len(tiles)):
                part = slice(0, rows // 2) if 2 * (i + 1) == len(tiles) else slice(rows // 2, rows)
                span = slice(kv * wide, (kv + 1) * wide)
                copy = pltpu.make_async_copy(block.at[part, span], out_ref.at[part, span], sems.at[done])
                copy.start()
                copies.append(copy)
                done += 1
    for copy in copies:
        copy.wait()


def attend(place, mine, theirs, base, lows, highs, probs):
    rows, value_portion = base.shape
    kv_heads = value_portion // HEAD_SIZE
    wide = kv_heads * GROUP * HEAD_SIZE
    flat = [p for per_head in probs for p in per_head]
    return pl.pallas_call(
        functools.partial(attend_kernel, kv_heads, len(lows)),
        out_shape=jax.ShapeDtypeStruct((rows, wide), jnp.bfloat16),
        in_specs=[VMEM] * (4 + len(lows) + len(highs) + len(flat)),
        out_specs=pl.BlockSpec(memory_space=pl.ANY),
        scratch_shapes=[pltpu.VMEM((rows, wide), jnp.bfloat16), pltpu.SemaphoreType.DMA((2 * kv_heads,))],
        compiler_params=pltpu.CompilerParams(vmem_limit_bytes=12 * 2**20),
        name="attend",
    )(place, mine, theirs, base, *lows, *highs, *flat)


def on_device(
    normed_token_rows,
    base_value_rows,
    queries,
    stacked_key_rows,
    adapter_of_row,
    sequence_lengths,
    adapter_down_weight,
    adapter_up_weight,
):
    n = lax.axis_size("rep")
    order = ring_order(n)
    ahead = [(order[i], order[(i + 1) % n]) for i in range(n)]
    back = [(b, a) for a, b in ahead]
    far = n // 2
    distances = [0] + [d for step in range(1, far) for d in (step, -step)] + [far]
    table = np.zeros((n, n), np.int32)
    for place, replica in enumerate(order):
        table[replica] = [order[(place - d) % n] for d in distances]
    ids = lax.dynamic_slice_in_dim(jnp.asarray(table), lax.axis_index("rep"), 1, 0)
    place = jnp.sum(
        jnp.where(adapter_of_row == ids, jnp.arange(n, dtype=jnp.int32)[None, :], 0), axis=1, keepdims=True
    )

    down = jnp.swapaxes(adapter_down_weight[0], 0, 1)
    both = jnp.concatenate([down, adapter_up_weight[0]], axis=1)
    half = both.shape[0] // 2

    def pass_round(piece, steps_ahead, steps_back):
        held = {0: piece}
        moving_ahead = moving_back = piece
        for step in range(1, far + 1):
            if step <= steps_ahead:
                moving_ahead = lax.ppermute(moving_ahead, "rep", ahead)
                held[step] = moving_ahead
            if step <= steps_back:
                moving_back = lax.ppermute(moving_back, "rep", back)
                held[-step if step < far else far] = moving_back
        return held

    low = pass_round(both[:half], far, far - 1)
    high = pass_round(both[half:], far - 1, far)

    kv_heads = stacked_key_rows.shape[1] // HEAD_SIZE
    arrivals = [[piece[d] for d in (step, -step)] for step in range(1, far) for piece in (low, high)]
    probs = [
        probs_of(sequence_lengths, queries, stacked_key_rows, kv, arrivals[kv - 1] if kv > 0 else [])
        for kv in range(kv_heads)
    ]

    partial = None
    for lo, hi in [(0, 3)] + [(a, a + 2) for a in range(3, n - 1, 2)] + [(n - 1, n)]:
        pieces = [piece for d in distances[lo:hi] for piece in (low[d], high[d])]
        after = arrivals[kv_heads - 1] if lo == 0 else []
        if hi == n:
            after = [p[0] for p in probs]
        partial = lowrank_of(lo, place, normed_token_rows, partial, pieces, after)
    other = lax.ppermute(partial, "tp", [(0, 1), (1, 0)])
    return attend(
        place,
        partial,
        other,
        base_value_rows,
        [low[d] for d in distances],
        [high[d] for d in distances],
        probs,
    )


def solution(mesh):
    placed = (
        P(("groups", "rep"), "tp"),
        P(("groups", "rep"), "tp"),
        P(("groups", "rep"), "tp"),
        P(("groups", "rep"), "tp"),
        P(("groups", "rep"), None),
        P(("groups", "rep"), None),
        P(("groups", "rep"), "tp", None),
        P(("groups", "rep"), None, "tp"),
    )
    return jax.shard_map(
        on_device, mesh=mesh, in_specs=placed, out_specs=P(("groups", "rep"), "tp"), check_vma=False
    )
```

```python
import functools

import jax
import jax.numpy as jnp
import numpy as np
from jax import lax
from jax.experimental import pallas as pl
from jax.experimental.pallas import tpu as pltpu
from jax.sharding import PartitionSpec as P

HEADS = 64
KEY_VALUE_HEADS = 8
HEAD_SIZE = 128
GROUP = HEADS // KEY_VALUE_HEADS
LONGEST = 192
TILE = 64
REACH = -(-(LONGEST - 1) // TILE)
adapter_scale = 2.0

VMEM = pl.BlockSpec(memory_space=pltpu.VMEM)
SMEM = pl.BlockSpec(memory_space=pltpu.SMEM)
NT = (((1,), (1,)), ((), ()))


def ring_order(n):
    if n == 8:
        return list(range(0, n, 2)) + list(range(n - 1, 0, -2))
    return list(range(n))


def windows(rows):
    found = []
    for tile in range(rows // TILE):
        first = max(0, tile - REACH) * TILE
        width = (tile + 1) * TILE - first
        width = -(-width // 128) * 128
        found.append((tile * TILE, first, width))
    return found


def ring_place(replica, n):
    if n == 8:
        return jnp.where(replica & 1 == 0, replica >> 1, n - 1 - (replica >> 1))
    return replica


def column(row):
    wide = jnp.broadcast_to(row.astype(jnp.float32), (8, row.shape[1]))
    return wide.T[:, :1].astype(jnp.int32)


def masks_kernel(n, me_ref, lengths_ref, adapter_ref, near_q_ref, near_k_ref, *refs):
    place_ref, segment_ref, across_ref = refs
    distance = ring_place(me_ref[0], n) - ring_place(adapter_ref[...], n)
    distance = jnp.where(distance < 0, distance + n, distance)
    place = jnp.where(distance <= n // 2, jnp.maximum(2 * distance - 1, 0), 2 * (n - distance))
    place_ref[...] = column(place)
    position = lax.broadcasted_iota(jnp.int32, place.shape, 1)
    segment = jnp.zeros(place.shape, jnp.int32)
    end = jnp.int32(0)
    for i in range(lengths_ref.shape[1]):
        end = end + lengths_ref[0, i]
        segment = segment + (position >= end).astype(jnp.int32)
    across_ref[...] = segment
    segment_ref[...] = column(segment)


def masks(n, lengths, adapter_row, queries, keys):
    rows = keys.shape[0]
    tall = jax.ShapeDtypeStruct((rows, 1), jnp.int32)
    me = jnp.reshape(lax.axis_index("rep"), (1,)).astype(jnp.int32)
    return pl.pallas_call(
        functools.partial(masks_kernel, n),
        out_shape=[tall, tall, jax.ShapeDtypeStruct((1, rows), jnp.int32)],
        in_specs=[SMEM, SMEM, VMEM, VMEM, VMEM],
        out_specs=[VMEM] * 3,
        cost_estimate=pl.CostEstimate(flops=1_000_000_000, bytes_accessed=16 * rows, transcendentals=0),
        compiler_params=pltpu.CompilerParams(vmem_limit_bytes=4 * 2**20),
        name="masks",
    )(me, lengths, adapter_row, queries, keys)


def probs_kernel(kv_head, segment_ref, across_ref, q_ref, k_ref, *refs):
    rows = k_ref.shape[0]
    tiles = windows(rows)
    p_refs = refs[-len(tiles) :]
    factor = float(np.log2(np.e) * HEAD_SIZE**-0.5)
    at = kv_head * HEAD_SIZE
    for p_ref, (start, first, width) in zip(p_refs, tiles):
        t = lax.broadcasted_iota(jnp.int32, (TILE, width), 0) + start
        s = lax.broadcasted_iota(jnp.int32, (TILE, width), 1) + first
        same = segment_ref[start : start + TILE, :] == across_ref[:, first : first + width]
        bias = jnp.where(same & (s <= t), 0.0, -1e30)
        keys = k_ref[first : first + width, at : at + HEAD_SIZE]
        for head in range(GROUP):
            column_at = (kv_head * GROUP + head) * HEAD_SIZE
            q = q_ref[start : start + TILE, column_at : column_at + HEAD_SIZE]
            scores = lax.dot_general(q, keys, NT, preferred_element_type=jnp.float32) + bias
            peak = jnp.max(scores, axis=1, keepdims=True)
            weights = jnp.exp2((scores - peak) * factor)
            inverse = 1.0 / jnp.sum(weights, axis=1, keepdims=True)
            p_ref[head * TILE : (head + 1) * TILE, :] = (weights * inverse).astype(jnp.bfloat16)


def probs_of(segment, across, queries, keys, kv_head, after):
    rows = keys.shape[0]
    shapes = [(GROUP * TILE, width) for _, _, width in windows(rows)]
    elements = sum(a * b for a, b in shapes)
    return pl.pallas_call(
        functools.partial(probs_kernel, kv_head),
        out_shape=[jax.ShapeDtypeStruct(s, jnp.bfloat16) for s in shapes],
        in_specs=[VMEM] * 4 + [pl.BlockSpec(memory_space=pl.ANY)] * len(after),
        out_specs=[VMEM] * len(shapes),
        cost_estimate=pl.CostEstimate(
            flops=2_000_000_000, bytes_accessed=2 * elements, transcendentals=elements
        ),
        compiler_params=pltpu.CompilerParams(vmem_limit_bytes=12 * 2**20),
        name="probs",
    )(segment, across, queries, keys, *after)


def lowrank_kernel(at, count, place_ref, x_ref, *refs):
    w_refs, out_ref = refs[:count], refs[-1]
    before_ref = refs[count] if at > 0 else None
    place = place_ref[...]
    rows, features = x_ref.shape
    half = w_refs[0].shape[0]
    stacked = jnp.concatenate([w_ref[:, :features] for w_ref in w_refs], axis=0)
    product = lax.dot_general(x_ref[...], stacked, NT, preferred_element_type=jnp.float32)
    sums = [jnp.zeros((rows, half), jnp.float32)] * 2
    for i in range(count):
        part = product[:, i * half : (i + 1) * half]
        sums[i % 2] = sums[i % 2] + jnp.where(place == at + i // 2, part, 0.0)
    total = jnp.concatenate(sums, axis=1)
    out_ref[...] = total if before_ref is None else total + before_ref[...]


def lowrank_of(at, place, x, before, pieces, after):
    rows, features = x.shape
    rank = 2 * pieces[0].shape[0]
    operands = [place, x] + pieces + ([] if before is None else [before])
    used = len(operands)
    operands = operands + after
    size = 2 * sum(p.size for p in pieces)
    return pl.pallas_call(
        functools.partial(lowrank_kernel, at, len(pieces)),
        out_shape=jax.ShapeDtypeStruct((rows, rank), jnp.float32),
        in_specs=[VMEM] * used + [pl.BlockSpec(memory_space=pl.ANY)] * len(after),
        out_specs=VMEM,
        cost_estimate=pl.CostEstimate(
            flops=1_700_000_000, bytes_accessed=2 * rows * features + size, transcendentals=0
        ),
        compiler_params=pltpu.CompilerParams(vmem_limit_bytes=8 * 2**20 + 2 * x.size + 2 * size),
        name="lowrank",
    )(*operands)


def attend_kernel(kv_heads, n, place_ref, mine_ref, theirs_ref, base_ref, *refs):
    rows, value_portion = base_ref.shape
    tiles = windows(rows)
    low_refs, high_refs = refs[:n], refs[n : 2 * n]
    p_refs = refs[2 * n : 2 * n + kv_heads * len(tiles)]
    out_ref, block, sems = refs[2 * n + kv_heads * len(tiles) :]
    rank = mine_ref.shape[1]
    features = low_refs[0].shape[1] - value_portion
    place = place_ref[...]
    lowrank = (mine_ref[...] + theirs_ref[...]).astype(jnp.bfloat16)
    twice = jnp.concatenate([lowrank, lowrank], axis=1)
    second = (lax.broadcasted_iota(jnp.int32, twice.shape, 1) >= rank).astype(jnp.int32)
    offset = place - second
    spread = jnp.concatenate(
        [jnp.where(offset == i, twice, jnp.zeros_like(twice)) for i in range(0, n, 2)], axis=1
    )
    up = jnp.concatenate(
        [ref[:, features:] for pair in zip(low_refs, high_refs) for ref in pair], axis=0
    )
    delta = jnp.dot(spread, up, preferred_element_type=jnp.float32).astype(jnp.bfloat16)
    values = (
        base_ref[...].astype(jnp.float32) + adapter_scale * delta.astype(jnp.float32)
    ).astype(jnp.bfloat16)
    copies = []
    wide = GROUP * HEAD_SIZE
    done = 0
    for kv in range(kv_heads):
        columns = slice(kv * HEAD_SIZE, (kv + 1) * HEAD_SIZE)
        for i, (start, first, width) in enumerate(tiles):
            mixed = jnp.dot(
                p_refs[kv * len(tiles) + i][...],
                values[first : first + width, columns],
                preferred_element_type=jnp.float32,
            ).astype(jnp.bfloat16)
            for head in range(GROUP):
                at = kv * wide + head * HEAD_SIZE
                block[start : start + TILE, at : at + HEAD_SIZE] = mixed[head * TILE : (head + 1) * TILE, :]
            if 2 * (i + 1) in (len(tiles), 2 * len(tiles)):
                part = slice(0, rows // 2) if 2 * (i + 1) == len(tiles) else slice(rows // 2, rows)
                span = slice(kv * wide, (kv + 1) * wide)
                copy = pltpu.make_async_copy(block.at[part, span], out_ref.at[part, span], sems.at[done])
                copy.start()
                copies.append(copy)
                done += 1
    for copy in copies:
        copy.wait()


def attend(place, mine, theirs, base, lows, highs, probs):
    rows, value_portion = base.shape
    kv_heads = value_portion // HEAD_SIZE
    wide = kv_heads * GROUP * HEAD_SIZE
    flat = [p for per_head in probs for p in per_head]
    return pl.pallas_call(
        functools.partial(attend_kernel, kv_heads, len(lows)),
        out_shape=jax.ShapeDtypeStruct((rows, wide), jnp.bfloat16),
        in_specs=[VMEM] * (4 + len(lows) + len(highs) + len(flat)),
        out_specs=pl.BlockSpec(memory_space=pl.ANY),
        scratch_shapes=[pltpu.VMEM((rows, wide), jnp.bfloat16), pltpu.SemaphoreType.DMA((2 * kv_heads,))],
        compiler_params=pltpu.CompilerParams(vmem_limit_bytes=12 * 2**20),
        name="attend",
    )(place, mine, theirs, base, *lows, *highs, *flat)


def on_device(
    normed_token_rows,
    base_value_rows,
    queries,
    stacked_key_rows,
    adapter_of_row,
    sequence_lengths,
    adapter_down_weight,
    adapter_up_weight,
):
    n = lax.axis_size("rep")
    order = ring_order(n)
    ahead = [(order[i], order[(i + 1) % n]) for i in range(n)]
    back = [(b, a) for a, b in ahead]
    far = n // 2
    distances = [0] + [d for step in range(1, far) for d in (step, -step)] + [far]
    down = jnp.swapaxes(adapter_down_weight[0], 0, 1)
    both = jnp.concatenate([down, adapter_up_weight[0]], axis=1)
    rank = both.shape[0]
    own_low, own_high = both[: rank // 2], both[rank // 2 :]
    place, segment, across = masks(
        n, sequence_lengths, adapter_of_row.reshape(1, -1), queries, stacked_key_rows
    )
    low, high = {0: own_low}, {0: own_high}

    def pass_round(held, pairs, sign, steps):
        piece = held[0]
        for step in range(1, steps + 1):
            piece = lax.ppermute(piece, "rep", pairs)
            held[sign * step if step < far else far] = piece

    pass_round(high, ahead, 1, far - 1)
    pass_round(low, back, -1, far - 1)
    pass_round(high, back, -1, far)
    pass_round(low, ahead, 1, far)

    kv_heads = stacked_key_rows.shape[1] // HEAD_SIZE
    arrivals = [
        pair
        for step in range(1, far)
        for pair in ([low[step], high[-step]], [high[step], low[-step]])
    ]
    probs = [
        probs_of(segment, across, queries, stacked_key_rows, kv, arrivals[kv // 2]) for kv in range(kv_heads)
    ]

    partial = None
    for lo, hi in [(0, 3)] + [(a, a + 2) for a in range(3, n - 1, 2)] + [(n - 1, n)]:
        pieces = [piece for d in distances[lo:hi] for piece in (low[d], high[d])]
        after = arrivals[kv_heads - 1] if lo == 0 else []
        if hi == n:
            after = [p[0] for p in probs]
        partial = lowrank_of(lo, place, normed_token_rows, partial, pieces, after)
    other = lax.ppermute(partial, "tp", [(0, 1), (1, 0)])
    return attend(
        place,
        partial,
        other,
        base_value_rows,
        [low[d] for d in distances],
        [high[d] for d in distances],
        probs,
    )


def solution(mesh):
    placed = (
        P(("groups", "rep"), "tp"),
        P(("groups", "rep"), "tp"),
        P(("groups", "rep"), "tp"),
        P(("groups", "rep"), "tp"),
        P(("groups", "rep"), None),
        P(("groups", "rep"), None),
        P(("groups", "rep"), "tp", None),
        P(("groups", "rep"), None, "tp"),
    )
    return jax.shard_map(
        on_device, mesh=mesh, in_specs=placed, out_specs=P(("groups", "rep"), "tp"), check_vma=False
    )
```

```python
import functools

import jax
import jax.numpy as jnp
import numpy as np
from jax import lax
from jax.experimental import pallas as pl
from jax.experimental.pallas import tpu as pltpu
from jax.sharding import PartitionSpec as P

HEADS = 64
KEY_VALUE_HEADS = 8
HEAD_SIZE = 128
GROUP = HEADS // KEY_VALUE_HEADS
LONGEST = 192
TILE = 64
REACH = -(-(LONGEST - 1) // TILE)
adapter_scale = 2.0

VMEM = pl.BlockSpec(memory_space=pltpu.VMEM)
SMEM = pl.BlockSpec(memory_space=pltpu.SMEM)
NT = (((1,), (1,)), ((), ()))


def ring_order(n):
    if n == 8:
        return list(range(0, n, 2)) + list(range(n - 1, 0, -2))
    return list(range(n))


def windows(rows):
    found = []
    for tile in range(rows // TILE):
        first = max(0, tile - REACH) * TILE
        width = (tile + 1) * TILE - first
        width = -(-width // 128) * 128
        found.append((tile * TILE, first, width))
    return found


def ring_place(replica, n):
    if n == 8:
        return jnp.where(replica & 1 == 0, replica >> 1, n - 1 - (replica >> 1))
    return replica


def column(row):
    wide = jnp.broadcast_to(row.astype(jnp.float32), (8, row.shape[1]))
    return wide.T[:, :1].astype(jnp.int32)


def masks_kernel(n, me_ref, lengths_ref, adapter_ref, near_q_ref, near_k_ref, *refs):
    place_ref, segment_ref, across_ref = refs
    distance = ring_place(me_ref[0], n) - ring_place(adapter_ref[...], n)
    distance = jnp.where(distance < 0, distance + n, distance)
    place = jnp.where(distance <= n // 2, jnp.maximum(2 * distance - 1, 0), 2 * (n - distance))
    place_ref[...] = column(place)
    position = lax.broadcasted_iota(jnp.int32, place.shape, 1)
    segment = jnp.zeros(place.shape, jnp.int32)
    end = jnp.int32(0)
    for i in range(lengths_ref.shape[1]):
        end = end + lengths_ref[0, i]
        segment = segment + (position >= end).astype(jnp.int32)
    across_ref[...] = segment
    segment_ref[...] = column(segment)


def masks(n, lengths, adapter_row, queries, keys):
    rows = keys.shape[0]
    tall = jax.ShapeDtypeStruct((rows, 1), jnp.int32)
    me = jnp.reshape(lax.axis_index("rep"), (1,)).astype(jnp.int32)
    return pl.pallas_call(
        functools.partial(masks_kernel, n),
        out_shape=[tall, tall, jax.ShapeDtypeStruct((1, rows), jnp.int32)],
        in_specs=[SMEM, SMEM, VMEM, VMEM, VMEM],
        out_specs=[VMEM] * 3,
        cost_estimate=pl.CostEstimate(flops=1_000_000_000, bytes_accessed=16 * rows, transcendentals=0),
        compiler_params=pltpu.CompilerParams(vmem_limit_bytes=4 * 2**20),
        name="masks",
    )(me, lengths, adapter_row, queries, keys)


def probs_kernel(kv_head, segment_ref, across_ref, q_ref, k_ref, *refs):
    rows = k_ref.shape[0]
    tiles = windows(rows)
    p_refs = refs[-len(tiles) :]
    factor = float(np.log2(np.e) * HEAD_SIZE**-0.5)
    at = kv_head * HEAD_SIZE
    for p_ref, (start, first, width) in zip(p_refs, tiles):
        t = lax.broadcasted_iota(jnp.int32, (TILE, width), 0) + start
        s = lax.broadcasted_iota(jnp.int32, (TILE, width), 1) + first
        same = segment_ref[start : start + TILE, :] == across_ref[:, first : first + width]
        bias = jnp.where(same & (s <= t), 0.0, -1e30)
        keys = k_ref[first : first + width, at : at + HEAD_SIZE]
        for head in range(GROUP):
            column_at = (kv_head * GROUP + head) * HEAD_SIZE
            q = q_ref[start : start + TILE, column_at : column_at + HEAD_SIZE]
            scores = lax.dot_general(q, keys, NT, preferred_element_type=jnp.float32) + bias
            peak = jnp.max(scores, axis=1, keepdims=True)
            weights = jnp.exp2((scores - peak) * factor)
            inverse = 1.0 / jnp.sum(weights, axis=1, keepdims=True)
            p_ref[head * TILE : (head + 1) * TILE, :] = (weights * inverse).astype(jnp.bfloat16)


def probs_of(segment, across, queries, keys, kv_head, after):
    rows = keys.shape[0]
    shapes = [(GROUP * TILE, width) for _, _, width in windows(rows)]
    elements = sum(a * b for a, b in shapes)
    return pl.pallas_call(
        functools.partial(probs_kernel, kv_head),
        out_shape=[jax.ShapeDtypeStruct(s, jnp.bfloat16) for s in shapes],
        in_specs=[VMEM] * 4 + [pl.BlockSpec(memory_space=pl.ANY)] * len(after),
        out_specs=[VMEM] * len(shapes),
        cost_estimate=pl.CostEstimate(
            flops=2_000_000_000, bytes_accessed=2 * elements, transcendentals=elements
        ),
        compiler_params=pltpu.CompilerParams(vmem_limit_bytes=12 * 2**20),
        name="probs",
    )(segment, across, queries, keys, *after)


def lowrank_kernel(at, count, place_ref, x_ref, *refs):
    w_refs, out_ref = refs[:count], refs[-1]
    before_ref = refs[count] if at > 0 else None
    place = place_ref[...]
    rows, features = x_ref.shape
    half = w_refs[0].shape[0]
    stacked = jnp.concatenate([w_ref[...] for w_ref in w_refs], axis=0)
    product = lax.dot_general(x_ref[...], stacked, NT, preferred_element_type=jnp.float32)
    sums = [jnp.zeros((rows, half), jnp.float32)] * 2
    for i in range(count):
        part = product[:, i * half : (i + 1) * half]
        sums[i % 2] = sums[i % 2] + jnp.where(place == at + i // 2, part, 0.0)
    total = jnp.concatenate(sums, axis=1)
    out_ref[...] = total if before_ref is None else total + before_ref[...]


def lowrank_of(at, place, x, before, pieces, after):
    rows, features = x.shape
    rank = 2 * pieces[0].shape[0]
    operands = [place, x] + pieces + ([] if before is None else [before])
    used = len(operands)
    operands = operands + after
    size = 2 * sum(p.size for p in pieces)
    return pl.pallas_call(
        functools.partial(lowrank_kernel, at, len(pieces)),
        out_shape=jax.ShapeDtypeStruct((rows, rank), jnp.float32),
        in_specs=[VMEM] * used + [pl.BlockSpec(memory_space=pl.ANY)] * len(after),
        out_specs=VMEM,
        cost_estimate=pl.CostEstimate(
            flops=1_700_000_000, bytes_accessed=2 * rows * features + size, transcendentals=0
        ),
        compiler_params=pltpu.CompilerParams(vmem_limit_bytes=8 * 2**20 + 2 * x.size + 2 * size),
        name="lowrank",
    )(*operands)


def attend_kernel(kv_heads, n, place_ref, mine_ref, theirs_ref, base_ref, *refs):
    rows = base_ref.shape[0]
    tiles = windows(rows)
    up_refs = refs[:n]
    p_refs = refs[n : n + kv_heads * len(tiles)]
    out_ref, block, sems = refs[n + kv_heads * len(tiles) :]
    rank = mine_ref.shape[1]
    place = place_ref[...]
    lowrank = (mine_ref[...] + theirs_ref[...]).astype(jnp.bfloat16)
    twice = jnp.concatenate([lowrank, lowrank], axis=1)
    second = (lax.broadcasted_iota(jnp.int32, twice.shape, 1) >= rank).astype(jnp.int32)
    offset = place - second
    spread = jnp.concatenate(
        [jnp.where(offset == i, twice, jnp.zeros_like(twice)) for i in range(0, n, 2)], axis=1
    )
    up = jnp.concatenate([up_ref[...] for up_ref in up_refs], axis=0)
    delta = jnp.dot(spread, up, preferred_element_type=jnp.float32).astype(jnp.bfloat16)
    values = (
        base_ref[...].astype(jnp.float32) + adapter_scale * delta.astype(jnp.float32)
    ).astype(jnp.bfloat16)
    copies = []
    wide = GROUP * HEAD_SIZE
    done = 0
    for kv in range(kv_heads):
        columns = slice(kv * HEAD_SIZE, (kv + 1) * HEAD_SIZE)
        for i, (start, first, width) in enumerate(tiles):
            mixed = jnp.dot(
                p_refs[kv * len(tiles) + i][...],
                values[first : first + width, columns],
                preferred_element_type=jnp.float32,
            ).astype(jnp.bfloat16)
            for head in range(GROUP):
                at = kv * wide + head * HEAD_SIZE
                block[start : start + TILE, at : at + HEAD_SIZE] = mixed[head * TILE : (head + 1) * TILE, :]
            if 2 * (i + 1) in (len(tiles), 2 * len(tiles)):
                part = slice(0, rows // 2) if 2 * (i + 1) == len(tiles) else slice(rows // 2, rows)
                span = slice(kv * wide, (kv + 1) * wide)
                copy = pltpu.make_async_copy(block.at[part, span], out_ref.at[part, span], sems.at[done])
                copy.start()
                copies.append(copy)
                done += 1
    for copy in copies:
        copy.wait()


def attend(place, mine, theirs, base, ups, probs):
    rows, value_portion = base.shape
    kv_heads = value_portion // HEAD_SIZE
    wide = kv_heads * GROUP * HEAD_SIZE
    flat = [p for per_head in probs for p in per_head]
    return pl.pallas_call(
        functools.partial(attend_kernel, kv_heads, len(ups)),
        out_shape=jax.ShapeDtypeStruct((rows, wide), jnp.bfloat16),
        in_specs=[VMEM] * (4 + len(ups) + len(flat)),
        out_specs=pl.BlockSpec(memory_space=pl.ANY),
        scratch_shapes=[pltpu.VMEM((rows, wide), jnp.bfloat16), pltpu.SemaphoreType.DMA((2 * kv_heads,))],
        compiler_params=pltpu.CompilerParams(vmem_limit_bytes=12 * 2**20),
        name="attend",
    )(place, mine, theirs, base, *ups, *flat)


def on_device(
    normed_token_rows,
    base_value_rows,
    queries,
    stacked_key_rows,
    adapter_of_row,
    sequence_lengths,
    adapter_down_weight,
    adapter_up_weight,
):
    n = lax.axis_size("rep")
    order = ring_order(n)
    ahead = [(order[i], order[(i + 1) % n]) for i in range(n)]
    back = [(b, a) for a, b in ahead]
    far = n // 2
    distances = [0] + [d for step in range(1, far) for d in (step, -step)] + [far]
    down = jnp.swapaxes(adapter_down_weight[0], 0, 1)
    rank = down.shape[0]
    low, high, up = {0: down[: rank // 2]}, {0: down[rank // 2 :]}, {0: adapter_up_weight[0]}
    place, segment, across = masks(
        n, sequence_lengths, adapter_of_row.reshape(1, -1), queries, stacked_key_rows
    )

    def pass_round(held, pairs, sign, steps):
        piece = held[0]
        for step in range(1, steps + 1):
            piece = lax.ppermute(piece, "rep", pairs)
            held[sign * step if step < far else far] = piece

    pass_round(high, ahead, 1, far - 1)
    pass_round(low, back, -1, far - 1)
    pass_round(high, back, -1, far)
    pass_round(low, ahead, 1, far)
    pass_round(up, ahead, 1, far)
    pass_round(up, back, -1, far - 1)

    kv_heads = stacked_key_rows.shape[1] // HEAD_SIZE
    arrivals = [
        pair
        for step in range(1, far)
        for pair in ([low[step], high[-step]], [high[step], low[-step]])
    ]
    probs = [
        probs_of(segment, across, queries, stacked_key_rows, kv, arrivals[kv // 2]) for kv in range(kv_heads)
    ]

    partial = None
    for lo, hi in [(0, 3)] + [(a, a + 2) for a in range(3, n - 1, 2)] + [(n - 1, n)]:
        pieces = [piece for d in distances[lo:hi] for piece in (low[d], high[d])]
        after = arrivals[kv_heads - 1] if lo == 0 else []
        if lo == n - 5:
            after = [up[far - 2], up[2 - far]]
        if hi == n:
            after = [p[0] for p in probs] + [up[far], up[1 - far]]
        partial = lowrank_of(lo, place, normed_token_rows, partial, pieces, after)
    other = lax.ppermute(partial, "tp", [(0, 1), (1, 0)])
    return attend(
        place,
        partial,
        other,
        base_value_rows,
        [up[d] for d in distances],
        probs,
    )


def solution(mesh):
    placed = (
        P(("groups", "rep"), "tp"),
        P(("groups", "rep"), "tp"),
        P(("groups", "rep"), "tp"),
        P(("groups", "rep"), "tp"),
        P(("groups", "rep"), None),
        P(("groups", "rep"), None),
        P(("groups", "rep"), "tp", None),
        P(("groups", "rep"), None, "tp"),
    )
    return jax.shard_map(
        on_device, mesh=mesh, in_specs=placed, out_specs=P(("groups", "rep"), "tp"), check_vma=False
    )
```

```python
import functools

import jax
import jax.numpy as jnp
import numpy as np
from jax import lax
from jax.experimental import pallas as pl
from jax.experimental.pallas import tpu as pltpu
from jax.sharding import PartitionSpec as P

HEADS = 64
KEY_VALUE_HEADS = 8
HEAD_SIZE = 128
GROUP = HEADS // KEY_VALUE_HEADS
LONGEST = 192
TILE = 64
REACH = -(-(LONGEST - 1) // TILE)
adapter_scale = 2.0

VMEM = pl.BlockSpec(memory_space=pltpu.VMEM)
SMEM = pl.BlockSpec(memory_space=pltpu.SMEM)
NT = (((1,), (1,)), ((), ()))


def ring_order(n):
    if n == 8:
        return list(range(0, n, 2)) + list(range(n - 1, 0, -2))
    return list(range(n))


def windows(rows):
    found = []
    for tile in range(rows // TILE):
        first = max(0, tile - REACH) * TILE
        width = (tile + 1) * TILE - first
        width = -(-width // 128) * 128
        found.append((tile * TILE, first, width))
    return found


def ring_place(replica, n):
    if n == 8:
        return jnp.where(replica & 1 == 0, replica >> 1, n - 1 - (replica >> 1))
    return replica


def column(row):
    wide = jnp.broadcast_to(row.astype(jnp.float32), (8, row.shape[1]))
    return wide.T[:, :1].astype(jnp.int32)


def masks_kernel(n, me_ref, lengths_ref, adapter_ref, near_q_ref, near_k_ref, *refs):
    place_ref, segment_ref, across_ref = refs[-3:]
    distance = ring_place(me_ref[0], n) - ring_place(adapter_ref[...], n)
    distance = jnp.where(distance < 0, distance + n, distance)
    place = jnp.where(distance <= n // 2, jnp.maximum(2 * distance - 1, 0), 2 * (n - distance))
    place_ref[...] = column(place)
    position = lax.broadcasted_iota(jnp.int32, place.shape, 1)
    segment = jnp.zeros(place.shape, jnp.int32)
    end = jnp.int32(0)
    for i in range(lengths_ref.shape[1]):
        end = end + lengths_ref[0, i]
        segment = segment + (position >= end).astype(jnp.int32)
    across_ref[...] = segment
    segment_ref[...] = column(segment)


def masks(n, lengths, adapter_row, queries, keys, after):
    rows = keys.shape[0]
    tall = jax.ShapeDtypeStruct((rows, 1), jnp.int32)
    me = jnp.reshape(lax.axis_index("rep"), (1,)).astype(jnp.int32)
    return pl.pallas_call(
        functools.partial(masks_kernel, n),
        out_shape=[tall, tall, jax.ShapeDtypeStruct((1, rows), jnp.int32)],
        in_specs=[SMEM, SMEM, VMEM, VMEM, VMEM] + [pl.BlockSpec(memory_space=pl.ANY)] * len(after),
        out_specs=[VMEM] * 3,
        cost_estimate=pl.CostEstimate(flops=1_000_000_000, bytes_accessed=16 * rows, transcendentals=0),
        compiler_params=pltpu.CompilerParams(vmem_limit_bytes=4 * 2**20),
        name="masks",
    )(me, lengths, adapter_row, queries, keys, *after)


def probs_kernel(kv_head, segment_ref, across_ref, q_ref, k_ref, *refs):
    rows = k_ref.shape[0]
    tiles = windows(rows)
    p_refs = refs[-len(tiles) :]
    factor = float(np.log2(np.e) * HEAD_SIZE**-0.5)
    at = kv_head * HEAD_SIZE
    for p_ref, (start, first, width) in zip(p_refs, tiles):
        t = lax.broadcasted_iota(jnp.int32, (TILE, width), 0) + start
        s = lax.broadcasted_iota(jnp.int32, (TILE, width), 1) + first
        same = segment_ref[start : start + TILE, :] == across_ref[:, first : first + width]
        bias = jnp.where(same & (s <= t), 0.0, -1e30)
        keys = k_ref[first : first + width, at : at + HEAD_SIZE]
        for head in range(GROUP):
            column_at = (kv_head * GROUP + head) * HEAD_SIZE
            q = q_ref[start : start + TILE, column_at : column_at + HEAD_SIZE]
            scores = lax.dot_general(q, keys, NT, preferred_element_type=jnp.float32) + bias
            peak = jnp.max(scores, axis=1, keepdims=True)
            weights = jnp.exp2((scores - peak) * factor)
            inverse = 1.0 / jnp.sum(weights, axis=1, keepdims=True)
            p_ref[head * TILE : (head + 1) * TILE, :] = (weights * inverse).astype(jnp.bfloat16)


def probs_of(segment, across, queries, keys, kv_head, after):
    rows = keys.shape[0]
    shapes = [(GROUP * TILE, width) for _, _, width in windows(rows)]
    elements = sum(a * b for a, b in shapes)
    return pl.pallas_call(
        functools.partial(probs_kernel, kv_head),
        out_shape=[jax.ShapeDtypeStruct(s, jnp.bfloat16) for s in shapes],
        in_specs=[VMEM] * 4 + [pl.BlockSpec(memory_space=pl.ANY)] * len(after),
        out_specs=[VMEM] * len(shapes),
        cost_estimate=pl.CostEstimate(
            flops=2_000_000_000, bytes_accessed=2 * elements, transcendentals=elements
        ),
        compiler_params=pltpu.CompilerParams(vmem_limit_bytes=12 * 2**20),
        name="probs",
    )(segment, across, queries, keys, *after)


def lowrank_kernel(at, count, place_ref, x_ref, *refs):
    w_refs, out_ref = refs[:count], refs[-1]
    before_ref = refs[count] if at > 0 else None
    place = place_ref[...]
    rows, features = x_ref.shape
    half = w_refs[0].shape[0]
    stacked = jnp.concatenate([w_ref[...] for w_ref in w_refs], axis=0)
    product = lax.dot_general(x_ref[...], stacked, NT, preferred_element_type=jnp.float32)
    sums = [jnp.zeros((rows, half), jnp.float32)] * 2
    for i in range(count):
        part = product[:, i * half : (i + 1) * half]
        sums[i % 2] = sums[i % 2] + jnp.where(place == at + i // 2, part, 0.0)
    total = jnp.concatenate(sums, axis=1)
    out_ref[...] = total if before_ref is None else total + before_ref[...]


def lowrank_of(at, place, x, before, pieces, after):
    rows, features = x.shape
    rank = 2 * pieces[0].shape[0]
    operands = [place, x] + pieces + ([] if before is None else [before])
    used = len(operands)
    operands = operands + after
    size = 2 * sum(p.size for p in pieces)
    return pl.pallas_call(
        functools.partial(lowrank_kernel, at, len(pieces)),
        out_shape=jax.ShapeDtypeStruct((rows, rank), jnp.float32),
        in_specs=[VMEM] * used + [pl.BlockSpec(memory_space=pl.ANY)] * len(after),
        out_specs=VMEM,
        cost_estimate=pl.CostEstimate(
            flops=1_700_000_000, bytes_accessed=2 * rows * features + size, transcendentals=0
        ),
        compiler_params=pltpu.CompilerParams(vmem_limit_bytes=8 * 2**20 + 2 * x.size + 2 * size),
        name="lowrank",
    )(*operands)


def attend_kernel(kv_heads, n, place_ref, mine_ref, theirs_ref, base_ref, *refs):
    rows = base_ref.shape[0]
    tiles = windows(rows)
    up_refs = refs[:n]
    p_refs = refs[n : n + kv_heads * len(tiles)]
    out_ref, block, sems = refs[n + kv_heads * len(tiles) :]
    rank = mine_ref.shape[1]
    place = place_ref[...]
    lowrank = (mine_ref[...] + theirs_ref[...]).astype(jnp.bfloat16)
    twice = jnp.concatenate([lowrank, lowrank], axis=1)
    second = (lax.broadcasted_iota(jnp.int32, twice.shape, 1) >= rank).astype(jnp.int32)
    offset = place - second
    spread = jnp.concatenate(
        [jnp.where(offset == i, twice, jnp.zeros_like(twice)) for i in range(0, n, 2)], axis=1
    )
    up = jnp.concatenate([up_ref[...] for up_ref in up_refs], axis=0)
    delta = jnp.dot(spread, up, preferred_element_type=jnp.float32).astype(jnp.bfloat16)
    values = (
        base_ref[...].astype(jnp.float32) + adapter_scale * delta.astype(jnp.float32)
    ).astype(jnp.bfloat16)
    copies = []
    wide = GROUP * HEAD_SIZE
    done = 0
    for kv in range(kv_heads):
        columns = slice(kv * HEAD_SIZE, (kv + 1) * HEAD_SIZE)
        for i, (start, first, width) in enumerate(tiles):
            mixed = jnp.dot(
                p_refs[kv * len(tiles) + i][...],
                values[first : first + width, columns],
                preferred_element_type=jnp.float32,
            ).astype(jnp.bfloat16)
            for head in range(GROUP):
                at = kv * wide + head * HEAD_SIZE
                block[start : start + TILE, at : at + HEAD_SIZE] = mixed[head * TILE : (head + 1) * TILE, :]
            if 2 * (i + 1) in (len(tiles), 2 * len(tiles)):
                part = slice(0, rows // 2) if 2 * (i + 1) == len(tiles) else slice(rows // 2, rows)
                span = slice(kv * wide, (kv + 1) * wide)
                copy = pltpu.make_async_copy(block.at[part, span], out_ref.at[part, span], sems.at[done])
                copy.start()
                copies.append(copy)
                done += 1
    for copy in copies:
        copy.wait()


def attend(place, mine, theirs, base, ups, probs):
    rows, value_portion = base.shape
    kv_heads = value_portion // HEAD_SIZE
    wide = kv_heads * GROUP * HEAD_SIZE
    flat = [p for per_head in probs for p in per_head]
    return pl.pallas_call(
        functools.partial(attend_kernel, kv_heads, len(ups)),
        out_shape=jax.ShapeDtypeStruct((rows, wide), jnp.bfloat16),
        in_specs=[VMEM] * (4 + len(ups) + len(flat)),
        out_specs=pl.BlockSpec(memory_space=pl.ANY),
        scratch_shapes=[pltpu.VMEM((rows, wide), jnp.bfloat16), pltpu.SemaphoreType.DMA((2 * kv_heads,))],
        compiler_params=pltpu.CompilerParams(vmem_limit_bytes=12 * 2**20),
        name="attend",
    )(place, mine, theirs, base, *ups, *flat)


def on_device(
    normed_token_rows,
    base_value_rows,
    queries,
    stacked_key_rows,
    adapter_of_row,
    sequence_lengths,
    adapter_down_weight,
    adapter_up_weight,
):
    n = lax.axis_size("rep")
    order = ring_order(n)
    ahead = [(order[i], order[(i + 1) % n]) for i in range(n)]
    back = [(b, a) for a, b in ahead]
    far = n // 2
    distances = [0] + [d for step in range(1, far) for d in (step, -step)] + [far]
    down = jnp.swapaxes(adapter_down_weight[0], 0, 1)
    rank = down.shape[0]
    low, high, up = {0: down[: rank // 2]}, {0: down[rank // 2 :]}, {0: adapter_up_weight[0]}
    def pass_round(held, pairs, sign, steps):
        piece = held[0]
        for step in range(1, steps + 1):
            piece = lax.ppermute(piece, "rep", pairs)
            held[sign * step if step < far else far] = piece

    pass_round(high, ahead, 1, far - 1)
    pass_round(low, back, -1, far - 1)
    pass_round(high, back, -1, far)
    pass_round(low, ahead, 1, far)
    pass_round(up, ahead, 1, far)
    pass_round(up, back, -1, far - 1)

    place, segment, across = masks(
        n, sequence_lengths, adapter_of_row.reshape(1, -1), queries, stacked_key_rows, [up[1], up[-1]]
    )
    kv_heads = stacked_key_rows.shape[1] // HEAD_SIZE
    arrivals = [
        pair
        for step in range(1, far)
        for pair in ([low[step], high[-step]], [high[step], low[-step]])
    ]
    up_after = [[up[2], up[-2]], [], [up[far - 1], up[1 - far]], []]
    probs = [
        probs_of(segment, across, queries, stacked_key_rows, kv, arrivals[kv // 2] + up_after[kv])
        for kv in range(kv_heads)
    ]

    partial = None
    for lo, hi in [(0, 3)] + [(a, a + 2) for a in range(3, n - 1, 2)] + [(n - 1, n)]:
        pieces = [piece for d in distances[lo:hi] for piece in (low[d], high[d])]
        after = arrivals[min(2, len(arrivals) - 1)] + [up[far]] if lo == 0 else []
        if hi == n:
            after = [p[0] for p in probs]
        partial = lowrank_of(lo, place, normed_token_rows, partial, pieces, after)
    other = lax.ppermute(partial, "tp", [(0, 1), (1, 0)])
    return attend(
        place,
        partial,
        other,
        base_value_rows,
        [up[d] for d in distances],
        probs,
    )


def solution(mesh):
    placed = (
        P(("groups", "rep"), "tp"),
        P(("groups", "rep"), "tp"),
        P(("groups", "rep"), "tp"),
        P(("groups", "rep"), "tp"),
        P(("groups", "rep"), None),
        P(("groups", "rep"), None),
        P(("groups", "rep"), "tp", None),
        P(("groups", "rep"), None, "tp"),
    )
    return jax.shard_map(
        on_device, mesh=mesh, in_specs=placed, out_specs=P(("groups", "rep"), "tp"), check_vma=False
    )
```

```python
import functools

import jax
import jax.numpy as jnp
import numpy as np
from jax import lax
from jax.experimental import pallas as pl
from jax.experimental.pallas import tpu as pltpu
from jax.sharding import PartitionSpec as P

HEADS = 64
KEY_VALUE_HEADS = 8
HEAD_SIZE = 128
GROUP = HEADS // KEY_VALUE_HEADS
LONGEST = 192
TILE = 64
REACH = -(-(LONGEST - 1) // TILE)
adapter_scale = 2.0

VMEM = pl.BlockSpec(memory_space=pltpu.VMEM)
SMEM = pl.BlockSpec(memory_space=pltpu.SMEM)
NT = (((1,), (1,)), ((), ()))


def ring_order(n):
    if n == 8:
        return list(range(0, n, 2)) + list(range(n - 1, 0, -2))
    return list(range(n))


def windows(rows):
    found = []
    for tile in range(rows // TILE):
        first = max(0, tile - REACH) * TILE
        width = (tile + 1) * TILE - first
        width = -(-width // 128) * 128
        found.append((tile * TILE, first, width))
    return found


def ring_place(replica, n):
    if n == 8:
        return jnp.where(replica & 1 == 0, replica >> 1, n - 1 - (replica >> 1))
    return replica


def column(row):
    wide = jnp.broadcast_to(row.astype(jnp.float32), (8, row.shape[1]))
    return wide.T[:, :1].astype(jnp.int32)


def masks_kernel(n, me_ref, lengths_ref, adapter_ref, near_q_ref, near_k_ref, *refs):
    place_ref, segment_ref, across_ref = refs
    distance = ring_place(me_ref[0], n) - ring_place(adapter_ref[...], n)
    distance = jnp.where(distance < 0, distance + n, distance)
    place = jnp.where(distance <= n // 2, jnp.maximum(2 * distance - 1, 0), 2 * (n - distance))
    place_ref[...] = column(place)
    position = lax.broadcasted_iota(jnp.int32, place.shape, 1)
    segment = jnp.zeros(place.shape, jnp.int32)
    end = jnp.int32(0)
    for i in range(lengths_ref.shape[1]):
        end = end + lengths_ref[0, i]
        segment = segment + (position >= end).astype(jnp.int32)
    across_ref[...] = segment
    segment_ref[...] = column(segment)


def masks(n, lengths, adapter_row, queries, keys):
    rows = keys.shape[0]
    tall = jax.ShapeDtypeStruct((rows, 1), jnp.int32)
    me = jnp.reshape(lax.axis_index("rep"), (1,)).astype(jnp.int32)
    return pl.pallas_call(
        functools.partial(masks_kernel, n),
        out_shape=[tall, tall, jax.ShapeDtypeStruct((1, rows), jnp.int32)],
        in_specs=[SMEM, SMEM, VMEM, VMEM, VMEM],
        out_specs=[VMEM] * 3,
        cost_estimate=pl.CostEstimate(flops=1_000_000_000, bytes_accessed=16 * rows, transcendentals=0),
        compiler_params=pltpu.CompilerParams(vmem_limit_bytes=4 * 2**20),
        name="masks",
    )(me, lengths, adapter_row, queries, keys)


def probs_kernel(kv_head, segment_ref, across_ref, q_ref, k_ref, *refs):
    rows = k_ref.shape[0]
    tiles = windows(rows)
    p_refs = refs[-len(tiles) :]
    factor = float(np.log2(np.e) * HEAD_SIZE**-0.5)
    at = kv_head * HEAD_SIZE
    for p_ref, (start, first, width) in zip(p_refs, tiles):
        t = lax.broadcasted_iota(jnp.int32, (TILE, width), 0) + start
        s = lax.broadcasted_iota(jnp.int32, (TILE, width), 1) + first
        same = segment_ref[start : start + TILE, :] == across_ref[:, first : first + width]
        bias = jnp.where(same & (s <= t), 0.0, -1e30)
        keys = k_ref[first : first + width, at : at + HEAD_SIZE]
        for head in range(GROUP):
            column_at = (kv_head * GROUP + head) * HEAD_SIZE
            q = q_ref[start : start + TILE, column_at : column_at + HEAD_SIZE]
            scores = lax.dot_general(q, keys, NT, preferred_element_type=jnp.float32) + bias
            peak = jnp.max(scores, axis=1, keepdims=True)
            weights = jnp.exp2((scores - peak) * factor)
            inverse = 1.0 / jnp.sum(weights, axis=1, keepdims=True)
            p_ref[head * TILE : (head + 1) * TILE, :] = (weights * inverse).astype(jnp.bfloat16)


def probs_of(segment, across, queries, keys, kv_head):
    rows = keys.shape[0]
    shapes = [(GROUP * TILE, width) for _, _, width in windows(rows)]
    elements = sum(a * b for a, b in shapes)
    return pl.pallas_call(
        functools.partial(probs_kernel, kv_head),
        out_shape=[jax.ShapeDtypeStruct(s, jnp.bfloat16) for s in shapes],
        in_specs=[VMEM] * 4,
        out_specs=[VMEM] * len(shapes),
        cost_estimate=pl.CostEstimate(
            flops=2_000_000_000, bytes_accessed=2 * elements, transcendentals=elements
        ),
        compiler_params=pltpu.CompilerParams(vmem_limit_bytes=12 * 2**20),
        name="probs",
    )(segment, across, queries, keys)


def lowrank_kernel(at, count, place_ref, x_ref, *refs):
    w_refs, (out_ref, up_ref) = refs[:count], refs[-2:]
    before_ref = refs[count] if at > 0 else None
    place = place_ref[...]
    rows, features = x_ref.shape
    half = w_refs[0].shape[0]
    stacked = jnp.concatenate([w_ref[:, :features] for w_ref in w_refs], axis=0)
    product = lax.dot_general(x_ref[...], stacked, NT, preferred_element_type=jnp.float32)
    sums = [jnp.zeros((rows, half), jnp.float32)] * 2
    for i in range(count):
        part = product[:, i * half : (i + 1) * half]
        sums[i % 2] = sums[i % 2] + jnp.where(place == at + i // 2, part, 0.0)
    up_ref[...] = jnp.concatenate([w_ref[:, features:] for w_ref in w_refs], axis=0)
    total = jnp.concatenate(sums, axis=1)
    out_ref[...] = total if before_ref is None else total + before_ref[...]


def lowrank_of(at, place, x, before, pieces, after):
    rows, features = x.shape
    half, held = pieces[0].shape
    rank = 2 * half
    operands = [place, x] + pieces + ([] if before is None else [before])
    used = len(operands)
    operands = operands + after
    size = 2 * sum(p.size for p in pieces)
    return pl.pallas_call(
        functools.partial(lowrank_kernel, at, len(pieces)),
        out_shape=[
            jax.ShapeDtypeStruct((rows, rank), jnp.float32),
            jax.ShapeDtypeStruct((half * len(pieces), held - features), pieces[0].dtype),
        ],
        in_specs=[VMEM] * used + [pl.BlockSpec(memory_space=pl.ANY)] * len(after),
        out_specs=[VMEM, VMEM],
        cost_estimate=pl.CostEstimate(
            flops=1_700_000_000, bytes_accessed=2 * rows * features + size, transcendentals=0
        ),
        compiler_params=pltpu.CompilerParams(vmem_limit_bytes=8 * 2**20 + 2 * x.size + 2 * size),
        name="lowrank",
    )(*operands)


def attend_kernel(kv_heads, place_ref, mine_ref, theirs_ref, base_ref, *refs):
    rows = base_ref.shape[0]
    tiles = windows(rows)
    up_refs = refs[: -kv_heads * len(tiles) - 3]
    p_refs = refs[len(up_refs) : -3]
    out_ref, block, sems = refs[-3:]
    rank = mine_ref.shape[1]
    n = sum(up_ref.shape[0] for up_ref in up_refs) // rank
    place = place_ref[...]
    lowrank = (mine_ref[...] + theirs_ref[...]).astype(jnp.bfloat16)
    twice = jnp.concatenate([lowrank, lowrank], axis=1)
    second = (lax.broadcasted_iota(jnp.int32, twice.shape, 1) >= rank).astype(jnp.int32)
    offset = place - second
    spread = jnp.concatenate(
        [jnp.where(offset == i, twice, jnp.zeros_like(twice)) for i in range(0, n, 2)], axis=1
    )
    up = jnp.concatenate([up_ref[...] for up_ref in up_refs], axis=0)
    delta = jnp.dot(spread, up, preferred_element_type=jnp.float32).astype(jnp.bfloat16)
    values = (
        base_ref[...].astype(jnp.float32) + adapter_scale * delta.astype(jnp.float32)
    ).astype(jnp.bfloat16)
    copies = []
    wide = GROUP * HEAD_SIZE
    done = 0
    for kv in range(kv_heads):
        columns = slice(kv * HEAD_SIZE, (kv + 1) * HEAD_SIZE)
        for i, (start, first, width) in enumerate(tiles):
            mixed = jnp.dot(
                p_refs[kv * len(tiles) + i][...],
                values[first : first + width, columns],
                preferred_element_type=jnp.float32,
            ).astype(jnp.bfloat16)
            for head in range(GROUP):
                at = kv * wide + head * HEAD_SIZE
                block[start : start + TILE, at : at + HEAD_SIZE] = mixed[head * TILE : (head + 1) * TILE, :]
            if 2 * (i + 1) in (len(tiles), 2 * len(tiles)):
                part = slice(0, rows // 2) if 2 * (i + 1) == len(tiles) else slice(rows // 2, rows)
                span = slice(kv * wide, (kv + 1) * wide)
                copy = pltpu.make_async_copy(block.at[part, span], out_ref.at[part, span], sems.at[done])
                copy.start()
                copies.append(copy)
                done += 1
    for copy in copies:
        copy.wait()


def attend(place, mine, theirs, base, ups, probs):
    rows, value_portion = base.shape
    kv_heads = value_portion // HEAD_SIZE
    wide = kv_heads * GROUP * HEAD_SIZE
    flat = [p for per_head in probs for p in per_head]
    return pl.pallas_call(
        functools.partial(attend_kernel, kv_heads),
        out_shape=jax.ShapeDtypeStruct((rows, wide), jnp.bfloat16),
        in_specs=[VMEM] * (4 + len(ups) + len(flat)),
        out_specs=pl.BlockSpec(memory_space=pl.ANY),
        scratch_shapes=[pltpu.VMEM((rows, wide), jnp.bfloat16), pltpu.SemaphoreType.DMA((2 * kv_heads,))],
        compiler_params=pltpu.CompilerParams(vmem_limit_bytes=12 * 2**20),
        name="attend",
    )(place, mine, theirs, base, *ups, *flat)


def on_device(
    normed_token_rows,
    base_value_rows,
    queries,
    stacked_key_rows,
    adapter_of_row,
    sequence_lengths,
    adapter_down_weight,
    adapter_up_weight,
):
    n = lax.axis_size("rep")
    order = ring_order(n)
    ahead = [(order[i], order[(i + 1) % n]) for i in range(n)]
    back = [(b, a) for a, b in ahead]
    far = n // 2
    distances = [0] + [d for step in range(1, far) for d in (step, -step)] + [far]
    down = jnp.swapaxes(adapter_down_weight[0], 0, 1)
    both = jnp.concatenate([down, adapter_up_weight[0]], axis=1)
    rank = both.shape[0]
    own_low, own_high = both[: rank // 2], both[rank // 2 :]
    place, segment, across = masks(
        n, sequence_lengths, adapter_of_row.reshape(1, -1), queries, stacked_key_rows
    )
    low, high = {0: own_low}, {0: own_high}

    def pass_round(held, pairs, sign, steps):
        piece = held[0]
        for step in range(1, steps + 1):
            piece = lax.ppermute(piece, "rep", pairs)
            held[sign * step if step < far else far] = piece

    pass_round(high, ahead, 1, far - 1)
    pass_round(low, back, -1, far - 1)
    pass_round(high, back, -1, far)
    pass_round(low, ahead, 1, far)

    kv_heads = stacked_key_rows.shape[1] // HEAD_SIZE
    arrivals = [
        pair
        for step in range(1, far)
        for pair in ([low[step], high[-step]], [high[step], low[-step]])
    ]
    probs = [
        probs_of(segment, across, queries, stacked_key_rows, kv) for kv in range(kv_heads)
    ]

    partial, ups = None, []
    for lo, hi in [(0, 3)] + [(a, a + 2) for a in range(3, n - 1, 2)] + [(n - 1, n)]:
        pieces = [piece for d in distances[lo:hi] for piece in (low[d], high[d])]
        after = arrivals[kv_heads - 1] if lo == 0 else []
        if hi == n:
            after = [p[0] for p in probs]
        partial, up = lowrank_of(lo, place, normed_token_rows, partial, pieces, after)
        ups.append(up)
    other = lax.ppermute(partial, "tp", [(0, 1), (1, 0)])
    return attend(
        place,
        partial,
        other,
        base_value_rows,
        ups,
        probs,
    )


def solution(mesh):
    placed = (
        P(("groups", "rep"), "tp"),
        P(("groups", "rep"), "tp"),
        P(("groups", "rep"), "tp"),
        P(("groups", "rep"), "tp"),
        P(("groups", "rep"), None),
        P(("groups", "rep"), None),
        P(("groups", "rep"), "tp", None),
        P(("groups", "rep"), None, "tp"),
    )
    return jax.shard_map(
        on_device, mesh=mesh, in_specs=placed, out_specs=P(("groups", "rep"), "tp"), check_vma=False
    )
```

```python
import functools

import jax
import jax.numpy as jnp
import numpy as np
from jax import lax
from jax.experimental import pallas as pl
from jax.experimental.pallas import tpu as pltpu
from jax.sharding import PartitionSpec as P

HEADS = 64
KEY_VALUE_HEADS = 8
HEAD_SIZE = 128
GROUP = HEADS // KEY_VALUE_HEADS
LONGEST = 192
TILE = 64
REACH = -(-(LONGEST - 1) // TILE)
adapter_scale = 2.0

VMEM = pl.BlockSpec(memory_space=pltpu.VMEM)
SMEM = pl.BlockSpec(memory_space=pltpu.SMEM)
NT = (((1,), (1,)), ((), ()))


def ring_order(n):
    if n == 8:
        return list(range(0, n, 2)) + list(range(n - 1, 0, -2))
    return list(range(n))


def windows(rows):
    found = []
    for tile in range(rows // TILE):
        first = max(0, tile - REACH) * TILE
        width = (tile + 1) * TILE - first
        width = -(-width // 128) * 128
        found.append((tile * TILE, first, width))
    return found


def ring_place(replica, n):
    if n == 8:
        return jnp.where(replica & 1 == 0, replica >> 1, n - 1 - (replica >> 1))
    return replica


def column(row):
    wide = jnp.broadcast_to(row.astype(jnp.float32), (8, row.shape[1]))
    return wide.T[:, :1].astype(jnp.int32)


def masks_kernel(n, me_ref, lengths_ref, adapter_ref, near_q_ref, near_k_ref, *refs):
    place_ref, segment_ref, across_ref, slot_ref, slot_across_ref = refs
    distance = ring_place(me_ref[0], n) - ring_place(adapter_ref[...], n)
    distance = jnp.where(distance < 0, distance + n, distance)
    place = jnp.where(distance <= n // 2, jnp.maximum(2 * distance - 1, 0), 2 * (n - distance))
    place_ref[...] = column(place)
    position = lax.broadcasted_iota(jnp.int32, place.shape, 1)
    segment = jnp.zeros(place.shape, jnp.int32)
    end = jnp.int32(0)
    for i in range(lengths_ref.shape[1]):
        end = end + lengths_ref[0, i]
        segment = segment + (position >= end).astype(jnp.int32)
    across_ref[...] = segment
    segment_ref[...] = column(segment)
    rows = place.shape[1]
    last = place == n - 1
    earlier = lax.broadcasted_iota(jnp.int32, (rows, rows), 0) < lax.broadcasted_iota(jnp.int32, (rows, rows), 1)
    ones = jnp.where(jnp.broadcast_to(last, (8, rows)), 1.0, 0.0).astype(jnp.bfloat16)
    count = jnp.dot(ones, jnp.where(earlier, 1.0, 0.0).astype(jnp.bfloat16), preferred_element_type=jnp.float32)
    slot = jnp.where(last, count[:1, :].astype(jnp.int32), -1)
    slot_across_ref[...] = slot
    slot_ref[...] = column(slot)


def masks(n, lengths, adapter_row, queries, keys):
    rows = keys.shape[0]
    tall, flat = [jax.ShapeDtypeStruct(shape, jnp.int32) for shape in ((rows, 1), (1, rows))]
    me = jnp.reshape(lax.axis_index("rep"), (1,)).astype(jnp.int32)
    return pl.pallas_call(
        functools.partial(masks_kernel, n),
        out_shape=[tall, tall, flat, tall, flat],
        in_specs=[SMEM, SMEM, VMEM, VMEM, VMEM],
        out_specs=[VMEM] * 5,
        cost_estimate=pl.CostEstimate(flops=1_000_000_000, bytes_accessed=16 * rows, transcendentals=0),
        compiler_params=pltpu.CompilerParams(vmem_limit_bytes=4 * 2**20),
        name="masks",
    )(me, lengths, adapter_row, queries, keys)


def probs_kernel(kv_head, segment_ref, across_ref, q_ref, k_ref, *refs):
    rows = k_ref.shape[0]
    tiles = windows(rows)
    p_refs = refs[-len(tiles) :]
    factor = float(np.log2(np.e) * HEAD_SIZE**-0.5)
    at = kv_head * HEAD_SIZE
    for p_ref, (start, first, width) in zip(p_refs, tiles):
        t = lax.broadcasted_iota(jnp.int32, (TILE, width), 0) + start
        s = lax.broadcasted_iota(jnp.int32, (TILE, width), 1) + first
        same = segment_ref[start : start + TILE, :] == across_ref[:, first : first + width]
        bias = jnp.where(same & (s <= t), 0.0, -1e30)
        keys = k_ref[first : first + width, at : at + HEAD_SIZE]
        for head in range(GROUP):
            column_at = (kv_head * GROUP + head) * HEAD_SIZE
            q = q_ref[start : start + TILE, column_at : column_at + HEAD_SIZE]
            scores = lax.dot_general(q, keys, NT, preferred_element_type=jnp.float32) + bias
            peak = jnp.max(scores, axis=1, keepdims=True)
            weights = jnp.exp2((scores - peak) * factor)
            inverse = 1.0 / jnp.sum(weights, axis=1, keepdims=True)
            p_ref[head * TILE : (head + 1) * TILE, :] = (weights * inverse).astype(jnp.bfloat16)


def probs_of(segment, across, queries, keys, kv_head, after):
    rows = keys.shape[0]
    shapes = [(GROUP * TILE, width) for _, _, width in windows(rows)]
    elements = sum(a * b for a, b in shapes)
    return pl.pallas_call(
        functools.partial(probs_kernel, kv_head),
        out_shape=[jax.ShapeDtypeStruct(s, jnp.bfloat16) for s in shapes],
        in_specs=[VMEM] * 4 + [pl.BlockSpec(memory_space=pl.ANY)] * len(after),
        out_specs=[VMEM] * len(shapes),
        cost_estimate=pl.CostEstimate(
            flops=2_000_000_000, bytes_accessed=2 * elements, transcendentals=elements
        ),
        compiler_params=pltpu.CompilerParams(vmem_limit_bytes=12 * 2**20),
        name="probs",
    )(segment, across, queries, keys, *after)


def lowrank_kernel(at, count, place_ref, x_ref, *refs):
    w_refs, (out_ref, up_ref) = refs[:count], refs[-2:]
    before_ref = refs[count] if at > 0 else None
    place = place_ref[...]
    rows, features = x_ref.shape
    half = w_refs[0].shape[0]
    stacked = jnp.concatenate([w_ref[:, :features] for w_ref in w_refs], axis=0)
    product = lax.dot_general(x_ref[...], stacked, NT, preferred_element_type=jnp.float32)
    sums = [jnp.zeros((rows, half), jnp.float32)] * 2
    for i in range(count):
        part = product[:, i * half : (i + 1) * half]
        sums[i % 2] = sums[i % 2] + jnp.where(place == at + i // 2, part, 0.0)
    up_ref[...] = jnp.concatenate([w_ref[:, features:] for w_ref in w_refs], axis=0)
    total = jnp.concatenate(sums, axis=1)
    out_ref[...] = total if before_ref is None else total + before_ref[...]


def lowrank_of(at, place, x, before, pieces, after):
    rows, features = x.shape
    half, held = pieces[0].shape
    rank = 2 * half
    operands = [place, x] + pieces + ([] if before is None else [before])
    used = len(operands)
    operands = operands + after
    size = 2 * sum(p.size for p in pieces)
    return pl.pallas_call(
        functools.partial(lowrank_kernel, at, len(pieces)),
        out_shape=[
            jax.ShapeDtypeStruct((rows, rank), jnp.float32),
            jax.ShapeDtypeStruct((half * len(pieces), held - features), pieces[0].dtype),
        ],
        in_specs=[VMEM] * used + [pl.BlockSpec(memory_space=pl.ANY)] * len(after),
        out_specs=[VMEM, VMEM],
        cost_estimate=pl.CostEstimate(
            flops=1_700_000_000, bytes_accessed=2 * rows * features + size, transcendentals=0
        ),
        compiler_params=pltpu.CompilerParams(vmem_limit_bytes=8 * 2**20 + 2 * x.size + 2 * size),
        name="lowrank",
    )(*operands)


def last_rows_kernel(slot_across_ref, x_ref, out_ref):
    room, rows = out_ref.shape[0], x_ref.shape[0]
    pick = lax.broadcasted_iota(jnp.int32, (room, rows), 0) == slot_across_ref[...]
    pick = jnp.where(pick, 1.0, 0.0).astype(jnp.bfloat16)
    step = 1024
    for at in range(0, x_ref.shape[1], step):
        picked = jnp.dot(pick, x_ref[:, at : at + step], preferred_element_type=jnp.float32)
        out_ref[:, at : at + step] = picked.astype(jnp.bfloat16)


def last_rows(slot_across, x, room):
    return pl.pallas_call(
        last_rows_kernel,
        out_shape=jax.ShapeDtypeStruct((room, x.shape[1]), x.dtype),
        in_specs=[VMEM, VMEM],
        out_specs=VMEM,
        cost_estimate=pl.CostEstimate(flops=1_500_000_000, bytes_accessed=2 * x.size, transcendentals=0),
        compiler_params=pltpu.CompilerParams(vmem_limit_bytes=8 * 2**20),
        name="last_rows",
    )(slot_across, x)


def last_probs_kernel(slot_ref, *refs):
    tiles = windows(slot_ref.shape[0])
    p_refs, out_refs = refs[: 2 * len(tiles)], refs[2 * len(tiles) :]
    for i, (_, first, width) in enumerate(tiles):
        pick = lax.broadcasted_iota(jnp.int32, (width, 128), 1) == slot_ref[first : first + width, :]
        pick = jnp.where(pick, 1.0, 0.0).astype(jnp.bfloat16)
        for side in range(2):
            picked = jnp.dot(p_refs[side * len(tiles) + i][...], pick, preferred_element_type=jnp.float32)
            out_refs[i][:, side * 128 : (side + 1) * 128] = picked.astype(jnp.bfloat16)


def last_probs(slot, left, right):
    pieces = left + right
    return pl.pallas_call(
        last_probs_kernel,
        out_shape=[jax.ShapeDtypeStruct((p.shape[0], 256), p.dtype) for p in left],
        in_specs=[VMEM] * (1 + len(pieces)),
        out_specs=[VMEM] * len(left),
        cost_estimate=pl.CostEstimate(
            flops=1_500_000_000, bytes_accessed=2 * sum(p.size for p in pieces), transcendentals=0
        ),
        compiler_params=pltpu.CompilerParams(vmem_limit_bytes=6 * 2**20),
        name="last_probs",
    )(slot, *pieces)


def early_kernel(kv_heads, place_ref, mine_ref, theirs_ref, base_ref, *refs):
    rows = base_ref.shape[0]
    tiles = windows(rows)
    up_refs = refs[: -kv_heads * len(tiles) - 1]
    p_refs, out_ref = refs[len(up_refs) : -1], refs[-1]
    rank = mine_ref.shape[1]
    held = sum(up_ref.shape[0] for up_ref in up_refs)
    pairs = -(-held // (2 * rank))
    place = place_ref[...]
    lowrank = (mine_ref[...] + theirs_ref[...]).astype(jnp.bfloat16)
    twice = jnp.concatenate([lowrank, lowrank], axis=1)
    second = (lax.broadcasted_iota(jnp.int32, twice.shape, 1) >= rank).astype(jnp.int32)
    offset = place - second
    spread = jnp.concatenate(
        [jnp.where(offset == 2 * i, twice, jnp.zeros_like(twice)) for i in range(pairs)], axis=1
    )
    ups = [up_ref[...] for up_ref in up_refs]
    if held < 2 * rank * pairs:
        ups.append(jnp.zeros((2 * rank * pairs - held, base_ref.shape[1]), jnp.bfloat16))
    delta = jnp.dot(
        spread, jnp.concatenate(ups, axis=0), preferred_element_type=jnp.float32
    ).astype(jnp.bfloat16)
    values = (
        base_ref[...].astype(jnp.float32) + adapter_scale * delta.astype(jnp.float32)
    ).astype(jnp.bfloat16)
    wide = GROUP * HEAD_SIZE
    for kv in range(kv_heads):
        columns = slice(kv * HEAD_SIZE, (kv + 1) * HEAD_SIZE)
        for i, (start, first, width) in enumerate(tiles):
            mixed = jnp.dot(
                p_refs[kv * len(tiles) + i][...],
                values[first : first + width, columns],
                preferred_element_type=jnp.float32,
            )
            for head in range(GROUP):
                at = kv * wide + head * HEAD_SIZE
                out_ref[start : start + TILE, at : at + HEAD_SIZE] = mixed[head * TILE : (head + 1) * TILE, :]


def early_product(place, mine, theirs, base, ups, probs):
    rows, value_portion = base.shape
    kv_heads = value_portion // HEAD_SIZE
    flat = [p for per_head in probs for p in per_head]
    return pl.pallas_call(
        functools.partial(early_kernel, kv_heads),
        out_shape=jax.ShapeDtypeStruct((rows, kv_heads * GROUP * HEAD_SIZE), jnp.float32),
        in_specs=[VMEM] * (4 + len(ups) + len(flat)),
        out_specs=VMEM,
        cost_estimate=pl.CostEstimate(flops=50_000_000, bytes_accessed=4 * rows, transcendentals=0),
        compiler_params=pltpu.CompilerParams(vmem_limit_bytes=8 * 2**20),
        name="early_product",
    )(place, mine, theirs, base, *ups, *flat)


def last_lowrank_kernel(x_ref, low_ref, high_ref, *refs):
    out_ref, up_ref = refs[-2:]
    features = x_ref.shape[1]
    stacked = jnp.concatenate([low_ref[:, :features], high_ref[:, :features]], axis=0)
    out_ref[...] = lax.dot_general(x_ref[...], stacked, NT, preferred_element_type=jnp.float32)
    up_ref[...] = jnp.concatenate([low_ref[:, features:], high_ref[:, features:]], axis=0)


def last_lowrank(x, low, high, after):
    rank, columns = 2 * low.shape[0], low.shape[1] - x.shape[1]
    return pl.pallas_call(
        last_lowrank_kernel,
        out_shape=[
            jax.ShapeDtypeStruct((x.shape[0], rank), jnp.float32),
            jax.ShapeDtypeStruct((rank, columns), low.dtype),
        ],
        in_specs=[VMEM] * 3 + [pl.BlockSpec(memory_space=pl.ANY)] * len(after),
        out_specs=[VMEM, VMEM],
        cost_estimate=pl.CostEstimate(flops=600_000_000, bytes_accessed=2 * x.size, transcendentals=0),
        compiler_params=pltpu.CompilerParams(vmem_limit_bytes=6 * 2**20),
        name="last_lowrank",
    )(x, low, high, *after)


def finish_kernel(mine_ref, theirs_ref, up_ref, early_ref, *refs):
    p_refs, (out_ref, block, sems) = refs[:-3], refs[-3:]
    rows = early_ref.shape[0]
    tiles = windows(rows)
    wide = GROUP * HEAD_SIZE
    lowrank = (mine_ref[...] + theirs_ref[...]).astype(jnp.bfloat16)
    delta = jnp.dot(lowrank, up_ref[...], preferred_element_type=jnp.float32).astype(jnp.bfloat16)
    change = (adapter_scale * delta.astype(jnp.float32)).astype(jnp.bfloat16)
    room = change.shape[0]
    if room < 128:
        change = jnp.concatenate([change, jnp.zeros((128 - room, change.shape[1]), jnp.bfloat16)], axis=0)
    none = jnp.zeros((128, HEAD_SIZE), jnp.bfloat16)
    copies = []
    for pair in range(len(p_refs) // len(tiles)):
        at = 2 * pair * HEAD_SIZE
        left, right = change[:, at : at + HEAD_SIZE], change[:, at + HEAD_SIZE : at + 2 * HEAD_SIZE]
        both = jnp.concatenate(
            [jnp.concatenate([left, none], axis=1), jnp.concatenate([none, right], axis=1)], axis=0
        )
        for i, (start, _, _) in enumerate(tiles):
            added = jnp.dot(p_refs[pair * len(tiles) + i][...], both, preferred_element_type=jnp.float32)
            for side in range(2):
                for head in range(GROUP):
                    at = (2 * pair + side) * wide + head * HEAD_SIZE
                    part = added[head * TILE : (head + 1) * TILE, side * HEAD_SIZE : (side + 1) * HEAD_SIZE]
                    whole = early_ref[start : start + TILE, at : at + HEAD_SIZE] + part
                    block[start : start + TILE, at : at + HEAD_SIZE] = whole.astype(jnp.bfloat16)
            if i % 2 == 1:
                rows_done = slice(start - TILE, start + TILE)
                span = slice(2 * pair * wide, 2 * (pair + 1) * wide)
                copy = pltpu.make_async_copy(
                    block.at[rows_done, span], out_ref.at[rows_done, span], sems.at[len(copies)]
                )
                copy.start()
                copies.append(copy)
    for copy in copies:
        copy.wait()


def finish(mine, theirs, up, early, picked):
    flat = [p for pair in picked for p in pair]
    return pl.pallas_call(
        finish_kernel,
        out_shape=jax.ShapeDtypeStruct(early.shape, jnp.bfloat16),
        in_specs=[VMEM] * (4 + len(flat)),
        out_specs=pl.BlockSpec(memory_space=pl.ANY),
        scratch_shapes=[pltpu.VMEM(early.shape, jnp.bfloat16), pltpu.SemaphoreType.DMA((len(flat) // 2,))],
        compiler_params=pltpu.CompilerParams(vmem_limit_bytes=10 * 2**20),
        name="finish",
    )(mine, theirs, up, early, *flat)


def on_device(
    normed_token_rows,
    base_value_rows,
    queries,
    stacked_key_rows,
    adapter_of_row,
    sequence_lengths,
    adapter_down_weight,
    adapter_up_weight,
):
    n = lax.axis_size("rep")
    order = ring_order(n)
    ahead = [(order[i], order[(i + 1) % n]) for i in range(n)]
    back = [(b, a) for a, b in ahead]
    far = n // 2
    distances = [0] + [d for step in range(1, far) for d in (step, -step)] + [far]
    down = jnp.swapaxes(adapter_down_weight[0], 0, 1)
    both = jnp.concatenate([down, adapter_up_weight[0]], axis=1)
    rank = both.shape[0]
    own_low, own_high = both[: rank // 2], both[rank // 2 :]
    place, segment, across, slot, slot_across = masks(
        n, sequence_lengths, adapter_of_row.reshape(1, -1), queries, stacked_key_rows
    )
    low, high = {0: own_low}, {0: own_high}

    def pass_round(held, pairs, sign, steps):
        piece = held[0]
        for step in range(1, steps + 1):
            piece = lax.ppermute(piece, "rep", pairs)
            held[sign * step if step < far else far] = piece

    pass_round(high, ahead, 1, far - 1)
    pass_round(low, back, -1, far - 1)
    pass_round(high, back, -1, far)
    pass_round(low, ahead, 1, far)

    kv_heads = stacked_key_rows.shape[1] // HEAD_SIZE
    arrivals = [
        pair
        for step in range(1, far)
        for pair in ([low[step], high[-step]], [high[step], low[-step]])
    ]
    probs = [
        probs_of(segment, across, queries, stacked_key_rows, kv, [low[1], high[-1]] if kv > 0 else [])
        for kv in range(kv_heads)
    ]

    picked = [last_probs(slot, probs[kv], probs[kv + 1]) for kv in range(0, kv_heads, 2)]
    most = 2 * normed_token_rows.shape[0] // n
    x_last = last_rows(slot_across, normed_token_rows, -(-most // 16) * 16)

    partial, ups = None, []
    for lo, hi in [(0, 3)] + [(a, a + 2) for a in range(3, n - 1, 2)]:
        pieces = [piece for d in distances[lo:hi] for piece in (low[d], high[d])]
        after = arrivals[kv_heads - 1] if lo == 0 else []
        partial, up = lowrank_of(lo, place, normed_token_rows, partial, pieces, after + ([x_last] + [p[0] for p in picked] if lo == n - 5 else []))
        ups.append(up)
    swap = [(0, 1), (1, 0)]
    early = early_product(place, partial, lax.ppermute(partial, "tp", swap), base_value_rows, ups, probs)
    last, last_up = last_lowrank(x_last, low[far], high[far], [early])
    return finish(last, lax.ppermute(last, "tp", swap), last_up, early, picked)


def solution(mesh):
    placed = (
        P(("groups", "rep"), "tp"),
        P(("groups", "rep"), "tp"),
        P(("groups", "rep"), "tp"),
        P(("groups", "rep"), "tp"),
        P(("groups", "rep"), None),
        P(("groups", "rep"), None),
        P(("groups", "rep"), "tp", None),
        P(("groups", "rep"), None, "tp"),
    )
    return jax.shard_map(
        on_device, mesh=mesh, in_specs=placed, out_specs=P(("groups", "rep"), "tp"), check_vma=False
    )
```

```python
import functools

import jax
import jax.numpy as jnp
import numpy as np
from jax import lax
from jax.experimental import pallas as pl
from jax.experimental.pallas import tpu as pltpu
from jax.sharding import PartitionSpec as P

HEADS = 64
KEY_VALUE_HEADS = 8
HEAD_SIZE = 128
GROUP = HEADS // KEY_VALUE_HEADS
LONGEST = 192
TILE = 64
REACH = -(-(LONGEST - 1) // TILE)
adapter_scale = 2.0

VMEM = pl.BlockSpec(memory_space=pltpu.VMEM)
SMEM = pl.BlockSpec(memory_space=pltpu.SMEM)
NT = (((1,), (1,)), ((), ()))


def ring_order(n):
    if n == 8:
        return list(range(0, n, 2)) + list(range(n - 1, 0, -2))
    return list(range(n))


def windows(rows):
    found = []
    for tile in range(rows // TILE):
        first = max(0, tile - REACH) * TILE
        width = (tile + 1) * TILE - first
        width = -(-width // 128) * 128
        found.append((tile * TILE, first, width))
    return found


def ring_place(replica, n):
    if n == 8:
        return jnp.where(replica & 1 == 0, replica >> 1, n - 1 - (replica >> 1))
    return replica


def column(row):
    wide = jnp.broadcast_to(row.astype(jnp.float32), (8, row.shape[1]))
    return wide.T[:, :1].astype(jnp.int32)


def masks_kernel(n, me_ref, lengths_ref, adapter_ref, near_q_ref, near_k_ref, *refs):
    place_ref, segment_ref, across_ref, slot_ref, slot_across_ref = refs
    distance = ring_place(me_ref[0], n) - ring_place(adapter_ref[...], n)
    distance = jnp.where(distance < 0, distance + n, distance)
    place = jnp.where(distance <= n // 2, jnp.maximum(2 * distance - 1, 0), 2 * (n - distance))
    place_ref[...] = column(place)
    position = lax.broadcasted_iota(jnp.int32, place.shape, 1)
    segment = jnp.zeros(place.shape, jnp.int32)
    end = jnp.int32(0)
    for i in range(lengths_ref.shape[1]):
        end = end + lengths_ref[0, i]
        segment = segment + (position >= end).astype(jnp.int32)
    across_ref[...] = segment
    segment_ref[...] = column(segment)
    rows = place.shape[1]
    last = place == n - 1
    earlier = lax.broadcasted_iota(jnp.int32, (rows, rows), 0) < lax.broadcasted_iota(jnp.int32, (rows, rows), 1)
    ones = jnp.where(jnp.broadcast_to(last, (8, rows)), 1.0, 0.0).astype(jnp.bfloat16)
    count = jnp.dot(ones, jnp.where(earlier, 1.0, 0.0).astype(jnp.bfloat16), preferred_element_type=jnp.float32)
    slot = jnp.where(last, count[:1, :].astype(jnp.int32), -1)
    slot_across_ref[...] = slot
    slot_ref[...] = column(slot)


def masks(n, lengths, adapter_row, queries, keys):
    rows = keys.shape[0]
    tall, flat = [jax.ShapeDtypeStruct(shape, jnp.int32) for shape in ((rows, 1), (1, rows))]
    me = jnp.reshape(lax.axis_index("rep"), (1,)).astype(jnp.int32)
    return pl.pallas_call(
        functools.partial(masks_kernel, n),
        out_shape=[tall, tall, flat, tall, flat],
        in_specs=[SMEM, SMEM, VMEM, VMEM, VMEM],
        out_specs=[VMEM] * 5,
        cost_estimate=pl.CostEstimate(flops=1_000_000_000, bytes_accessed=16 * rows, transcendentals=0),
        compiler_params=pltpu.CompilerParams(vmem_limit_bytes=4 * 2**20),
        name="masks",
    )(me, lengths, adapter_row, queries, keys)


def probs_kernel(kv_head, segment_ref, across_ref, q_ref, k_ref, *refs):
    rows = k_ref.shape[0]
    tiles = windows(rows)
    p_refs = refs[-len(tiles) :]
    factor = float(np.log2(np.e) * HEAD_SIZE**-0.5)
    at = kv_head * HEAD_SIZE
    for p_ref, (start, first, width) in zip(p_refs, tiles):
        t = lax.broadcasted_iota(jnp.int32, (TILE, width), 0) + start
        s = lax.broadcasted_iota(jnp.int32, (TILE, width), 1) + first
        same = segment_ref[start : start + TILE, :] == across_ref[:, first : first + width]
        bias = jnp.where(same & (s <= t), 0.0, -1e30)
        keys = k_ref[first : first + width, at : at + HEAD_SIZE]
        for head in range(GROUP):
            column_at = (kv_head * GROUP + head) * HEAD_SIZE
            q = q_ref[start : start + TILE, column_at : column_at + HEAD_SIZE]
            scores = lax.dot_general(q, keys, NT, preferred_element_type=jnp.float32) + bias
            peak = jnp.max(scores, axis=1, keepdims=True)
            weights = jnp.exp2((scores - peak) * factor)
            inverse = 1.0 / jnp.sum(weights, axis=1, keepdims=True)
            p_ref[head * TILE : (head + 1) * TILE, :] = (weights * inverse).astype(jnp.bfloat16)


def probs_of(segment, across, queries, keys, kv_head):
    rows = keys.shape[0]
    shapes = [(GROUP * TILE, width) for _, _, width in windows(rows)]
    elements = sum(a * b for a, b in shapes)
    return pl.pallas_call(
        functools.partial(probs_kernel, kv_head),
        out_shape=[jax.ShapeDtypeStruct(s, jnp.bfloat16) for s in shapes],
        in_specs=[VMEM] * 4,
        out_specs=[VMEM] * len(shapes),
        cost_estimate=pl.CostEstimate(
            flops=2_000_000_000, bytes_accessed=2 * elements, transcendentals=elements
        ),
        compiler_params=pltpu.CompilerParams(vmem_limit_bytes=12 * 2**20),
        name="probs",
    )(segment, across, queries, keys)


def lowrank_kernel(at, count, place_ref, x_ref, *refs):
    w_refs, (out_ref, up_ref) = refs[:count], refs[-2:]
    before_ref = refs[count] if at > 0 else None
    place = place_ref[...]
    rows, features = x_ref.shape
    half = w_refs[0].shape[0]
    stacked = jnp.concatenate([w_ref[:, :features] for w_ref in w_refs], axis=0)
    product = lax.dot_general(x_ref[...], stacked, NT, preferred_element_type=jnp.float32)
    sums = [jnp.zeros((rows, half), jnp.float32)] * 2
    for i in range(count):
        part = product[:, i * half : (i + 1) * half]
        sums[i % 2] = sums[i % 2] + jnp.where(place == at + i // 2, part, 0.0)
    up_ref[...] = jnp.concatenate([w_ref[:, features:] for w_ref in w_refs], axis=0)
    total = jnp.concatenate(sums, axis=1)
    out_ref[...] = total if before_ref is None else total + before_ref[...]


def lowrank_of(at, place, x, before, pieces, after):
    rows, features = x.shape
    half, held = pieces[0].shape
    rank = 2 * half
    operands = [place, x] + pieces + ([] if before is None else [before])
    used = len(operands)
    operands = operands + after
    size = 2 * sum(p.size for p in pieces)
    return pl.pallas_call(
        functools.partial(lowrank_kernel, at, len(pieces)),
        out_shape=[
            jax.ShapeDtypeStruct((rows, rank), jnp.float32),
            jax.ShapeDtypeStruct((half * len(pieces), held - features), pieces[0].dtype),
        ],
        in_specs=[VMEM] * used + [pl.BlockSpec(memory_space=pl.ANY)] * len(after),
        out_specs=[VMEM, VMEM],
        cost_estimate=pl.CostEstimate(
            flops=1_700_000_000, bytes_accessed=2 * rows * features + size, transcendentals=0
        ),
        compiler_params=pltpu.CompilerParams(vmem_limit_bytes=8 * 2**20 + 2 * x.size + 2 * size),
        name="lowrank",
    )(*operands)


def last_rows_kernel(slot_across_ref, x_ref, out_ref):
    room, rows = out_ref.shape[0], x_ref.shape[0]
    pick = lax.broadcasted_iota(jnp.int32, (room, rows), 0) == slot_across_ref[...]
    pick = jnp.where(pick, 1.0, 0.0).astype(jnp.bfloat16)
    step = 1024
    for at in range(0, x_ref.shape[1], step):
        picked = jnp.dot(pick, x_ref[:, at : at + step], preferred_element_type=jnp.float32)
        out_ref[:, at : at + step] = picked.astype(jnp.bfloat16)


def last_rows(slot_across, x, room):
    return pl.pallas_call(
        last_rows_kernel,
        out_shape=jax.ShapeDtypeStruct((room, x.shape[1]), x.dtype),
        in_specs=[VMEM, VMEM],
        out_specs=VMEM,
        cost_estimate=pl.CostEstimate(flops=100_000_000, bytes_accessed=2 * x.shape[0], transcendentals=0),
        compiler_params=pltpu.CompilerParams(vmem_limit_bytes=8 * 2**20),
        name="last_rows",
    )(slot_across, x)


def last_probs_kernel(slot_ref, *refs):
    tiles = windows(slot_ref.shape[0])
    p_refs, out_refs = refs[: 2 * len(tiles)], refs[2 * len(tiles) :]
    for i, (_, first, width) in enumerate(tiles):
        pick = lax.broadcasted_iota(jnp.int32, (width, 128), 1) == slot_ref[first : first + width, :]
        pick = jnp.where(pick, 1.0, 0.0).astype(jnp.bfloat16)
        for side in range(2):
            picked = jnp.dot(p_refs[side * len(tiles) + i][...], pick, preferred_element_type=jnp.float32)
            out_refs[i][:, side * 128 : (side + 1) * 128] = picked.astype(jnp.bfloat16)


def last_probs(slot, left, right):
    pieces = left + right
    return pl.pallas_call(
        last_probs_kernel,
        out_shape=[jax.ShapeDtypeStruct((p.shape[0], 256), p.dtype) for p in left],
        in_specs=[VMEM] * (1 + len(pieces)),
        out_specs=[VMEM] * len(left),
        cost_estimate=pl.CostEstimate(
            flops=100_000_000, bytes_accessed=2 * slot.size, transcendentals=0
        ),
        compiler_params=pltpu.CompilerParams(vmem_limit_bytes=6 * 2**20),
        name="last_probs",
    )(slot, *pieces)


def early_kernel(kv_heads, place_ref, mine_ref, theirs_ref, base_ref, *refs):
    rows = base_ref.shape[0]
    tiles = windows(rows)
    up_refs = refs[: -kv_heads * len(tiles) - 1]
    p_refs, out_ref = refs[len(up_refs) : -1], refs[-1]
    rank = mine_ref.shape[1]
    held = sum(up_ref.shape[0] for up_ref in up_refs)
    pairs = -(-held // (2 * rank))
    place = place_ref[...]
    lowrank = (mine_ref[...] + theirs_ref[...]).astype(jnp.bfloat16)
    twice = jnp.concatenate([lowrank, lowrank], axis=1)
    second = (lax.broadcasted_iota(jnp.int32, twice.shape, 1) >= rank).astype(jnp.int32)
    offset = place - second
    spread = jnp.concatenate(
        [jnp.where(offset == 2 * i, twice, jnp.zeros_like(twice)) for i in range(pairs)], axis=1
    )
    ups = [up_ref[...] for up_ref in up_refs]
    if held < 2 * rank * pairs:
        ups.append(jnp.zeros((2 * rank * pairs - held, base_ref.shape[1]), jnp.bfloat16))
    delta = jnp.dot(
        spread, jnp.concatenate(ups, axis=0), preferred_element_type=jnp.float32
    ).astype(jnp.bfloat16)
    values = (
        base_ref[...].astype(jnp.float32) + adapter_scale * delta.astype(jnp.float32)
    ).astype(jnp.bfloat16)
    wide = GROUP * HEAD_SIZE
    for kv in range(kv_heads):
        columns = slice(kv * HEAD_SIZE, (kv + 1) * HEAD_SIZE)
        for i, (start, first, width) in enumerate(tiles):
            mixed = jnp.dot(
                p_refs[kv * len(tiles) + i][...],
                values[first : first + width, columns],
                preferred_element_type=jnp.float32,
            )
            for head in range(GROUP):
                at = kv * wide + head * HEAD_SIZE
                out_ref[start : start + TILE, at : at + HEAD_SIZE] = mixed[head * TILE : (head + 1) * TILE, :]


def early_product(place, mine, theirs, base, ups, probs):
    rows, value_portion = base.shape
    kv_heads = value_portion // HEAD_SIZE
    flat = [p for per_head in probs for p in per_head]
    return pl.pallas_call(
        functools.partial(early_kernel, kv_heads),
        out_shape=jax.ShapeDtypeStruct((rows, kv_heads * GROUP * HEAD_SIZE), jnp.float32),
        in_specs=[VMEM] * (4 + len(ups) + len(flat)),
        out_specs=VMEM,
        cost_estimate=pl.CostEstimate(flops=50_000_000, bytes_accessed=4 * rows, transcendentals=0),
        compiler_params=pltpu.CompilerParams(vmem_limit_bytes=8 * 2**20),
        name="early_product",
    )(place, mine, theirs, base, *ups, *flat)


def last_lowrank_kernel(x_ref, low_ref, high_ref, *refs):
    out_ref, up_ref = refs[-2:]
    features = x_ref.shape[1]
    stacked = jnp.concatenate([low_ref[:, :features], high_ref[:, :features]], axis=0)
    out_ref[...] = lax.dot_general(x_ref[...], stacked, NT, preferred_element_type=jnp.float32)
    up_ref[...] = jnp.concatenate([low_ref[:, features:], high_ref[:, features:]], axis=0)


def last_lowrank(x, low, high, after):
    rank, columns = 2 * low.shape[0], low.shape[1] - x.shape[1]
    return pl.pallas_call(
        last_lowrank_kernel,
        out_shape=[
            jax.ShapeDtypeStruct((x.shape[0], rank), jnp.float32),
            jax.ShapeDtypeStruct((rank, columns), low.dtype),
        ],
        in_specs=[VMEM] * 3 + [pl.BlockSpec(memory_space=pl.ANY)] * len(after),
        out_specs=[VMEM, VMEM],
        cost_estimate=pl.CostEstimate(flops=600_000_000, bytes_accessed=2 * x.size, transcendentals=0),
        compiler_params=pltpu.CompilerParams(vmem_limit_bytes=6 * 2**20),
        name="last_lowrank",
    )(x, low, high, *after)


def finish_kernel(mine_ref, theirs_ref, up_ref, early_ref, *refs):
    p_refs, (out_ref, block, sems) = refs[:-3], refs[-3:]
    rows = early_ref.shape[0]
    tiles = windows(rows)
    wide = GROUP * HEAD_SIZE
    lowrank = (mine_ref[...] + theirs_ref[...]).astype(jnp.bfloat16)
    delta = jnp.dot(lowrank, up_ref[...], preferred_element_type=jnp.float32).astype(jnp.bfloat16)
    change = (adapter_scale * delta.astype(jnp.float32)).astype(jnp.bfloat16)
    room = change.shape[0]
    if room < 128:
        change = jnp.concatenate([change, jnp.zeros((128 - room, change.shape[1]), jnp.bfloat16)], axis=0)
    none = jnp.zeros((128, HEAD_SIZE), jnp.bfloat16)
    copies = []
    for pair in range(len(p_refs) // len(tiles)):
        at = 2 * pair * HEAD_SIZE
        left, right = change[:, at : at + HEAD_SIZE], change[:, at + HEAD_SIZE : at + 2 * HEAD_SIZE]
        both = jnp.concatenate(
            [jnp.concatenate([left, none], axis=1), jnp.concatenate([none, right], axis=1)], axis=0
        )
        for i, (start, _, _) in enumerate(tiles):
            added = jnp.dot(p_refs[pair * len(tiles) + i][...], both, preferred_element_type=jnp.float32)
            for side in range(2):
                for head in range(GROUP):
                    at = (2 * pair + side) * wide + head * HEAD_SIZE
                    part = added[head * TILE : (head + 1) * TILE, side * HEAD_SIZE : (side + 1) * HEAD_SIZE]
                    whole = early_ref[start : start + TILE, at : at + HEAD_SIZE] + part
                    block[start : start + TILE, at : at + HEAD_SIZE] = whole.astype(jnp.bfloat16)
            if i % 2 == 1:
                rows_done = slice(start - TILE, start + TILE)
                span = slice(2 * pair * wide, 2 * (pair + 1) * wide)
                copy = pltpu.make_async_copy(
                    block.at[rows_done, span], out_ref.at[rows_done, span], sems.at[len(copies)]
                )
                copy.start()
                copies.append(copy)
    for copy in copies:
        copy.wait()


def finish(mine, theirs, up, early, picked):
    flat = [p for pair in picked for p in pair]
    return pl.pallas_call(
        finish_kernel,
        out_shape=jax.ShapeDtypeStruct(early.shape, jnp.bfloat16),
        in_specs=[VMEM] * (4 + len(flat)),
        out_specs=pl.BlockSpec(memory_space=pl.ANY),
        scratch_shapes=[pltpu.VMEM(early.shape, jnp.bfloat16), pltpu.SemaphoreType.DMA((len(flat) // 2,))],
        compiler_params=pltpu.CompilerParams(vmem_limit_bytes=10 * 2**20),
        name="finish",
    )(mine, theirs, up, early, *flat)


def on_device(
    normed_token_rows,
    base_value_rows,
    queries,
    stacked_key_rows,
    adapter_of_row,
    sequence_lengths,
    adapter_down_weight,
    adapter_up_weight,
):
    n = lax.axis_size("rep")
    order = ring_order(n)
    ahead = [(order[i], order[(i + 1) % n]) for i in range(n)]
    back = [(b, a) for a, b in ahead]
    far = n // 2
    distances = [0] + [d for step in range(1, far) for d in (step, -step)] + [far]
    down = jnp.swapaxes(adapter_down_weight[0], 0, 1)
    both = jnp.concatenate([down, adapter_up_weight[0]], axis=1)
    rank = both.shape[0]
    own_low, own_high = both[: rank // 2], both[rank // 2 :]
    place, segment, across, slot, slot_across = masks(
        n, sequence_lengths, adapter_of_row.reshape(1, -1), queries, stacked_key_rows
    )
    low, high = {0: own_low}, {0: own_high}

    def pass_round(held, pairs, sign, steps):
        piece = held[0]
        for step in range(1, steps + 1):
            piece = lax.ppermute(piece, "rep", pairs)
            held[sign * step if step < far else far] = piece

    pass_round(high, ahead, 1, far - 1)
    pass_round(low, back, -1, far - 1)
    pass_round(high, back, -1, far)
    pass_round(low, ahead, 1, far)

    kv_heads = stacked_key_rows.shape[1] // HEAD_SIZE
    arrivals = [
        pair
        for step in range(1, far)
        for pair in ([low[step], high[-step]], [high[step], low[-step]])
    ]
    probs = [
        probs_of(segment, across, queries, stacked_key_rows, kv) for kv in range(kv_heads)
    ]

    picked = [last_probs(slot, probs[kv], probs[kv + 1]) for kv in range(0, kv_heads, 2)]
    most = 2 * normed_token_rows.shape[0] // n
    x_last = last_rows(slot_across, normed_token_rows, -(-most // 16) * 16)

    partial, ups = None, []
    for lo, hi in [(0, 3)] + [(a, a + 2) for a in range(3, n - 1, 2)]:
        pieces = [piece for d in distances[lo:hi] for piece in (low[d], high[d])]
        after = arrivals[kv_heads - 1] if lo == 0 else []
        partial, up = lowrank_of(lo, place, normed_token_rows, partial, pieces, after + ([x_last] + [p[0] for p in picked] if lo == n - 5 else []))
        ups.append(up)
    swap = [(0, 1), (1, 0)]
    early = early_product(place, partial, lax.ppermute(partial, "tp", swap), base_value_rows, ups, probs)
    last, last_up = last_lowrank(x_last, low[far], high[far], [early])
    return finish(last, lax.ppermute(last, "tp", swap), last_up, early, picked)


def solution(mesh):
    placed = (
        P(("groups", "rep"), "tp"),
        P(("groups", "rep"), "tp"),
        P(("groups", "rep"), "tp"),
        P(("groups", "rep"), "tp"),
        P(("groups", "rep"), None),
        P(("groups", "rep"), None),
        P(("groups", "rep"), "tp", None),
        P(("groups", "rep"), None, "tp"),
    )
    return jax.shard_map(
        on_device, mesh=mesh, in_specs=placed, out_specs=P(("groups", "rep"), "tp"), check_vma=False
    )
```

```python
import functools

import jax
import jax.numpy as jnp
import numpy as np
from jax import lax
from jax.experimental import pallas as pl
from jax.experimental.pallas import tpu as pltpu
from jax.sharding import PartitionSpec as P

HEADS = 64
KEY_VALUE_HEADS = 8
HEAD_SIZE = 128
GROUP = HEADS // KEY_VALUE_HEADS
LONGEST = 192
TILE = 64
REACH = -(-(LONGEST - 1) // TILE)
adapter_scale = 2.0

VMEM = pl.BlockSpec(memory_space=pltpu.VMEM)
SMEM = pl.BlockSpec(memory_space=pltpu.SMEM)
NT = (((1,), (1,)), ((), ()))


def ring_order(n):
    if n == 8:
        return list(range(0, n, 2)) + list(range(n - 1, 0, -2))
    return list(range(n))


def windows(rows):
    found = []
    for tile in range(rows // TILE):
        first = max(0, tile - REACH) * TILE
        width = (tile + 1) * TILE - first
        width = -(-width // 128) * 128
        found.append((tile * TILE, first, width))
    return found


def ring_place(replica, n):
    if n == 8:
        return jnp.where(replica & 1 == 0, replica >> 1, n - 1 - (replica >> 1))
    return replica


def column(row):
    wide = jnp.broadcast_to(row.astype(jnp.float32), (8, row.shape[1]))
    return wide.T[:, :1].astype(jnp.int32)


def masks_kernel(n, me_ref, lengths_ref, adapter_ref, near_q_ref, near_k_ref, *refs):
    place_ref, segment_ref, across_ref, slot_ref, slot_across_ref = refs
    distance = ring_place(me_ref[0], n) - ring_place(adapter_ref[...], n)
    distance = jnp.where(distance < 0, distance + n, distance)
    place = jnp.where(distance <= n // 2, jnp.maximum(2 * distance - 1, 0), 2 * (n - distance))
    place_ref[...] = column(place)
    position = lax.broadcasted_iota(jnp.int32, place.shape, 1)
    segment = jnp.zeros(place.shape, jnp.int32)
    end = jnp.int32(0)
    for i in range(lengths_ref.shape[1]):
        end = end + lengths_ref[0, i]
        segment = segment + (position >= end).astype(jnp.int32)
    across_ref[...] = segment
    segment_ref[...] = column(segment)
    rows = place.shape[1]
    last = place == n - 1
    earlier = lax.broadcasted_iota(jnp.int32, (rows, rows), 0) < lax.broadcasted_iota(jnp.int32, (rows, rows), 1)
    ones = jnp.where(jnp.broadcast_to(last, (8, rows)), 1.0, 0.0).astype(jnp.bfloat16)
    count = jnp.dot(ones, jnp.where(earlier, 1.0, 0.0).astype(jnp.bfloat16), preferred_element_type=jnp.float32)
    slot = jnp.where(last, count[:1, :].astype(jnp.int32), -1)
    slot_across_ref[...] = slot
    slot_ref[...] = column(slot)


def masks(n, lengths, adapter_row, queries, keys):
    rows = keys.shape[0]
    tall, flat = [jax.ShapeDtypeStruct(shape, jnp.int32) for shape in ((rows, 1), (1, rows))]
    me = jnp.reshape(lax.axis_index("rep"), (1,)).astype(jnp.int32)
    return pl.pallas_call(
        functools.partial(masks_kernel, n),
        out_shape=[tall, tall, flat, tall, flat],
        in_specs=[SMEM, SMEM, VMEM, VMEM, VMEM],
        out_specs=[VMEM] * 5,
        cost_estimate=pl.CostEstimate(flops=1_000_000_000, bytes_accessed=16 * rows, transcendentals=0),
        compiler_params=pltpu.CompilerParams(vmem_limit_bytes=4 * 2**20),
        name="masks",
    )(me, lengths, adapter_row, queries, keys)


def probs_kernel(kv_head, segment_ref, across_ref, q_ref, k_ref, *refs):
    rows = k_ref.shape[0]
    tiles = windows(rows)
    p_refs = refs[-len(tiles) :]
    factor = float(np.log2(np.e) * HEAD_SIZE**-0.5)
    at = kv_head * HEAD_SIZE
    for p_ref, (start, first, width) in zip(p_refs, tiles):
        t = lax.broadcasted_iota(jnp.int32, (TILE, width), 0) + start
        s = lax.broadcasted_iota(jnp.int32, (TILE, width), 1) + first
        same = segment_ref[start : start + TILE, :] == across_ref[:, first : first + width]
        bias = jnp.where(same & (s <= t), 0.0, -1e30)
        keys = k_ref[first : first + width, at : at + HEAD_SIZE]
        for head in range(GROUP):
            column_at = (kv_head * GROUP + head) * HEAD_SIZE
            q = q_ref[start : start + TILE, column_at : column_at + HEAD_SIZE]
            scores = lax.dot_general(q, keys, NT, preferred_element_type=jnp.float32) + bias
            peak = jnp.max(scores, axis=1, keepdims=True)
            weights = jnp.exp2((scores - peak) * factor)
            inverse = 1.0 / jnp.sum(weights, axis=1, keepdims=True)
            p_ref[head * TILE : (head + 1) * TILE, :] = (weights * inverse).astype(jnp.bfloat16)


def probs_of(segment, across, queries, keys, kv_head):
    rows = keys.shape[0]
    shapes = [(GROUP * TILE, width) for _, _, width in windows(rows)]
    elements = sum(a * b for a, b in shapes)
    return pl.pallas_call(
        functools.partial(probs_kernel, kv_head),
        out_shape=[jax.ShapeDtypeStruct(s, jnp.bfloat16) for s in shapes],
        in_specs=[VMEM] * 4,
        out_specs=[VMEM] * len(shapes),
        cost_estimate=pl.CostEstimate(
            flops=2_000_000_000, bytes_accessed=2 * elements, transcendentals=elements
        ),
        compiler_params=pltpu.CompilerParams(vmem_limit_bytes=12 * 2**20),
        name="probs",
    )(segment, across, queries, keys)


def lowrank_kernel(at, count, place_ref, x_ref, *refs):
    w_refs, (out_ref, up_ref) = refs[:count], refs[-2:]
    before_ref = refs[count] if at > 0 else None
    place = place_ref[...]
    rows, features = x_ref.shape
    half = w_refs[0].shape[0]
    stacked = jnp.concatenate([w_ref[:, :features] for w_ref in w_refs], axis=0)
    product = lax.dot_general(x_ref[...], stacked, NT, preferred_element_type=jnp.float32)
    sums = [jnp.zeros((rows, half), jnp.float32)] * 2
    for i in range(count):
        part = product[:, i * half : (i + 1) * half]
        sums[i % 2] = sums[i % 2] + jnp.where(place == at + i // 2, part, 0.0)
    up_ref[...] = jnp.concatenate([w_ref[:, features:] for w_ref in w_refs], axis=0)
    total = jnp.concatenate(sums, axis=1)
    out_ref[...] = total if before_ref is None else total + before_ref[...]


def lowrank_of(at, place, x, before, pieces, after):
    rows, features = x.shape
    half, held = pieces[0].shape
    rank = 2 * half
    operands = [place, x] + pieces + ([] if before is None else [before])
    used = len(operands)
    operands = operands + after
    size = 2 * sum(p.size for p in pieces)
    return pl.pallas_call(
        functools.partial(lowrank_kernel, at, len(pieces)),
        out_shape=[
            jax.ShapeDtypeStruct((rows, rank), jnp.float32),
            jax.ShapeDtypeStruct((half * len(pieces), held - features), pieces[0].dtype),
        ],
        in_specs=[VMEM] * used + [pl.BlockSpec(memory_space=pl.ANY)] * len(after),
        out_specs=[VMEM, VMEM],
        cost_estimate=pl.CostEstimate(
            flops=1_700_000_000, bytes_accessed=2 * rows * features + size, transcendentals=0
        ),
        compiler_params=pltpu.CompilerParams(vmem_limit_bytes=8 * 2**20 + 2 * x.size + 2 * size),
        name="lowrank",
    )(*operands)


def last_rows_kernel(slot_across_ref, x_ref, out_ref):
    room, rows = out_ref.shape[0], x_ref.shape[0]
    pick = lax.broadcasted_iota(jnp.int32, (room, rows), 0) == slot_across_ref[...]
    pick = jnp.where(pick, 1.0, 0.0).astype(jnp.bfloat16)
    step = 1024
    for at in range(0, x_ref.shape[1], step):
        picked = jnp.dot(pick, x_ref[:, at : at + step], preferred_element_type=jnp.float32)
        out_ref[:, at : at + step] = picked.astype(jnp.bfloat16)


def last_rows(slot_across, x, room):
    return pl.pallas_call(
        last_rows_kernel,
        out_shape=jax.ShapeDtypeStruct((room, x.shape[1]), x.dtype),
        in_specs=[VMEM, VMEM],
        out_specs=VMEM,
        cost_estimate=pl.CostEstimate(flops=100_000_000, bytes_accessed=2 * x.shape[0], transcendentals=0),
        compiler_params=pltpu.CompilerParams(vmem_limit_bytes=8 * 2**20),
        name="last_rows",
    )(slot_across, x)


def last_probs_kernel(slot_ref, *refs):
    tiles = windows(slot_ref.shape[0])
    p_refs, out_refs = refs[: 2 * len(tiles)], refs[2 * len(tiles) :]
    for i, (_, first, width) in enumerate(tiles):
        pick = lax.broadcasted_iota(jnp.int32, (width, 128), 1) == slot_ref[first : first + width, :]
        pick = jnp.where(pick, 1.0, 0.0).astype(jnp.bfloat16)
        for side in range(2):
            picked = jnp.dot(p_refs[side * len(tiles) + i][...], pick, preferred_element_type=jnp.float32)
            out_refs[i][:, side * 128 : (side + 1) * 128] = picked.astype(jnp.bfloat16)


def last_probs(slot, left, right):
    pieces = left + right
    return pl.pallas_call(
        last_probs_kernel,
        out_shape=[jax.ShapeDtypeStruct((p.shape[0], 256), p.dtype) for p in left],
        in_specs=[VMEM] * (1 + len(pieces)),
        out_specs=[VMEM] * len(left),
        cost_estimate=pl.CostEstimate(
            flops=100_000_000, bytes_accessed=2 * slot.size, transcendentals=0
        ),
        compiler_params=pltpu.CompilerParams(vmem_limit_bytes=6 * 2**20),
        name="last_probs",
    )(slot, *pieces)


def early_kernel(kv_heads, place_ref, mine_ref, theirs_ref, base_ref, *refs):
    rows = base_ref.shape[0]
    tiles = windows(rows)
    up_refs = refs[: -kv_heads * len(tiles) - 1]
    p_refs, out_ref = refs[len(up_refs) : -1], refs[-1]
    rank = mine_ref.shape[1]
    held = sum(up_ref.shape[0] for up_ref in up_refs)
    pairs = -(-held // (2 * rank))
    place = place_ref[...]
    lowrank = (mine_ref[...] + theirs_ref[...]).astype(jnp.bfloat16)
    twice = jnp.concatenate([lowrank, lowrank], axis=1)
    second = (lax.broadcasted_iota(jnp.int32, twice.shape, 1) >= rank).astype(jnp.int32)
    offset = place - second
    spread = jnp.concatenate(
        [jnp.where(offset == 2 * i, twice, jnp.zeros_like(twice)) for i in range(pairs)], axis=1
    )
    ups = [up_ref[...] for up_ref in up_refs]
    if held < 2 * rank * pairs:
        ups.append(jnp.zeros((2 * rank * pairs - held, base_ref.shape[1]), jnp.bfloat16))
    delta = jnp.dot(
        spread, jnp.concatenate(ups, axis=0), preferred_element_type=jnp.float32
    ).astype(jnp.bfloat16)
    values = (
        base_ref[...].astype(jnp.float32) + adapter_scale * delta.astype(jnp.float32)
    ).astype(jnp.bfloat16)
    wide = GROUP * HEAD_SIZE
    for kv in range(kv_heads):
        columns = slice(kv * HEAD_SIZE, (kv + 1) * HEAD_SIZE)
        for i, (start, first, width) in enumerate(tiles):
            mixed = jnp.dot(
                p_refs[kv * len(tiles) + i][...],
                values[first : first + width, columns],
                preferred_element_type=jnp.float32,
            )
            for head in range(GROUP):
                at = kv * wide + head * HEAD_SIZE
                out_ref[start : start + TILE, at : at + HEAD_SIZE] = mixed[head * TILE : (head + 1) * TILE, :]


def early_product(place, mine, theirs, base, ups, probs):
    rows, value_portion = base.shape
    kv_heads = value_portion // HEAD_SIZE
    flat = [p for per_head in probs for p in per_head]
    return pl.pallas_call(
        functools.partial(early_kernel, kv_heads),
        out_shape=jax.ShapeDtypeStruct((rows, kv_heads * GROUP * HEAD_SIZE), jnp.float32),
        in_specs=[VMEM] * (4 + len(ups) + len(flat)),
        out_specs=VMEM,
        cost_estimate=pl.CostEstimate(flops=50_000_000, bytes_accessed=4 * rows, transcendentals=0),
        compiler_params=pltpu.CompilerParams(vmem_limit_bytes=8 * 2**20),
        name="early_product",
    )(place, mine, theirs, base, *ups, *flat)


def last_lowrank_kernel(x_ref, low_ref, high_ref, *refs):
    out_ref, up_ref = refs[-2:]
    features = x_ref.shape[1]
    stacked = jnp.concatenate([low_ref[:, :features], high_ref[:, :features]], axis=0)
    out_ref[...] = lax.dot_general(x_ref[...], stacked, NT, preferred_element_type=jnp.float32)
    up_ref[...] = jnp.concatenate([low_ref[:, features:], high_ref[:, features:]], axis=0)


def last_lowrank(x, low, high, after):
    rank, columns = 2 * low.shape[0], low.shape[1] - x.shape[1]
    return pl.pallas_call(
        last_lowrank_kernel,
        out_shape=[
            jax.ShapeDtypeStruct((x.shape[0], rank), jnp.float32),
            jax.ShapeDtypeStruct((rank, columns), low.dtype),
        ],
        in_specs=[VMEM] * 3 + [pl.BlockSpec(memory_space=pl.ANY)] * len(after),
        out_specs=[VMEM, VMEM],
        cost_estimate=pl.CostEstimate(flops=600_000_000, bytes_accessed=2 * x.size, transcendentals=0),
        compiler_params=pltpu.CompilerParams(vmem_limit_bytes=6 * 2**20),
        name="last_lowrank",
    )(x, low, high, *after)


def finish_kernel(mine_ref, theirs_ref, up_ref, early_ref, *refs):
    p_refs, (out_ref, block, sems) = refs[:-3], refs[-3:]
    rows = early_ref.shape[0]
    tiles = windows(rows)
    wide = GROUP * HEAD_SIZE
    lowrank = (mine_ref[...] + theirs_ref[...]).astype(jnp.bfloat16)
    delta = jnp.dot(lowrank, up_ref[...], preferred_element_type=jnp.float32).astype(jnp.bfloat16)
    change = (adapter_scale * delta.astype(jnp.float32)).astype(jnp.bfloat16)
    room = change.shape[0]
    if room < 128:
        change = jnp.concatenate([change, jnp.zeros((128 - room, change.shape[1]), jnp.bfloat16)], axis=0)
    none = jnp.zeros((128, HEAD_SIZE), jnp.bfloat16)
    copies = []
    for pair in range(len(p_refs) // len(tiles)):
        at = 2 * pair * HEAD_SIZE
        left, right = change[:, at : at + HEAD_SIZE], change[:, at + HEAD_SIZE : at + 2 * HEAD_SIZE]
        both = jnp.concatenate(
            [jnp.concatenate([left, none], axis=1), jnp.concatenate([none, right], axis=1)], axis=0
        )
        for i, (start, _, _) in enumerate(tiles):
            p_ref = p_refs[pair * len(tiles) + i]
            for half in range(2):
                heads = range(half * GROUP // 2, (half + 1) * GROUP // 2)
                near = slice(heads[0] * TILE, (heads[-1] + 1) * TILE)
                added = jnp.dot(p_ref[near, :], both, preferred_element_type=jnp.float32)
                for side in range(2):
                    for k, head in enumerate(heads):
                        at = (2 * pair + side) * wide + head * HEAD_SIZE
                        part = added[k * TILE : (k + 1) * TILE, side * HEAD_SIZE : (side + 1) * HEAD_SIZE]
                        whole = early_ref[start : start + TILE, at : at + HEAD_SIZE] + part
                        block[start : start + TILE, at : at + HEAD_SIZE] = whole.astype(jnp.bfloat16)
            rows_done = slice(start, start + TILE)
            span = slice(2 * pair * wide, 2 * (pair + 1) * wide)
            copy = pltpu.make_async_copy(
                block.at[rows_done, span], out_ref.at[rows_done, span], sems.at[len(copies)]
            )
            copy.start()
            copies.append(copy)
    for copy in copies:
        copy.wait()


def finish(mine, theirs, up, early, picked):
    flat = [p for pair in picked for p in pair]
    return pl.pallas_call(
        finish_kernel,
        out_shape=jax.ShapeDtypeStruct(early.shape, jnp.bfloat16),
        in_specs=[VMEM] * (4 + len(flat)),
        out_specs=pl.BlockSpec(memory_space=pl.ANY),
        scratch_shapes=[pltpu.VMEM(early.shape, jnp.bfloat16), pltpu.SemaphoreType.DMA((len(flat),))],
        compiler_params=pltpu.CompilerParams(vmem_limit_bytes=10 * 2**20),
        name="finish",
    )(mine, theirs, up, early, *flat)


def on_device(
    normed_token_rows,
    base_value_rows,
    queries,
    stacked_key_rows,
    adapter_of_row,
    sequence_lengths,
    adapter_down_weight,
    adapter_up_weight,
):
    n = lax.axis_size("rep")
    order = ring_order(n)
    ahead = [(order[i], order[(i + 1) % n]) for i in range(n)]
    back = [(b, a) for a, b in ahead]
    far = n // 2
    distances = [0] + [d for step in range(1, far) for d in (step, -step)] + [far]
    down = jnp.swapaxes(adapter_down_weight[0], 0, 1)
    both = jnp.concatenate([down, adapter_up_weight[0]], axis=1)
    rank = both.shape[0]
    own_low, own_high = both[: rank // 2], both[rank // 2 :]
    place, segment, across, slot, slot_across = masks(
        n, sequence_lengths, adapter_of_row.reshape(1, -1), queries, stacked_key_rows
    )
    low, high = {0: own_low}, {0: own_high}

    def pass_round(held, pairs, sign, steps):
        piece = held[0]
        for step in range(1, steps + 1):
            piece = lax.ppermute(piece, "rep", pairs)
            held[sign * step if step < far else far] = piece

    pass_round(high, ahead, 1, far - 1)
    pass_round(low, back, -1, far - 1)
    pass_round(high, back, -1, far)
    pass_round(low, ahead, 1, far)

    kv_heads = stacked_key_rows.shape[1] // HEAD_SIZE
    arrivals = [
        pair
        for step in range(1, far)
        for pair in ([low[step], high[-step]], [high[step], low[-step]])
    ]
    probs = [
        probs_of(segment, across, queries, stacked_key_rows, kv) for kv in range(kv_heads)
    ]

    picked = [last_probs(slot, probs[kv], probs[kv + 1]) for kv in range(0, kv_heads, 2)]
    most = 2 * normed_token_rows.shape[0] // n
    x_last = last_rows(slot_across, normed_token_rows, -(-most // 16) * 16)

    partial, ups = None, []
    for lo, hi in [(0, 3)] + [(a, a + 2) for a in range(3, n - 1, 2)]:
        pieces = [piece for d in distances[lo:hi] for piece in (low[d], high[d])]
        after = arrivals[kv_heads - 1] if lo == 0 else []
        partial, up = lowrank_of(lo, place, normed_token_rows, partial, pieces, after + ([x_last] + [p[0] for p in picked] if lo == n - 5 else []))
        ups.append(up)
    swap = [(0, 1), (1, 0)]
    early = early_product(place, partial, lax.ppermute(partial, "tp", swap), base_value_rows, ups, probs)
    last, last_up = last_lowrank(x_last, low[far], high[far], [early])
    return finish(last, lax.ppermute(last, "tp", swap), last_up, early, picked)


def solution(mesh):
    placed = (
        P(("groups", "rep"), "tp"),
        P(("groups", "rep"), "tp"),
        P(("groups", "rep"), "tp"),
        P(("groups", "rep"), "tp"),
        P(("groups", "rep"), None),
        P(("groups", "rep"), None),
        P(("groups", "rep"), "tp", None),
        P(("groups", "rep"), None, "tp"),
    )
    return jax.shard_map(
        on_device, mesh=mesh, in_specs=placed, out_specs=P(("groups", "rep"), "tp"), check_vma=False
    )
```

```python
import functools

import jax
import jax.numpy as jnp
import numpy as np
from jax import lax
from jax.experimental import pallas as pl
from jax.experimental.pallas import tpu as pltpu
from jax.sharding import PartitionSpec as P

HEADS = 64
KEY_VALUE_HEADS = 8
HEAD_SIZE = 128
GROUP = HEADS // KEY_VALUE_HEADS
LONGEST = 192
TILE = 64
REACH = -(-(LONGEST - 1) // TILE)
adapter_scale = 2.0

VMEM = pl.BlockSpec(memory_space=pltpu.VMEM)
SMEM = pl.BlockSpec(memory_space=pltpu.SMEM)
NT = (((1,), (1,)), ((), ()))


def ring_order(n):
    if n == 8:
        return list(range(0, n, 2)) + list(range(n - 1, 0, -2))
    return list(range(n))


def windows(rows):
    found = []
    for tile in range(rows // TILE):
        first = max(0, tile - REACH) * TILE
        width = (tile + 1) * TILE - first
        width = -(-width // 128) * 128
        found.append((tile * TILE, first, width))
    return found


def ring_place(replica, n):
    if n == 8:
        return jnp.where(replica & 1 == 0, replica >> 1, n - 1 - (replica >> 1))
    return replica


def pack_kernel(down_ref, up_ref, low_ref, high_ref, sems):
    half, features = low_ref.shape[0], down_ref.shape[1]
    copies = []
    for i, piece_ref in enumerate((low_ref, high_ref)):
        ranks = slice(i * half, (i + 1) * half)
        for part_ref, columns in ((down_ref, slice(0, features)), (up_ref, slice(features, piece_ref.shape[1]))):
            copies.append(
                pltpu.make_async_copy(part_ref.at[ranks, :], piece_ref.at[:, columns], sems.at[len(copies)])
            )
    for copy in copies:
        copy.start()
    for copy in copies:
        copy.wait()


def pack(down, up):
    piece = jax.ShapeDtypeStruct((down.shape[0] // 2, down.shape[1] + up.shape[1]), down.dtype)
    return pl.pallas_call(
        pack_kernel,
        out_shape=[piece, piece],
        in_specs=[pl.BlockSpec(memory_space=pl.ANY)] * 2,
        out_specs=[pl.BlockSpec(memory_space=pl.ANY)] * 2,
        scratch_shapes=[pltpu.SemaphoreType.DMA((4,))],
        cost_estimate=pl.CostEstimate(flops=0, bytes_accessed=4 * piece.size, transcendentals=0),
        compiler_params=pltpu.CompilerParams(vmem_limit_bytes=60 * 2**20),
        name="pack",
    )(down, up)


def column(row):
    wide = jnp.broadcast_to(row.astype(jnp.float32), (8, row.shape[1]))
    return wide.T[:, :1].astype(jnp.int32)


def masks_kernel(n, me_ref, lengths_ref, adapter_ref, near_q_ref, near_k_ref, *refs):
    place_ref, segment_ref, across_ref, slot_ref, slot_across_ref = refs
    distance = ring_place(me_ref[0], n) - ring_place(adapter_ref[...], n)
    distance = jnp.where(distance < 0, distance + n, distance)
    place = jnp.where(distance <= n // 2, jnp.maximum(2 * distance - 1, 0), 2 * (n - distance))
    place_ref[...] = column(place)
    position = lax.broadcasted_iota(jnp.int32, place.shape, 1)
    segment = jnp.zeros(place.shape, jnp.int32)
    end = jnp.int32(0)
    for i in range(lengths_ref.shape[1]):
        end = end + lengths_ref[0, i]
        segment = segment + (position >= end).astype(jnp.int32)
    across_ref[...] = segment
    segment_ref[...] = column(segment)
    rows = place.shape[1]
    last = place == n - 1
    earlier = lax.broadcasted_iota(jnp.int32, (rows, rows), 0) < lax.broadcasted_iota(jnp.int32, (rows, rows), 1)
    ones = jnp.where(jnp.broadcast_to(last, (8, rows)), 1.0, 0.0).astype(jnp.bfloat16)
    count = jnp.dot(ones, jnp.where(earlier, 1.0, 0.0).astype(jnp.bfloat16), preferred_element_type=jnp.float32)
    slot = jnp.where(last, count[:1, :].astype(jnp.int32), -1)
    slot_across_ref[...] = slot
    slot_ref[...] = column(slot)


def masks(n, lengths, adapter_row, queries, keys):
    rows = keys.shape[0]
    tall, flat = [jax.ShapeDtypeStruct(shape, jnp.int32) for shape in ((rows, 1), (1, rows))]
    me = jnp.reshape(lax.axis_index("rep"), (1,)).astype(jnp.int32)
    return pl.pallas_call(
        functools.partial(masks_kernel, n),
        out_shape=[tall, tall, flat, tall, flat],
        in_specs=[SMEM, SMEM, VMEM, VMEM, VMEM],
        out_specs=[VMEM] * 5,
        cost_estimate=pl.CostEstimate(flops=1_000_000_000, bytes_accessed=16 * rows, transcendentals=0),
        compiler_params=pltpu.CompilerParams(vmem_limit_bytes=4 * 2**20),
        name="masks",
    )(me, lengths, adapter_row, queries, keys)


def probs_kernel(kv_head, segment_ref, across_ref, q_ref, k_ref, *refs):
    rows = k_ref.shape[0]
    tiles = windows(rows)
    p_refs = refs[-len(tiles) :]
    factor = float(np.log2(np.e) * HEAD_SIZE**-0.5)
    at = kv_head * HEAD_SIZE
    for p_ref, (start, first, width) in zip(p_refs, tiles):
        t = lax.broadcasted_iota(jnp.int32, (TILE, width), 0) + start
        s = lax.broadcasted_iota(jnp.int32, (TILE, width), 1) + first
        same = segment_ref[start : start + TILE, :] == across_ref[:, first : first + width]
        bias = jnp.where(same & (s <= t), 0.0, -1e30)
        keys = k_ref[first : first + width, at : at + HEAD_SIZE]
        for head in range(GROUP):
            column_at = (kv_head * GROUP + head) * HEAD_SIZE
            q = q_ref[start : start + TILE, column_at : column_at + HEAD_SIZE]
            scores = lax.dot_general(q, keys, NT, preferred_element_type=jnp.float32) + bias
            peak = jnp.max(scores, axis=1, keepdims=True)
            weights = jnp.exp2((scores - peak) * factor)
            inverse = 1.0 / jnp.sum(weights, axis=1, keepdims=True)
            p_ref[head * TILE : (head + 1) * TILE, :] = (weights * inverse).astype(jnp.bfloat16)


def probs_of(segment, across, queries, keys, kv_head):
    rows = keys.shape[0]
    shapes = [(GROUP * TILE, width) for _, _, width in windows(rows)]
    elements = sum(a * b for a, b in shapes)
    return pl.pallas_call(
        functools.partial(probs_kernel, kv_head),
        out_shape=[jax.ShapeDtypeStruct(s, jnp.bfloat16) for s in shapes],
        in_specs=[VMEM] * 4,
        out_specs=[VMEM] * len(shapes),
        cost_estimate=pl.CostEstimate(
            flops=2_000_000_000, bytes_accessed=2 * elements, transcendentals=elements
        ),
        compiler_params=pltpu.CompilerParams(vmem_limit_bytes=12 * 2**20),
        name="probs",
    )(segment, across, queries, keys)


def lowrank_kernel(at, count, place_ref, x_ref, *refs):
    w_refs, (out_ref, up_ref) = refs[:count], refs[-2:]
    before_ref = refs[count] if at > 0 else None
    place = place_ref[...]
    rows, features = x_ref.shape
    half = w_refs[0].shape[0]
    stacked = jnp.concatenate([w_ref[:, :features] for w_ref in w_refs], axis=0)
    product = lax.dot_general(x_ref[...], stacked, NT, preferred_element_type=jnp.float32)
    sums = [jnp.zeros((rows, half), jnp.float32)] * 2
    for i in range(count):
        part = product[:, i * half : (i + 1) * half]
        sums[i % 2] = sums[i % 2] + jnp.where(place == at + i // 2, part, 0.0)
    up_ref[...] = jnp.concatenate([w_ref[:, features:] for w_ref in w_refs], axis=0)
    total = jnp.concatenate(sums, axis=1)
    out_ref[...] = total if before_ref is None else total + before_ref[...]


def lowrank_of(at, place, x, before, pieces, after):
    rows, features = x.shape
    half, held = pieces[0].shape
    rank = 2 * half
    operands = [place, x] + pieces + ([] if before is None else [before])
    used = len(operands)
    operands = operands + after
    size = 2 * sum(p.size for p in pieces)
    return pl.pallas_call(
        functools.partial(lowrank_kernel, at, len(pieces)),
        out_shape=[
            jax.ShapeDtypeStruct((rows, rank), jnp.float32),
            jax.ShapeDtypeStruct((half * len(pieces), held - features), pieces[0].dtype),
        ],
        in_specs=[VMEM] * used + [pl.BlockSpec(memory_space=pl.ANY)] * len(after),
        out_specs=[VMEM, VMEM],
        cost_estimate=pl.CostEstimate(
            flops=1_700_000_000, bytes_accessed=2 * rows * features + size, transcendentals=0
        ),
        compiler_params=pltpu.CompilerParams(vmem_limit_bytes=8 * 2**20 + 2 * x.size + 2 * size),
        name="lowrank",
    )(*operands)


def last_rows_kernel(slot_across_ref, x_ref, out_ref):
    room, rows = out_ref.shape[0], x_ref.shape[0]
    pick = lax.broadcasted_iota(jnp.int32, (room, rows), 0) == slot_across_ref[...]
    pick = jnp.where(pick, 1.0, 0.0).astype(jnp.bfloat16)
    step = 1024
    for at in range(0, x_ref.shape[1], step):
        picked = jnp.dot(pick, x_ref[:, at : at + step], preferred_element_type=jnp.float32)
        out_ref[:, at : at + step] = picked.astype(jnp.bfloat16)


def last_rows(slot_across, x, room):
    return pl.pallas_call(
        last_rows_kernel,
        out_shape=jax.ShapeDtypeStruct((room, x.shape[1]), x.dtype),
        in_specs=[VMEM, VMEM],
        out_specs=VMEM,
        cost_estimate=pl.CostEstimate(flops=100_000_000, bytes_accessed=2 * x.shape[0], transcendentals=0),
        compiler_params=pltpu.CompilerParams(vmem_limit_bytes=8 * 2**20),
        name="last_rows",
    )(slot_across, x)


def last_probs_kernel(slot_ref, *refs):
    tiles = windows(slot_ref.shape[0])
    p_refs, out_refs = refs[: 2 * len(tiles)], refs[2 * len(tiles) :]
    for i, (_, first, width) in enumerate(tiles):
        pick = lax.broadcasted_iota(jnp.int32, (width, 128), 1) == slot_ref[first : first + width, :]
        pick = jnp.where(pick, 1.0, 0.0).astype(jnp.bfloat16)
        for side in range(2):
            picked = jnp.dot(p_refs[side * len(tiles) + i][...], pick, preferred_element_type=jnp.float32)
            out_refs[i][:, side * 128 : (side + 1) * 128] = picked.astype(jnp.bfloat16)


def last_probs(slot, left, right):
    pieces = left + right
    return pl.pallas_call(
        last_probs_kernel,
        out_shape=[jax.ShapeDtypeStruct((p.shape[0], 256), p.dtype) for p in left],
        in_specs=[VMEM] * (1 + len(pieces)),
        out_specs=[VMEM] * len(left),
        cost_estimate=pl.CostEstimate(
            flops=100_000_000, bytes_accessed=2 * slot.size, transcendentals=0
        ),
        compiler_params=pltpu.CompilerParams(vmem_limit_bytes=6 * 2**20),
        name="last_probs",
    )(slot, *pieces)


def early_kernel(kv_heads, place_ref, mine_ref, theirs_ref, base_ref, *refs):
    rows = base_ref.shape[0]
    tiles = windows(rows)
    up_refs = refs[: -kv_heads * len(tiles) - 1]
    p_refs, out_ref = refs[len(up_refs) : -1], refs[-1]
    rank = mine_ref.shape[1]
    held = sum(up_ref.shape[0] for up_ref in up_refs)
    pairs = -(-held // (2 * rank))
    place = place_ref[...]
    lowrank = (mine_ref[...] + theirs_ref[...]).astype(jnp.bfloat16)
    twice = jnp.concatenate([lowrank, lowrank], axis=1)
    second = (lax.broadcasted_iota(jnp.int32, twice.shape, 1) >= rank).astype(jnp.int32)
    offset = place - second
    spread = jnp.concatenate(
        [jnp.where(offset == 2 * i, twice, jnp.zeros_like(twice)) for i in range(pairs)], axis=1
    )
    ups = [up_ref[...] for up_ref in up_refs]
    if held < 2 * rank * pairs:
        ups.append(jnp.zeros((2 * rank * pairs - held, base_ref.shape[1]), jnp.bfloat16))
    delta = jnp.dot(
        spread, jnp.concatenate(ups, axis=0), preferred_element_type=jnp.float32
    ).astype(jnp.bfloat16)
    values = (
        base_ref[...].astype(jnp.float32) + adapter_scale * delta.astype(jnp.float32)
    ).astype(jnp.bfloat16)
    wide = GROUP * HEAD_SIZE
    for kv in range(kv_heads):
        columns = slice(kv * HEAD_SIZE, (kv + 1) * HEAD_SIZE)
        for i, (start, first, width) in enumerate(tiles):
            mixed = jnp.dot(
                p_refs[kv * len(tiles) + i][...],
                values[first : first + width, columns],
                preferred_element_type=jnp.float32,
            )
            for head in range(GROUP):
                at = kv * wide + head * HEAD_SIZE
                out_ref[start : start + TILE, at : at + HEAD_SIZE] = mixed[head * TILE : (head + 1) * TILE, :]


def early_product(place, mine, theirs, base, ups, probs):
    rows, value_portion = base.shape
    kv_heads = value_portion // HEAD_SIZE
    flat = [p for per_head in probs for p in per_head]
    return pl.pallas_call(
        functools.partial(early_kernel, kv_heads),
        out_shape=jax.ShapeDtypeStruct((rows, kv_heads * GROUP * HEAD_SIZE), jnp.float32),
        in_specs=[VMEM] * (4 + len(ups) + len(flat)),
        out_specs=VMEM,
        cost_estimate=pl.CostEstimate(flops=50_000_000, bytes_accessed=4 * rows, transcendentals=0),
        compiler_params=pltpu.CompilerParams(vmem_limit_bytes=8 * 2**20),
        name="early_product",
    )(place, mine, theirs, base, *ups, *flat)


def last_lowrank_kernel(x_ref, low_ref, high_ref, *refs):
    out_ref, up_ref = refs[-2:]
    features = x_ref.shape[1]
    stacked = jnp.concatenate([low_ref[:, :features], high_ref[:, :features]], axis=0)
    out_ref[...] = lax.dot_general(x_ref[...], stacked, NT, preferred_element_type=jnp.float32)
    up_ref[...] = jnp.concatenate([low_ref[:, features:], high_ref[:, features:]], axis=0)


def last_lowrank(x, low, high, after):
    rank, columns = 2 * low.shape[0], low.shape[1] - x.shape[1]
    return pl.pallas_call(
        last_lowrank_kernel,
        out_shape=[
            jax.ShapeDtypeStruct((x.shape[0], rank), jnp.float32),
            jax.ShapeDtypeStruct((rank, columns), low.dtype),
        ],
        in_specs=[VMEM] * 3 + [pl.BlockSpec(memory_space=pl.ANY)] * len(after),
        out_specs=[VMEM, VMEM],
        cost_estimate=pl.CostEstimate(flops=600_000_000, bytes_accessed=2 * x.size, transcendentals=0),
        compiler_params=pltpu.CompilerParams(vmem_limit_bytes=6 * 2**20),
        name="last_lowrank",
    )(x, low, high, *after)


def finish_kernel(mine_ref, theirs_ref, up_ref, early_ref, *refs):
    p_refs, (out_ref, block, sems) = refs[:-3], refs[-3:]
    rows = early_ref.shape[0]
    tiles = windows(rows)
    wide = GROUP * HEAD_SIZE
    lowrank = (mine_ref[...] + theirs_ref[...]).astype(jnp.bfloat16)
    delta = jnp.dot(lowrank, up_ref[...], preferred_element_type=jnp.float32).astype(jnp.bfloat16)
    change = (adapter_scale * delta.astype(jnp.float32)).astype(jnp.bfloat16)
    room = change.shape[0]
    if room < 128:
        change = jnp.concatenate([change, jnp.zeros((128 - room, change.shape[1]), jnp.bfloat16)], axis=0)
    none = jnp.zeros((128, HEAD_SIZE), jnp.bfloat16)
    copies = []
    for pair in range(len(p_refs) // len(tiles)):
        at = 2 * pair * HEAD_SIZE
        left, right = change[:, at : at + HEAD_SIZE], change[:, at + HEAD_SIZE : at + 2 * HEAD_SIZE]
        both = jnp.concatenate(
            [jnp.concatenate([left, none], axis=1), jnp.concatenate([none, right], axis=1)], axis=0
        )
        for i, (start, _, _) in enumerate(tiles):
            p_ref = p_refs[pair * len(tiles) + i]
            for half in range(2):
                heads = range(half * GROUP // 2, (half + 1) * GROUP // 2)
                near = slice(heads[0] * TILE, (heads[-1] + 1) * TILE)
                added = jnp.dot(p_ref[near, :], both, preferred_element_type=jnp.float32)
                for side in range(2):
                    for k, head in enumerate(heads):
                        at = (2 * pair + side) * wide + head * HEAD_SIZE
                        part = added[k * TILE : (k + 1) * TILE, side * HEAD_SIZE : (side + 1) * HEAD_SIZE]
                        whole = early_ref[start : start + TILE, at : at + HEAD_SIZE] + part
                        block[start : start + TILE, at : at + HEAD_SIZE] = whole.astype(jnp.bfloat16)
            rows_done = slice(start, start + TILE)
            span = slice(2 * pair * wide, 2 * (pair + 1) * wide)
            copy = pltpu.make_async_copy(
                block.at[rows_done, span], out_ref.at[rows_done, span], sems.at[len(copies)]
            )
            copy.start()
            copies.append(copy)
    for copy in copies:
        copy.wait()


def finish(mine, theirs, up, early, picked):
    flat = [p for pair in picked for p in pair]
    return pl.pallas_call(
        finish_kernel,
        out_shape=jax.ShapeDtypeStruct(early.shape, jnp.bfloat16),
        in_specs=[VMEM] * (4 + len(flat)),
        out_specs=pl.BlockSpec(memory_space=pl.ANY),
        scratch_shapes=[pltpu.VMEM(early.shape, jnp.bfloat16), pltpu.SemaphoreType.DMA((len(flat),))],
        compiler_params=pltpu.CompilerParams(vmem_limit_bytes=10 * 2**20),
        name="finish",
    )(mine, theirs, up, early, *flat)


def on_device(
    normed_token_rows,
    base_value_rows,
    queries,
    stacked_key_rows,
    adapter_of_row,
    sequence_lengths,
    adapter_down_weight,
    adapter_up_weight,
):
    n = lax.axis_size("rep")
    order = ring_order(n)
    ahead = [(order[i], order[(i + 1) % n]) for i in range(n)]
    back = [(b, a) for a, b in ahead]
    far = n // 2
    distances = [0] + [d for step in range(1, far) for d in (step, -step)] + [far]
    down = jnp.swapaxes(adapter_down_weight[0], 0, 1)
    own_low, own_high = pack(down, adapter_up_weight[0])
    place, segment, across, slot, slot_across = masks(
        n, sequence_lengths, adapter_of_row.reshape(1, -1), queries, stacked_key_rows
    )
    low, high = {0: own_low}, {0: own_high}

    def pass_round(held, pairs, sign, steps):
        piece = held[0]
        for step in range(1, steps + 1):
            piece = lax.ppermute(piece, "rep", pairs)
            held[sign * step if step < far else far] = piece

    pass_round(high, ahead, 1, far - 1)
    pass_round(low, back, -1, far - 1)
    pass_round(high, back, -1, far)
    pass_round(low, ahead, 1, far)

    kv_heads = stacked_key_rows.shape[1] // HEAD_SIZE
    arrivals = [
        pair
        for step in range(1, far)
        for pair in ([low[step], high[-step]], [high[step], low[-step]])
    ]
    probs = [
        probs_of(segment, across, queries, stacked_key_rows, kv) for kv in range(kv_heads)
    ]

    picked = [last_probs(slot, probs[kv], probs[kv + 1]) for kv in range(0, kv_heads, 2)]
    most = 2 * normed_token_rows.shape[0] // n
    x_last = last_rows(slot_across, normed_token_rows, -(-most // 16) * 16)

    partial, ups = None, []
    for lo, hi in [(0, 3)] + [(a, a + 2) for a in range(3, n - 1, 2)]:
        pieces = [piece for d in distances[lo:hi] for piece in (low[d], high[d])]
        after = arrivals[kv_heads - 1] if lo == 0 else []
        partial, up = lowrank_of(lo, place, normed_token_rows, partial, pieces, after + ([x_last] + [p[0] for p in picked] if lo == n - 5 else []))
        ups.append(up)
    swap = [(0, 1), (1, 0)]
    early = early_product(place, partial, lax.ppermute(partial, "tp", swap), base_value_rows, ups, probs)
    last, last_up = last_lowrank(x_last, low[far], high[far], [early])
    return finish(last, lax.ppermute(last, "tp", swap), last_up, early, picked)


def solution(mesh):
    placed = (
        P(("groups", "rep"), "tp"),
        P(("groups", "rep"), "tp"),
        P(("groups", "rep"), "tp"),
        P(("groups", "rep"), "tp"),
        P(("groups", "rep"), None),
        P(("groups", "rep"), None),
        P(("groups", "rep"), "tp", None),
        P(("groups", "rep"), None, "tp"),
    )
    return jax.shard_map(
        on_device, mesh=mesh, in_specs=placed, out_specs=P(("groups", "rep"), "tp"), check_vma=False
    )
```

```python
import functools

import jax
import jax.numpy as jnp
import numpy as np
from jax import lax
from jax.experimental import pallas as pl
from jax.experimental.pallas import tpu as pltpu
from jax.sharding import PartitionSpec as P

HEADS = 64
KEY_VALUE_HEADS = 8
HEAD_SIZE = 128
GROUP = HEADS // KEY_VALUE_HEADS
LONGEST = 192
TILE = 64
REACH = -(-(LONGEST - 1) // TILE)
adapter_scale = 2.0

VMEM = pl.BlockSpec(memory_space=pltpu.VMEM)
SMEM = pl.BlockSpec(memory_space=pltpu.SMEM)
NT = (((1,), (1,)), ((), ()))


def ring_order(n):
    if n == 8:
        return list(range(0, n, 2)) + list(range(n - 1, 0, -2))
    return list(range(n))


def windows(rows):
    found = []
    for tile in range(rows // TILE):
        first = max(0, tile - REACH) * TILE
        width = (tile + 1) * TILE - first
        width = -(-width // 128) * 128
        found.append((tile * TILE, first, width))
    return found


def ring_place(replica, n):
    if n == 8:
        return jnp.where(replica & 1 == 0, replica >> 1, n - 1 - (replica >> 1))
    return replica


def column(row):
    wide = jnp.broadcast_to(row.astype(jnp.float32), (8, row.shape[1]))
    return wide.T[:, :1].astype(jnp.int32)


def masks_kernel(n, me_ref, lengths_ref, adapter_ref, near_q_ref, near_k_ref, *refs):
    place_ref, segment_ref, across_ref, slot_ref, slot_across_ref = refs
    distance = ring_place(me_ref[0], n) - ring_place(adapter_ref[...], n)
    distance = jnp.where(distance < 0, distance + n, distance)
    place = jnp.where(distance <= n // 2, jnp.maximum(2 * distance - 1, 0), 2 * (n - distance))
    place_ref[...] = column(place)
    position = lax.broadcasted_iota(jnp.int32, place.shape, 1)
    segment = jnp.zeros(place.shape, jnp.int32)
    end = jnp.int32(0)
    for i in range(lengths_ref.shape[1]):
        end = end + lengths_ref[0, i]
        segment = segment + (position >= end).astype(jnp.int32)
    across_ref[...] = segment
    segment_ref[...] = column(segment)
    rows = place.shape[1]
    last = place == n - 1
    earlier = lax.broadcasted_iota(jnp.int32, (rows, rows), 0) < lax.broadcasted_iota(jnp.int32, (rows, rows), 1)
    ones = jnp.where(jnp.broadcast_to(last, (8, rows)), 1.0, 0.0).astype(jnp.bfloat16)
    count = jnp.dot(ones, jnp.where(earlier, 1.0, 0.0).astype(jnp.bfloat16), preferred_element_type=jnp.float32)
    slot = jnp.where(last, count[:1, :].astype(jnp.int32), -1)
    slot_across_ref[...] = slot
    slot_ref[...] = column(slot)


def masks(n, lengths, adapter_row, queries, keys):
    rows = keys.shape[0]
    tall, flat = [jax.ShapeDtypeStruct(shape, jnp.int32) for shape in ((rows, 1), (1, rows))]
    me = jnp.reshape(lax.axis_index("rep"), (1,)).astype(jnp.int32)
    return pl.pallas_call(
        functools.partial(masks_kernel, n),
        out_shape=[tall, tall, flat, tall, flat],
        in_specs=[SMEM, SMEM, VMEM, VMEM, VMEM],
        out_specs=[VMEM] * 5,
        cost_estimate=pl.CostEstimate(flops=1_000_000_000, bytes_accessed=16 * rows, transcendentals=0),
        compiler_params=pltpu.CompilerParams(vmem_limit_bytes=4 * 2**20),
        name="masks",
    )(me, lengths, adapter_row, queries, keys)


def probs_kernel(kv_head, segment_ref, across_ref, q_ref, k_ref, *refs):
    rows = k_ref.shape[0]
    tiles = windows(rows)
    p_refs = refs[-len(tiles) :]
    factor = float(np.log2(np.e) * HEAD_SIZE**-0.5)
    at = kv_head * HEAD_SIZE
    for p_ref, (start, first, width) in zip(p_refs, tiles):
        t = lax.broadcasted_iota(jnp.int32, (TILE, width), 0) + start
        s = lax.broadcasted_iota(jnp.int32, (TILE, width), 1) + first
        same = segment_ref[start : start + TILE, :] == across_ref[:, first : first + width]
        bias = jnp.where(same & (s <= t), 0.0, -1e30)
        keys = k_ref[first : first + width, at : at + HEAD_SIZE]
        for head in range(GROUP):
            column_at = (kv_head * GROUP + head) * HEAD_SIZE
            q = q_ref[start : start + TILE, column_at : column_at + HEAD_SIZE]
            scores = lax.dot_general(q, keys, NT, preferred_element_type=jnp.float32) + bias
            peak = jnp.max(scores, axis=1, keepdims=True)
            weights = jnp.exp2((scores - peak) * factor)
            inverse = 1.0 / jnp.sum(weights, axis=1, keepdims=True)
            p_ref[head * TILE : (head + 1) * TILE, :] = (weights * inverse).astype(jnp.bfloat16)


def probs_of(segment, across, queries, keys, kv_head):
    rows = keys.shape[0]
    shapes = [(GROUP * TILE, width) for _, _, width in windows(rows)]
    elements = sum(a * b for a, b in shapes)
    return pl.pallas_call(
        functools.partial(probs_kernel, kv_head),
        out_shape=[jax.ShapeDtypeStruct(s, jnp.bfloat16) for s in shapes],
        in_specs=[VMEM] * 4,
        out_specs=[VMEM] * len(shapes),
        cost_estimate=pl.CostEstimate(
            flops=2_000_000_000, bytes_accessed=2 * elements, transcendentals=elements
        ),
        compiler_params=pltpu.CompilerParams(vmem_limit_bytes=12 * 2**20),
        name="probs",
    )(segment, across, queries, keys)


def lowrank_kernel(at, count, place_ref, x_ref, *refs):
    w_refs, (out_ref, up_ref) = refs[:count], refs[-2:]
    before_ref = refs[count] if at > 0 else None
    place = place_ref[...]
    rows, features = x_ref.shape
    half = w_refs[0].shape[0]
    stacked = jnp.concatenate([w_ref[:, :features] for w_ref in w_refs], axis=0)
    product = lax.dot_general(x_ref[...], stacked, NT, preferred_element_type=jnp.float32)
    sums = [jnp.zeros((rows, half), jnp.float32)] * 2
    for i in range(count):
        part = product[:, i * half : (i + 1) * half]
        sums[i % 2] = sums[i % 2] + jnp.where(place == at + i // 2, part, 0.0)
    up_ref[...] = jnp.concatenate([w_ref[:, features:] for w_ref in w_refs], axis=0)
    total = jnp.concatenate(sums, axis=1)
    out_ref[...] = total if before_ref is None else total + before_ref[...]


def lowrank_of(at, place, x, before, pieces, after):
    rows, features = x.shape
    half, held = pieces[0].shape
    rank = 2 * half
    operands = [place, x] + pieces + ([] if before is None else [before])
    used = len(operands)
    operands = operands + after
    size = 2 * sum(p.size for p in pieces)
    return pl.pallas_call(
        functools.partial(lowrank_kernel, at, len(pieces)),
        out_shape=[
            jax.ShapeDtypeStruct((rows, rank), jnp.float32),
            jax.ShapeDtypeStruct((half * len(pieces), held - features), pieces[0].dtype),
        ],
        in_specs=[VMEM] * used + [pl.BlockSpec(memory_space=pl.ANY)] * len(after),
        out_specs=[VMEM, VMEM],
        cost_estimate=pl.CostEstimate(
            flops=1_000_000_000, bytes_accessed=2 * rows + size // features, transcendentals=0
        ),
        compiler_params=pltpu.CompilerParams(vmem_limit_bytes=8 * 2**20 + 2 * x.size + 2 * size),
        name="lowrank",
    )(*operands)


def last_rows_kernel(slot_across_ref, x_ref, out_ref):
    room, rows = out_ref.shape[0], x_ref.shape[0]
    pick = lax.broadcasted_iota(jnp.int32, (room, rows), 0) == slot_across_ref[...]
    pick = jnp.where(pick, 1.0, 0.0).astype(jnp.bfloat16)
    step = 1024
    for at in range(0, x_ref.shape[1], step):
        picked = jnp.dot(pick, x_ref[:, at : at + step], preferred_element_type=jnp.float32)
        out_ref[:, at : at + step] = picked.astype(jnp.bfloat16)


def last_rows(slot_across, x, room):
    return pl.pallas_call(
        last_rows_kernel,
        out_shape=jax.ShapeDtypeStruct((room, x.shape[1]), x.dtype),
        in_specs=[VMEM, VMEM],
        out_specs=VMEM,
        cost_estimate=pl.CostEstimate(flops=100_000_000, bytes_accessed=2 * x.shape[0], transcendentals=0),
        compiler_params=pltpu.CompilerParams(vmem_limit_bytes=8 * 2**20),
        name="last_rows",
    )(slot_across, x)


def last_probs_kernel(slot_ref, *refs):
    tiles = windows(slot_ref.shape[0])
    p_refs, out_refs = refs[: 2 * len(tiles)], refs[2 * len(tiles) :]
    for i, (_, first, width) in enumerate(tiles):
        pick = lax.broadcasted_iota(jnp.int32, (width, 128), 1) == slot_ref[first : first + width, :]
        pick = jnp.where(pick, 1.0, 0.0).astype(jnp.bfloat16)
        for side in range(2):
            picked = jnp.dot(p_refs[side * len(tiles) + i][...], pick, preferred_element_type=jnp.float32)
            out_refs[i][:, side * 128 : (side + 1) * 128] = picked.astype(jnp.bfloat16)


def last_probs(slot, left, right):
    pieces = left + right
    return pl.pallas_call(
        last_probs_kernel,
        out_shape=[jax.ShapeDtypeStruct((p.shape[0], 256), p.dtype) for p in left],
        in_specs=[VMEM] * (1 + len(pieces)),
        out_specs=[VMEM] * len(left),
        cost_estimate=pl.CostEstimate(
            flops=100_000_000, bytes_accessed=2 * slot.size, transcendentals=0
        ),
        compiler_params=pltpu.CompilerParams(vmem_limit_bytes=6 * 2**20),
        name="last_probs",
    )(slot, *pieces)


def early_kernel(kv_heads, place_ref, mine_ref, theirs_ref, base_ref, *refs):
    rows = base_ref.shape[0]
    tiles = windows(rows)
    up_refs = refs[: -kv_heads * len(tiles) - 1]
    p_refs, out_ref = refs[len(up_refs) : -1], refs[-1]
    rank = mine_ref.shape[1]
    held = sum(up_ref.shape[0] for up_ref in up_refs)
    pairs = -(-held // (2 * rank))
    place = place_ref[...]
    lowrank = (mine_ref[...] + theirs_ref[...]).astype(jnp.bfloat16)
    twice = jnp.concatenate([lowrank, lowrank], axis=1)
    second = (lax.broadcasted_iota(jnp.int32, twice.shape, 1) >= rank).astype(jnp.int32)
    offset = place - second
    spread = jnp.concatenate(
        [jnp.where(offset == 2 * i, twice, jnp.zeros_like(twice)) for i in range(pairs)], axis=1
    )
    ups = [up_ref[...] for up_ref in up_refs]
    if held < 2 * rank * pairs:
        ups.append(jnp.zeros((2 * rank * pairs - held, base_ref.shape[1]), jnp.bfloat16))
    delta = jnp.dot(
        spread, jnp.concatenate(ups, axis=0), preferred_element_type=jnp.float32
    ).astype(jnp.bfloat16)
    values = (
        base_ref[...].astype(jnp.float32) + adapter_scale * delta.astype(jnp.float32)
    ).astype(jnp.bfloat16)
    wide = GROUP * HEAD_SIZE
    for kv in range(kv_heads):
        columns = slice(kv * HEAD_SIZE, (kv + 1) * HEAD_SIZE)
        for i, (start, first, width) in enumerate(tiles):
            mixed = jnp.dot(
                p_refs[kv * len(tiles) + i][...],
                values[first : first + width, columns],
                preferred_element_type=jnp.float32,
            )
            for head in range(GROUP):
                at = kv * wide + head * HEAD_SIZE
                out_ref[start : start + TILE, at : at + HEAD_SIZE] = mixed[head * TILE : (head + 1) * TILE, :]


def early_product(place, mine, theirs, base, ups, probs):
    rows, value_portion = base.shape
    kv_heads = value_portion // HEAD_SIZE
    flat = [p for per_head in probs for p in per_head]
    return pl.pallas_call(
        functools.partial(early_kernel, kv_heads),
        out_shape=jax.ShapeDtypeStruct((rows, kv_heads * GROUP * HEAD_SIZE), jnp.float32),
        in_specs=[VMEM] * (4 + len(ups) + len(flat)),
        out_specs=VMEM,
        cost_estimate=pl.CostEstimate(flops=50_000_000, bytes_accessed=4 * rows, transcendentals=0),
        compiler_params=pltpu.CompilerParams(vmem_limit_bytes=8 * 2**20),
        name="early_product",
    )(place, mine, theirs, base, *ups, *flat)


def last_lowrank_kernel(x_ref, low_ref, high_ref, *refs):
    out_ref, up_ref = refs[-2:]
    features = x_ref.shape[1]
    stacked = jnp.concatenate([low_ref[:, :features], high_ref[:, :features]], axis=0)
    out_ref[...] = lax.dot_general(x_ref[...], stacked, NT, preferred_element_type=jnp.float32)
    up_ref[...] = jnp.concatenate([low_ref[:, features:], high_ref[:, features:]], axis=0)


def last_lowrank(x, low, high, after):
    rank, columns = 2 * low.shape[0], low.shape[1] - x.shape[1]
    return pl.pallas_call(
        last_lowrank_kernel,
        out_shape=[
            jax.ShapeDtypeStruct((x.shape[0], rank), jnp.float32),
            jax.ShapeDtypeStruct((rank, columns), low.dtype),
        ],
        in_specs=[VMEM] * 3 + [pl.BlockSpec(memory_space=pl.ANY)] * len(after),
        out_specs=[VMEM, VMEM],
        cost_estimate=pl.CostEstimate(flops=600_000_000, bytes_accessed=2 * x.size, transcendentals=0),
        compiler_params=pltpu.CompilerParams(vmem_limit_bytes=6 * 2**20),
        name="last_lowrank",
    )(x, low, high, *after)


def finish_kernel(mine_ref, theirs_ref, up_ref, early_ref, *refs):
    p_refs, (out_ref, block, sems) = refs[:-3], refs[-3:]
    rows = early_ref.shape[0]
    tiles = windows(rows)
    wide = GROUP * HEAD_SIZE
    lowrank = (mine_ref[...] + theirs_ref[...]).astype(jnp.bfloat16)
    delta = jnp.dot(lowrank, up_ref[...], preferred_element_type=jnp.float32).astype(jnp.bfloat16)
    change = (adapter_scale * delta.astype(jnp.float32)).astype(jnp.bfloat16)
    room = change.shape[0]
    if room < 128:
        change = jnp.concatenate([change, jnp.zeros((128 - room, change.shape[1]), jnp.bfloat16)], axis=0)
    none = jnp.zeros((128, HEAD_SIZE), jnp.bfloat16)
    copies = []
    for pair in range(len(p_refs) // len(tiles)):
        at = 2 * pair * HEAD_SIZE
        left, right = change[:, at : at + HEAD_SIZE], change[:, at + HEAD_SIZE : at + 2 * HEAD_SIZE]
        both = jnp.concatenate(
            [jnp.concatenate([left, none], axis=1), jnp.concatenate([none, right], axis=1)], axis=0
        )
        for i, (start, _, _) in enumerate(tiles):
            p_ref = p_refs[pair * len(tiles) + i]
            for half in range(2):
                heads = range(half * GROUP // 2, (half + 1) * GROUP // 2)
                near = slice(heads[0] * TILE, (heads[-1] + 1) * TILE)
                added = jnp.dot(p_ref[near, :], both, preferred_element_type=jnp.float32)
                for side in range(2):
                    for k, head in enumerate(heads):
                        at = (2 * pair + side) * wide + head * HEAD_SIZE
                        part = added[k * TILE : (k + 1) * TILE, side * HEAD_SIZE : (side + 1) * HEAD_SIZE]
                        whole = early_ref[start : start + TILE, at : at + HEAD_SIZE] + part
                        block[start : start + TILE, at : at + HEAD_SIZE] = whole.astype(jnp.bfloat16)
            rows_done = slice(start, start + TILE)
            span = slice(2 * pair * wide, 2 * (pair + 1) * wide)
            copy = pltpu.make_async_copy(
                block.at[rows_done, span], out_ref.at[rows_done, span], sems.at[len(copies)]
            )
            copy.start()
            copies.append(copy)
    for copy in copies:
        copy.wait()


def finish(mine, theirs, up, early, picked):
    flat = [p for pair in picked for p in pair]
    return pl.pallas_call(
        finish_kernel,
        out_shape=jax.ShapeDtypeStruct(early.shape, jnp.bfloat16),
        in_specs=[VMEM] * (4 + len(flat)),
        out_specs=pl.BlockSpec(memory_space=pl.ANY),
        scratch_shapes=[pltpu.VMEM(early.shape, jnp.bfloat16), pltpu.SemaphoreType.DMA((len(flat),))],
        compiler_params=pltpu.CompilerParams(vmem_limit_bytes=10 * 2**20),
        name="finish",
    )(mine, theirs, up, early, *flat)


def on_device(
    normed_token_rows,
    base_value_rows,
    queries,
    stacked_key_rows,
    adapter_of_row,
    sequence_lengths,
    adapter_down_weight,
    adapter_up_weight,
):
    n = lax.axis_size("rep")
    order = ring_order(n)
    ahead = [(order[i], order[(i + 1) % n]) for i in range(n)]
    back = [(b, a) for a, b in ahead]
    far = n // 2
    distances = [0] + [d for step in range(1, far) for d in (step, -step)] + [far]
    down = jnp.swapaxes(adapter_down_weight[0], 0, 1)
    both = jnp.concatenate([down, adapter_up_weight[0]], axis=1)
    rank = both.shape[0]
    own_low, own_high = both[: rank // 2], both[rank // 2 :]
    place, segment, across, slot, slot_across = masks(
        n, sequence_lengths, adapter_of_row.reshape(1, -1), queries, stacked_key_rows
    )
    low, high = {0: own_low}, {0: own_high}

    def pass_round(held, pairs, sign, steps):
        piece = held[0]
        for step in range(1, steps + 1):
            piece = lax.ppermute(piece, "rep", pairs)
            held[sign * step if step < far else far] = piece

    pass_round(high, ahead, 1, far - 1)
    pass_round(low, back, -1, far - 1)
    pass_round(high, back, -1, far)
    pass_round(low, ahead, 1, far)

    kv_heads = stacked_key_rows.shape[1] // HEAD_SIZE
    arrivals = [
        pair
        for step in range(1, far)
        for pair in ([low[step], high[-step]], [high[step], low[-step]])
    ]
    probs = [
        probs_of(segment, across, queries, stacked_key_rows, kv) for kv in range(kv_heads)
    ]

    picked = [last_probs(slot, probs[kv], probs[kv + 1]) for kv in range(0, kv_heads, 2)]
    most = 2 * normed_token_rows.shape[0] // n
    x_last = last_rows(slot_across, normed_token_rows, -(-most // 16) * 16)

    partial, ups = None, []
    for lo, hi in [(0, 3)] + [(a, a + 2) for a in range(3, n - 1, 2)]:
        pieces = [piece for d in distances[lo:hi] for piece in (low[d], high[d])]
        after = arrivals[kv_heads - 1] if lo == 0 else []
        partial, up = lowrank_of(lo, place, normed_token_rows, partial, pieces, after + ([x_last] + [p[0] for p in picked] if lo == n - 5 else []))
        ups.append(up)
    swap = [(0, 1), (1, 0)]
    early = early_product(place, partial, lax.ppermute(partial, "tp", swap), base_value_rows, ups, probs)
    last, last_up = last_lowrank(x_last, low[far], high[far], [early])
    return finish(last, lax.ppermute(last, "tp", swap), last_up, early, picked)


def solution(mesh):
    placed = (
        P(("groups", "rep"), "tp"),
        P(("groups", "rep"), "tp"),
        P(("groups", "rep"), "tp"),
        P(("groups", "rep"), "tp"),
        P(("groups", "rep"), None),
        P(("groups", "rep"), None),
        P(("groups", "rep"), "tp", None),
        P(("groups", "rep"), None, "tp"),
    )
    return jax.shard_map(
        on_device, mesh=mesh, in_specs=placed, out_specs=P(("groups", "rep"), "tp"), check_vma=False
    )
```
